128 devices in a mesh: row: 8 (over y, core), col: 16 (over z, x).
Axes of the slice: x: 4, y: 4, z: 4, core: 2. Of those that a mesh axis runs over, the one named last changes fastest.
Arguments:
- embedded: bfloat16 [128, 393216], P('row', 'col'), may hold values from -6 to 6
- window_target_device: int32 [16, 256], P('row', 'col'), may hold values from -1 to 127, as said below
- window_device_slot: int32 [16, 256], P('row', 'col'), may hold values from -1 to 15, as said below
- cloud_mask_token: bfloat16 [192], replicated, may hold values from -4 to 4
- query_key_value_weight: bfloat16 [2, 192, 576], replicated, may hold values from -0.4375 to 0.4375
- projection_weight: bfloat16 [2, 192, 192], replicated, may hold values from -0.4375 to 0.4375
- up_weight: bfloat16 [2, 192, 768], replicated, may hold values from -0.4375 to 0.4375
- down_weight: bfloat16 [2, 768, 192], replicated, may hold values from -0.21875 to 0.21875
- bias_net_input_weight: float32 [2, 2, 512], replicated, may hold values from -4 to 4
- bias_net_first_bias: float32 [2, 512], replicated, may hold values from -3 to 3
- bias_net_output_weight: float32 [2, 512, 6], replicated, may hold values from -0.25 to 0.25
- temper: float32 [2, 6], replicated, may hold values from 1 to 10
- norm_gain_values: float32 [2, 2, 192], replicated, may hold values from 0.25 to 1.75
Outputs:
- features: bfloat16 [128, 393216], P('row', 'col')
- packed: bfloat16 [2048, 12288], P(('row', 'col'))
The draws below stay inside these ranges and needn't reach their ends.
Inputs may be any that keep to these rules, and one draw needn't show every extreme that they name: `window_target_device`: devices are numbered row index * 16 + col index. A quarter of the devices hold 32 visible windows each, a quarter 3 * 8, a quarter 32 / 4 and a quarter none; which devices and which windows are drawn. Every device is named by exactly 16 visible windows, and by at most 1 windows of any one device. `window_device_slot`: -1 exactly where window_target_device is -1; the windows that name one device carry the slots 0 to 15, each once.
All inputs are finite; a program needn't handle non-finite values.
Results may differ from the reference program's by a relative error of at most 0.02.
Values may be sent and summed in bfloat16 or wider, within the bound.
No kernel may reach another device: no remote copies, remote signals or barrier semaphores. Data moves between devices by JAX's collectives and lax.ppermute only.
A program may use at most 128 MiB of HBM per device.

```python
import math
import jax
import jax.numpy as jnp
from jax import lax

C = 192
ATTENTION_HEADS = 6
HIDDEN_SIZE = 768
BIAS_NET_UNITS = 512
WIN = 8
SHIFT = 4
TH = 16
TW = 128
SLOTS = 16
H = 128
W = 2048
WROWS = 16
WCOLS = 256
PACKED = 2048
N_ROW = 8
N_COL = 16


def plan_tables(key):
    k_class, k_pick, k_order, k_dest = jax.random.split(key, 4)
    devices = N_ROW * N_COL
    n_local = TH // WIN * (TW // WIN)
    dev_class = jax.random.permutation(k_class, devices).astype(jnp.int32) * 4 // devices
    levels = jnp.array([n_local, 3 * n_local // 4, n_local // 4, 0], jnp.int32)
    counts = levels[dev_class]
    picked = jax.vmap(lambda one_key: jax.random.permutation(one_key, n_local))(jax.random.split(k_pick, devices)).astype(jnp.int32)
    rank_in = jnp.argsort(picked, axis=1).astype(jnp.int32)
    visible = rank_in < counts[:, None]
    src_order = jax.random.permutation(k_order, devices).astype(jnp.int32)
    ordered = counts[src_order]
    starts = jnp.cumsum(ordered) - ordered
    offset = jnp.zeros((devices,), jnp.int32).at[src_order].set(starts.astype(jnp.int32))
    flags = visible.astype(jnp.int32)
    local_rank = jnp.cumsum(flags, axis=1) - flags
    glob_rank = offset[:, None] + local_rank
    dest_perm = jax.random.permutation(k_dest, devices).astype(jnp.int32)
    targets = jnp.where(visible, dest_perm[glob_rank % devices], -1).astype(jnp.int32)
    slots = jnp.where(visible, glob_rank // devices, -1).astype(jnp.int32)

    def layout(table):
        table = table.reshape(N_ROW, N_COL, TH // WIN, TW // WIN).transpose(0, 2, 1, 3)
        return table.reshape(WROWS, WCOLS)
    return (layout(targets), layout(slots))


def draw_window_target_device(key, part):
    targets, slots = plan_tables(key)
    return targets


def draw_window_device_slot(key, part):
    targets, slots = plan_tables(key)
    return slots


def block_levels(rng, extent, cuts, low, high):
    loudness = 1.0
    for position, shards_of in cuts:
        steps = jax.random.uniform(jax.random.fold_in(jax.random.fold_in(rng, 6), position), (shards_of,), jnp.float32, low / len(cuts), high / len(cuts))
        loudness = loudness * jnp.repeat(jnp.exp(steps), extent[position] // shards_of).reshape((-1,) + (1,) * (len(extent) - 1 - position))
    return loudness


def bell_draw(rng, shape, deviation, most, pieces=(), held_as=jnp.bfloat16):
    values = jax.random.normal(rng, shape, jnp.float32) * deviation
    if len(pieces) > 0:
        values = block_levels(rng, shape, pieces, -0.22, 0.18) * values
    return jnp.clip(values, min=-most, max=most).astype(held_as)


def setup_inputs(seed: int = 0) -> dict:
    arg_keys = jax.random.split(jax.random.key(seed), 14)
    return {
        "embedded": bell_draw(arg_keys[0], (H, W * C), 1.0, 6.0, ((0, 8), (1, 16))),
        "window_target_device": draw_window_target_device(jax.random.fold_in(arg_keys[13], 71), 0),
        "window_device_slot": draw_window_device_slot(jax.random.fold_in(arg_keys[13], 71), 0),
        "cloud_mask_token": bell_draw(arg_keys[3], (C,), 1.0, 4.0),
        "query_key_value_weight": bell_draw(arg_keys[4], (2, C, 3 * C), C ** -0.5, 0.4375),
        "projection_weight": bell_draw(arg_keys[5], (2, C, C), C ** -0.5, 0.4375),
        "up_weight": bell_draw(arg_keys[6], (2, C, HIDDEN_SIZE), C ** -0.5, 0.4375),
        "down_weight": bell_draw(arg_keys[7], (2, HIDDEN_SIZE, C), HIDDEN_SIZE ** -0.5, 0.21875),
        "bias_net_input_weight": bell_draw(arg_keys[8], (2, 2, BIAS_NET_UNITS), 2 ** -0.5, 4.0, (), jnp.float32),
        "bias_net_first_bias": bell_draw(arg_keys[9], (2, BIAS_NET_UNITS), 0.5, 3.0, (), jnp.float32),
        "bias_net_output_weight": bell_draw(arg_keys[10], (2, BIAS_NET_UNITS, ATTENTION_HEADS), BIAS_NET_UNITS ** -0.5, 0.25, (), jnp.float32),
        "temper": jnp.clip(jnp.exp(jax.random.uniform(arg_keys[11], (2, ATTENTION_HEADS), jnp.float32, math.log(1.0), math.log(10.0))), 1.0, 10.0),
        "norm_gain_values": jnp.clip(1.0 + 0.15 * jax.random.normal(arg_keys[12], (2, 2, C), jnp.float32), 0.25, 1.75),
    }


finest = lax.Precision.HIGHEST

def layer_norm(values, gain_row):
    row_mean = lax.optimization_barrier(jnp.mean(values, -1, keepdims=True))
    centred = values - row_mean
    spread = lax.optimization_barrier(jnp.mean(centred * centred, -1, keepdims=True))
    return centred * lax.rsqrt(spread + 1e-05) * gain_row

def relative_position_bias(first_layer, first_bias, second_layer):
    cell_ids = jnp.arange(WIN * WIN)
    across = cell_ids // WIN
    along_row = cell_ids % WIN
    offsets = jnp.stack([across[:, None] - across[None, :], along_row[:, None] - along_row[None, :]], -1).astype(jnp.float32)
    scaled = offsets * (8.0 / (WIN - 1))
    coords = jnp.sign(scaled) * jnp.log2(jnp.abs(scaled) + 1.0) / 3.0
    hidden_units = jax.nn.relu(jnp.dot(coords.reshape(-1, 2), first_layer, precision=finest) + first_bias)
    logits = jnp.dot(hidden_units, second_layer, precision=finest)
    n_heads = second_layer.shape[1]
    return (16.0 * jax.nn.sigmoid(logits)).T.reshape(n_heads, WIN * WIN, WIN * WIN)

def swin_block(windows, region, query_key_value_weight, projection_weight, up_weight, down_weight, bias_term, temper, gains):
    n_windows, n_places, n_feat = windows.shape
    n_heads = temper.shape[0]
    flat_rows = windows.reshape(n_windows * n_places, n_feat)
    triple = jnp.dot(flat_rows, query_key_value_weight, preferred_element_type=jnp.float32).astype(jnp.bfloat16)
    triple = triple.reshape(n_windows, n_places, 3, n_heads, n_feat // n_heads)
    queries = triple[:, :, 0].astype(jnp.float32)
    keys_now = triple[:, :, 1].astype(jnp.float32)
    values_now = triple[:, :, 2].astype(jnp.float32)
    queries = queries * lax.rsqrt(lax.optimization_barrier(jnp.sum(queries * queries, -1, keepdims=True)) + 1e-06)
    keys_now = keys_now * lax.rsqrt(lax.optimization_barrier(jnp.sum(keys_now * keys_now, -1, keepdims=True)) + 1e-06)
    scores = jnp.einsum('nqhd,nkhd->nhqk', queries, keys_now, precision=finest) * temper[:, None, None] + bias_term
    if region is not None:
        scores = scores + jnp.where(region[:, :, None] == region[:, None, :], 0.0, -100.0)[:, None].astype(scores.dtype)
    weights_now = jax.nn.softmax(scores, axis=-1).astype(jnp.bfloat16)
    mixed_heads = jnp.einsum('nhqk,nkhd->nqhd', weights_now.astype(jnp.float32), values_now, precision=finest)
    mixed_heads = mixed_heads.astype(jnp.bfloat16).reshape(n_windows * n_places, n_feat)
    attended = jnp.dot(mixed_heads, projection_weight, preferred_element_type=jnp.float32)
    hidden = (flat_rows.astype(jnp.float32) + layer_norm(attended, gains[0])).astype(jnp.bfloat16)
    expanded = jax.nn.gelu(jnp.dot(hidden, up_weight, preferred_element_type=jnp.float32), approximate=False).astype(jnp.bfloat16)
    reduced = jnp.dot(expanded, down_weight, preferred_element_type=jnp.float32)
    result = hidden.astype(jnp.float32) + layer_norm(reduced, gains[1])
    return result.astype(jnp.bfloat16).reshape(n_windows, n_places, n_feat)

def to_windows(token_grid):
    n_rows, n_cols, n_chan = token_grid.shape
    tiled = token_grid.reshape(n_rows // WIN, WIN, n_cols // WIN, WIN, n_chan).transpose(0, 2, 1, 3, 4)
    return tiled.reshape(n_rows // WIN, n_cols // WIN, WIN * WIN, n_chan)

def from_windows(win_tiles):
    win_rows, win_cols, n_places, n_chan = win_tiles.shape
    tiled = win_tiles.reshape(win_rows, win_cols, WIN, WIN, n_chan).transpose(0, 2, 1, 3, 4)
    return tiled.reshape(win_rows * WIN, win_cols * WIN, n_chan)

def reference(embedded, window_target_device, window_device_slot, cloud_mask_token, query_key_value_weight, projection_weight, up_weight, down_weight, bias_net_input_weight, bias_net_first_bias, bias_net_output_weight, temper, norm_gain_values):
    total_rows = embedded.shape[0]
    total_cols = embedded.shape[1] // C
    token_grid = embedded.reshape(total_rows, total_cols, C)

    def layer_params(layer_number):
        bias_term = relative_position_bias(bias_net_input_weight[layer_number], bias_net_first_bias[layer_number], bias_net_output_weight[layer_number])
        return (query_key_value_weight[layer_number], projection_weight[layer_number], up_weight[layer_number], down_weight[layer_number], bias_term, temper[layer_number], norm_gain_values[layer_number])
    first_params = layer_params(0)
    first_out = lax.map(lambda blocks: swin_block(blocks, None, *first_params), to_windows(token_grid))
    visible = window_target_device >= 0
    kept_out = jnp.where(visible[:, :, None, None], first_out, cloud_mask_token[None, None, None, :])
    flat_index = jnp.where(visible, window_target_device * SLOTS + window_device_slot, PACKED).reshape(-1).astype(jnp.int32)
    packed = jnp.zeros((PACKED, WIN * WIN, C), jnp.bfloat16).at[flat_index].set(first_out.reshape(-1, WIN * WIN, C), mode='drop')
    middle = from_windows(kept_out)
    rolled = jnp.roll(middle, (-SHIFT, -SHIFT), axis=(0, 1))
    row_ids = jnp.arange(total_rows)
    col_ids = jnp.arange(total_cols)
    band_rows = (row_ids >= total_rows - WIN).astype(jnp.int32) + (row_ids >= total_rows - SHIFT).astype(jnp.int32)
    band_cols = (col_ids >= total_cols - WIN).astype(jnp.int32) + (col_ids >= total_cols - SHIFT).astype(jnp.int32)
    region = band_rows[:, None] * 3 + band_cols[None, :]
    region_tiles = to_windows(region[:, :, None])[..., 0]
    second_params = layer_params(1)
    second = lax.map(lambda pair_in: swin_block(pair_in[0], pair_in[1], *second_params), (to_windows(rolled), region_tiles))
    restored = jnp.roll(from_windows(second), (SHIFT, SHIFT), axis=(0, 1))
    return (restored.reshape(total_rows, total_cols * C), packed.reshape(PACKED, WIN * WIN * C))
```

```python
import functools
import math

import jax
import jax.numpy as jnp
import numpy as np
from jax import lax
from jax.experimental import pallas as pl
from jax.experimental.pallas import tpu as pltpu
from jax.sharding import PartitionSpec as P

WIN = 8
HALF = WIN // 2
CELLS = WIN * WIN
LOG2E = math.log2(math.e)
F32 = jnp.float32
BF16 = jnp.bfloat16
VMEM_BYTES = 60 * 2**20
SMEM = pl.BlockSpec(memory_space=pltpu.SMEM)
ANY = pl.BlockSpec(memory_space=pl.ANY)


def log_step(offset):
    scaled = np.abs(offset).astype(np.float32) * np.float32(8.0 / (WIN - 1))
    return np.sign(offset) * np.log2(scaled + 1.0) / 3.0


def offset_coords():
    lane = np.arange(128)
    across = np.maximum(WIN - 1 - lane // WIN, 1 - WIN)
    down = np.concatenate([-(lane % WIN), np.minimum(WIN - lane % WIN, WIN - 1)])
    return np.stack([log_step(down), log_step(np.tile(across, 2))], 1).astype(np.float32)


def head_blocks(rows, row_block, cols, col_block):
    same = (np.arange(rows) // row_block)[:, None] == (np.arange(cols) // col_block)[None, :]
    return same.astype(np.float32)


def constants(n_heads, n_feat):
    per_head = n_feat // n_heads
    return (
        jnp.asarray(offset_coords(), F32),
        jnp.asarray(head_blocks(n_feat, per_head, n_feat, per_head), BF16),
        jnp.asarray(head_blocks(n_heads * CELLS, CELLS, n_feat, per_head), BF16),
        jnp.asarray(head_blocks(n_heads, 1, n_feat, per_head), BF16),
    )


def dot(a, b):
    return jnp.dot(a, b, preferred_element_type=F32)


def dot_nt(a, b):
    return lax.dot_general(a, b, (((1,), (1,)), ((), ())), preferred_element_type=F32)


def bias_strips(coords_ref, net_in, net_first, net_out, strips_ref):
    coords = coords_ref[...]
    units = jnp.maximum(
        coords[:, 0:1] * net_in[0:1, :] + coords[:, 1:2] * net_in[1:2, :] + net_first[...], 0.0
    )
    logits = lax.dot_general(
        net_out[...], units, (((0,), (1,)), ((), ())),
        precision=lax.Precision.HIGHEST, preferred_element_type=F32,
    )
    n_heads = logits.shape[0]
    logits = jnp.concatenate([logits, jnp.zeros((8 - n_heads, 256), F32)], 0)
    table = 16.0 * LOG2E / (1.0 + jnp.exp(-logits))
    before, after = table[:, :128], table[:, 128:]
    cell = lax.broadcasted_iota(jnp.int32, (8, 128), 1) % WIN
    for u in range(WIN):
        strip = jnp.where(
            cell >= u,
            pltpu.roll(before, u, 1) if u else before,
            pltpu.roll(after, (u - WIN) % 128, 1),
        )
        strips_ref[:, u, :] = strip


def turned(strip):
    cell = lax.broadcasted_iota(jnp.int32, (WIN, 128), 1) % WIN
    strip = pltpu.roll(strip, HALF, 0)
    return jnp.where(cell < HALF, pltpu.roll(strip, 128 - HALF, 1), pltpu.roll(strip, HALF, 1))


def bias_rows(strips, w):
    lane = lax.broadcasted_iota(jnp.int32, (WIN, 128), 1)
    back = (WIN - 1 - w) * WIN
    parts = []
    for pair in range(len(strips) // 2):
        low = pltpu.roll(strips[2 * pair], (128 - back) % 128, 1)
        high = pltpu.roll(strips[2 * pair + 1], (192 - back) % 128, 1)
        parts.append(jnp.where(lane < CELLS, low, high))
    return jnp.concatenate(parts, 1)


def layer_norm(values, gain_row):
    row_mean = jnp.mean(values, -1, keepdims=True)
    centred = values - row_mean
    spread = jnp.mean(centred * centred, -1, keepdims=True)
    return centred * lax.rsqrt(spread + 1e-05) * gain_row


def unit_vectors(t, heads_ref):
    t = t.astype(BF16).astype(F32)
    squares = dot((t * t).astype(BF16), heads_ref[...])
    return t * lax.rsqrt(squares + 1e-06)


def temper_row(temper, layer, mask_ref):
    row = jnp.zeros((1, mask_ref.shape[1]), F32)
    for h in range(mask_ref.shape[0]):
        row = row + (temper[layer, h] * LOG2E) * mask_ref[h : h + 1, :].astype(F32)
    return row


def spread_heads(t, mask_ref):
    low = [t[:, :128] * mask_ref[h : h + 1, :128] for h in range(4)]
    high = [t[:, 128:] * mask_ref[h : h + 1, 128:] for h in range(4, 6)]
    return jnp.concatenate(low, 0), jnp.concatenate(high, 0)


def scores_of(q, k, mask_ref):
    low, high = spread_heads(k, mask_ref)
    return jnp.concatenate([dot_nt(q[:, :128], low), dot_nt(q[:, 128:], high)], 1)


def weighted(p, low, high):
    return jnp.concatenate([dot(p[:, :256], low), dot(p[:, 256:], high)], 1)


def totals_of(p, ones_ref):
    return weighted(p, ones_ref[:256, :128], ones_ref[256:, 128:])


def dense_tail(x, mixed, proj_ref, up_ref, down_ref, gain_ref):
    attended = dot(mixed.astype(BF16), proj_ref[...])
    hidden = (x + layer_norm(attended, gain_ref[0:1, :])).astype(BF16)
    raised = dot(hidden, up_ref[...])
    expanded = (0.5 * raised * (1.0 + lax.erf(raised * math.sqrt(0.5)))).astype(BF16)
    reduced = dot(expanded, down_ref[...])
    return (hidden.astype(F32) + layer_norm(reduced, gain_ref[1:2, :])).astype(BF16)


def split_weights(qkv_ref, q_w, k_w, v_w):
    n_feat = q_w.shape[0]
    q_w[...] = qkv_ref[:, :n_feat]
    k_w[...] = qkv_ref[:, n_feat : 2 * n_feat]
    v_w[...] = qkv_ref[:, 2 * n_feat :]


def first_kernel(
    groups,
    targets, temper, emb_ref, token_ref, coords_ref, heads_ref, ones_ref, mask_ref,
    net_in, net_first, net_out, qkv_ref, proj_ref, up_ref, down_ref, gain_ref,
    mid0_ref, mid1_ref, left_ref, right_ref, send_ref,
    bias_ref, strips_ref, q_w, k_w, v_w, p_ref, staging, sems,
):
    step = pl.program_id(0)
    n_heads, n_feat = mask_ref.shape

    @pl.when(step == 0)
    def _():
        bias_strips(coords_ref, net_in, net_first, net_out, strips_ref)
        strips = [strips_ref[h] for h in range(n_heads)]
        for w in range(WIN):
            bias_ref[w * WIN : (w + 1) * WIN, :] = bias_rows(strips, w)
        split_weights(qkv_ref, q_w, k_w, v_w)

    tiles = []
    for group in range(groups):
        slabs = []
        for w in range(WIN):
            at = (group * WIN + w) * n_feat
            slabs.append(emb_ref[:, at : at + n_feat].astype(F32))
        for i in range(2):
            tiles.append(jnp.concatenate([s[i * WIN : (i + 1) * WIN] for s in slabs], 0))
    x = jnp.concatenate(tiles, 0)
    xb = x.astype(BF16)
    q = (unit_vectors(dot(xb, q_w[...]), heads_ref) * temper_row(temper, 0, mask_ref)).astype(BF16)
    k = unit_vectors(dot(xb, k_w[...]), heads_ref).astype(BF16)
    v = dot(xb, v_w[...]).astype(BF16)
    bias = bias_ref[...]
    mixed = []
    for n in range(2 * groups):
        rows = slice(n * CELLS, (n + 1) * CELLS)
        p_ref[rows, :] = jnp.exp2(scores_of(q[rows], k[rows], mask_ref) + bias).astype(BF16)
    for n in range(2 * groups):
        rows = slice(n * CELLS, (n + 1) * CELLS)
        mixed.append(weighted(p_ref[rows, :], *spread_heads(v[rows], mask_ref)))
    mixed = jnp.concatenate(mixed, 0) / totals_of(p_ref[...], ones_ref)
    y = dense_tail(x, mixed, proj_ref, up_ref, down_ref, gain_ref).astype(F32)

    token = token_ref[...].astype(F32)
    for group in range(groups):
        for i in range(2):
            n = 2 * group + i
            j = step * groups + group
            target = targets[i, j]
            tile = y[n * CELLS : (n + 1) * CELLS]
            kept = jnp.where(target >= 0, tile, token).astype(BF16)
            mid = (mid0_ref, mid1_ref)[i]
            mid[2 * group] = kept[:32]
            mid[2 * group + 1] = kept[32:]
            if group == 0:

                @pl.when(step == 0)
                def _(i=i, kept=kept):
                    left_ref[i] = kept[:32]

            if group == groups - 1:

                @pl.when(step == pl.num_programs(0) - 1)
                def _(i=i, kept=kept):
                    right_ref[i] = kept[32:]

            slot = j * 2 + i
            staging[slot, :64] = tile[:, :128].astype(BF16)
            tails = tile[:, 128:].reshape(4, 2, WIN, 64)
            joined = jnp.concatenate([tails[:, 0], tails[:, 1]], -1)
            staging[slot, 64:] = joined.reshape(32, 128).astype(BF16)

            @pl.when(target >= 0)
            def _(slot=slot, target=target):
                pltpu.make_async_copy(staging.at[slot], send_ref.at[target], sems.at[slot]).start()

    @pl.when(step == pl.num_programs(0) - 1)
    def _():
        def finish(slot, carry):
            target = targets[lax.rem(slot, 2), slot // 2]

            @pl.when(target >= 0)
            def _():
                pltpu.make_async_copy(staging.at[slot], send_ref.at[target], sems.at[slot]).wait()

            return carry

        lax.fori_loop(0, staging.shape[0], finish, 0)


def whole(array):
    zeros = (0,) * array.ndim
    return pl.BlockSpec(array.shape, lambda *_: zeros)


def one_layer(array, layer):
    rest = array.shape[1:]
    at = (layer,) + (0,) * len(rest)
    return pl.BlockSpec((None,) + rest, lambda *_: at)


def layer_scratch(n_heads, n_feat):
    square = pltpu.VMEM((n_feat, n_feat), BF16)
    return [pltpu.VMEM((8, WIN, 128), F32), square, square, square]


def first_layer(embedded, targets, temper, token, consts, params, devices, groups=8):
    n_heads, n_feat = consts[3].shape
    columns = embedded.shape[1] // (WIN * n_feat)
    side = jax.ShapeDtypeStruct((2, 32, n_feat), BF16)
    mid = jax.ShapeDtypeStruct((2 * columns, 32, n_feat), BF16)
    mid_spec = pl.BlockSpec((2 * groups, 32, n_feat), lambda g: (g, 0, 0))
    return pl.pallas_call(
        functools.partial(first_kernel, groups),
        grid=(columns // groups,),
        out_shape=(mid, mid, side, side, jax.ShapeDtypeStruct((devices, 96, 128), BF16)),
        in_specs=[SMEM, SMEM, pl.BlockSpec((2 * WIN, groups * WIN * n_feat), lambda g: (0, g))]
        + [whole(a) for a in (token,) + consts]
        + [one_layer(a, 0) for a in params],
        out_specs=(mid_spec, mid_spec, whole(side), whole(side), ANY),
        scratch_shapes=[pltpu.VMEM((CELLS, n_heads * CELLS), F32)]
        + layer_scratch(n_heads, n_feat)
        + [
            pltpu.VMEM((groups * 2 * CELLS, n_heads * CELLS), BF16),
            pltpu.VMEM((2 * columns, 96, 128), BF16),
            pltpu.SemaphoreType.DMA((2 * columns,)),
        ],
        compiler_params=pltpu.CompilerParams(vmem_limit_bytes=VMEM_BYTES),
        cost_estimate=pl.CostEstimate(flops=2 * 10**9, bytes_accessed=6 * 10**6, transcendentals=10**6),
        name="first_layer",
    )(targets, temper, embedded, token, *consts, *params)


def second_kernel(
    groups,
    place, temper, mid0_ref, mid1_ref, above_ref, below_ref, left_ref, right_ref,
    nw_ref, ne_ref, sw_ref, se_ref, coords_ref, heads_ref, ones_ref, mask_ref,
    net_in, net_first, net_out, qkv_ref, proj_ref, up_ref, down_ref, gain_ref,
    out_ref,
    bias_ref, strips_ref, q_w, k_w, v_w, ext, p_ref, sems,
):
    step = pl.program_id(0)
    n_heads, n_feat = mask_ref.shape
    n_half = mid0_ref.shape[0]
    row, col, last_row, last_col = place[0], place[1], place[2], place[3]

    @pl.when(step == 0)
    def _():
        inner = pl.ds(1, n_half)
        end = n_half + 1
        copies = [
            pltpu.make_async_copy(src, dst, sems.at[n])
            for n, (src, dst) in enumerate(
                [
                    (above_ref, ext.at[0, inner]),
                    (mid0_ref, ext.at[1, inner]),
                    (mid1_ref, ext.at[2, inner]),
                    (below_ref, ext.at[3, inner]),
                    (left_ref, ext.at[pl.ds(1, 2), 0]),
                    (right_ref, ext.at[pl.ds(1, 2), end]),
                    (nw_ref.at[1], ext.at[0, 0]),
                    (ne_ref.at[1], ext.at[0, end]),
                    (sw_ref.at[0], ext.at[3, 0]),
                    (se_ref.at[0], ext.at[3, end]),
                ]
            )
        ]
        for copy in copies:
            copy.start()
        for spare in range(n_half + 2, ext.shape[1]):
            ext[:, spare] = jnp.zeros((4, 32, n_feat), BF16)
        split_weights(qkv_ref, q_w, k_w, v_w)
        bias_strips(coords_ref, net_in, net_first, net_out, strips_ref)
        strips = [turned(strips_ref[h]) for h in range(n_heads)]
        lane = lax.broadcasted_iota(jnp.int32, (WIN, n_heads * CELLS), 1)
        upper = lax.broadcasted_iota(jnp.int32, (WIN, n_heads * CELLS), 0) < HALF
        other_rows = upper != (lane % WIN < HALF)
        top, bottom = row == 0, row == last_row
        edge_rows = other_rows & ((upper & top) | (~upper & bottom))
        for w in range(WIN):
            other_cols = (lane % CELLS >= CELLS // 2) != (w >= HALF)
            rows = slice(w * WIN, (w + 1) * WIN)
            bias = bias_rows(strips, w)
            away = -100.0 * LOG2E
            bias_ref[0, rows, :] = bias
            bias_ref[1, rows, :] = bias + jnp.where(other_cols, away, 0.0)
            bias_ref[2, rows, :] = bias + jnp.where(edge_rows, away, 0.0)
            bias_ref[3, rows, :] = bias + jnp.where(edge_rows | other_cols, away, 0.0)
        for copy in copies:
            copy.wait()

    first_half = 2 * groups * step
    upper = lax.broadcasted_iota(jnp.int32, (CELLS, n_feat), 0) % WIN < HALF

    def tile_of(line, group):
        return jnp.concatenate(
            [ext[line, first_half + 2 * group], ext[line, first_half + 2 * group + 1]], 0
        )

    own, around = [], []
    for group in range(groups):
        own += [tile_of(1, group), tile_of(2, group)]
        around.append(jnp.where(upper, tile_of(3, group), tile_of(0, group)))
    xb = jnp.concatenate(own, 0)
    xa = jnp.concatenate(around, 0)
    q = (unit_vectors(dot(xb, q_w[...]), heads_ref) * temper_row(temper, 1, mask_ref)).astype(BF16)
    keys = [unit_vectors(dot(t, k_w[...]), heads_ref).astype(BF16) for t in (xb, xa)]
    values = [dot(t, v_w[...]).astype(BF16) for t in (xb, xa)]

    def tiles(t, group):
        low = 2 * group * CELLS
        return t[low : low + CELLS], t[low + CELLS : low + 2 * CELLS]

    def three(parts, group):
        zero, one = tiles(parts[0], group)
        ring = parts[1][group * CELLS : (group + 1) * CELLS]
        return (
            jnp.where(upper, one, zero),
            jnp.where(upper, zero, ring),
            jnp.where(upper, ring, one),
        )

    upper_wide = lax.broadcasted_iota(jnp.int32, (CELLS, n_heads * CELLS), 0) % WIN < HALF
    for group in range(groups):
        zero, one = tiles(q, group)
        inside, over, under = three(keys, group)
        column = step * groups + group
        cut = ((column == 0) & (col == 0)) | ((column == n_half // 2) & (col == last_col))
        cut = cut.astype(jnp.int32)
        rows = slice(2 * group * CELLS, (2 * group + 1) * CELLS)
        scores = scores_of(jnp.where(upper, one, zero), inside, mask_ref)
        p_ref[rows, :] = jnp.exp2(scores + bias_ref[cut]).astype(BF16)
        edge = jnp.where(upper, zero, one)
        scores = jnp.where(
            upper_wide, scores_of(edge, over, mask_ref), scores_of(edge, under, mask_ref)
        )
        rows = slice((2 * group + 1) * CELLS, (2 * group + 2) * CELLS)
        p_ref[rows, :] = jnp.exp2(scores + bias_ref[2 + cut]).astype(BF16)
    totals = totals_of(p_ref[...], ones_ref)
    mixed = []
    for group in range(groups):
        inside, over, under = three(values, group)
        rows = slice(2 * group * CELLS, (2 * group + 1) * CELLS)
        middle = weighted(p_ref[rows, :], *spread_heads(inside, mask_ref)) / totals[rows]
        rows = slice((2 * group + 1) * CELLS, (2 * group + 2) * CELLS)
        p = p_ref[rows, :]
        edge = jnp.where(
            upper,
            weighted(p, *spread_heads(over, mask_ref)),
            weighted(p, *spread_heads(under, mask_ref)),
        ) / totals[rows]
        mixed += [jnp.where(upper, edge, middle), jnp.where(upper, middle, edge)]
    mixed = jnp.concatenate(mixed, 0)
    y = dense_tail(xb.astype(F32), mixed, proj_ref, up_ref, down_ref, gain_ref).astype(F32)

    for group in range(groups):
        zero, one = tiles(y, group)
        for half in range(2):
            slabs = []
            for w in range(half * HALF, (half + 1) * HALF):
                rows = slice(w * WIN, (w + 1) * WIN)
                slabs.append(jnp.concatenate([zero[rows], one[rows]], 0))
            strip = jnp.concatenate(slabs, 1).astype(BF16)
            at = first_half + 2 * group + half - 1

            @pl.when((at >= 0) & (at < n_half))
            def _(at=at, strip=strip):
                width = HALF * n_feat
                out_ref[:, pl.ds(pl.multiple_of(at * width, 128), width)] = strip


def second_layer(place, temper, pieces, consts, params, groups=6):
    n_heads, n_feat = consts[3].shape
    n_half = pieces[0].shape[0]
    steps = -(-(n_half // 2 + 1) // groups)
    out = jax.ShapeDtypeStruct((2 * WIN, n_half * HALF * n_feat), BF16)
    return pl.pallas_call(
        functools.partial(second_kernel, groups),
        grid=(steps,),
        out_shape=out,
        in_specs=[SMEM, SMEM]
        + [ANY] * len(pieces)
        + [whole(a) for a in consts]
        + [one_layer(a, 1) for a in params],
        out_specs=whole(out),
        scratch_shapes=[pltpu.VMEM((4, CELLS, n_heads * CELLS), F32)]
        + layer_scratch(n_heads, n_feat)
        + [
            pltpu.VMEM((4, 2 * groups * steps, 32, n_feat), BF16),
            pltpu.VMEM((groups * 2 * CELLS, n_heads * CELLS), BF16),
            pltpu.SemaphoreType.DMA((len(pieces),)),
        ],
        compiler_params=pltpu.CompilerParams(vmem_limit_bytes=VMEM_BYTES),
        cost_estimate=pl.CostEstimate(flops=3 * 10**9, bytes_accessed=6 * 10**6, transcendentals=10**6),
        name="second_layer",
    )(place, temper, *pieces, *consts, *params)


def pack_kernel(me, codes_ref, arrived_ref, out_ref, held, sems):
    slots = out_ref.shape[0]
    codes = codes_ref[...]
    sender = lax.broadcasted_iota(jnp.int32, codes.shape, 0)
    copies = []
    for slot in range(slots):
        hit = jnp.where(codes == me[0] * slots + slot, sender, 0).astype(F32)
        source = jnp.sum(hit).astype(jnp.int32)
        copies.append(pltpu.make_async_copy(arrived_ref.at[source], held.at[slot], sems.at[slot]))
        copies[-1].start()
    for copy in copies:
        copy.wait()
    lane = lax.broadcasted_iota(jnp.int32, (slots, 128), 1)

    def rows_of(at):
        return jnp.swapaxes(held[:, at : at + WIN, :].astype(F32), 0, 1)

    for pair in range(WIN // 2):
        even = rows_of(2 * pair * WIN)
        odd = rows_of((2 * pair + 1) * WIN)
        tails = rows_of(CELLS + pair * WIN)
        for u in range(WIN):
            moved = pltpu.roll(odd[u], 64, 1)
            joined = [
                even[u],
                jnp.where(lane < 64, tails[u], moved),
                jnp.where(lane < 64, moved, tails[u]),
            ]
            at = (u * WIN + 2 * pair) * 192
            out_ref[:, at : at + 384] = jnp.concatenate(joined, 1).astype(BF16)


def pack_rows(me, codes, arrived, slots, width):
    return pl.pallas_call(
        pack_kernel,
        out_shape=jax.ShapeDtypeStruct((slots, width), BF16),
        in_specs=[SMEM, pl.BlockSpec(memory_space=pltpu.VMEM), ANY],
        out_specs=pl.BlockSpec(memory_space=pltpu.VMEM),
        scratch_shapes=[
            pltpu.VMEM((slots,) + arrived.shape[1:], BF16),
            pltpu.SemaphoreType.DMA((slots,)),
        ],
        compiler_params=pltpu.CompilerParams(vmem_limit_bytes=VMEM_BYTES),
        name="pack_rows",
    )(me, codes, arrived)


def moved(block, rows, cols):
    n_row, n_col = lax.axis_size("row"), lax.axis_size("col")
    route = [
        (r * n_col + c, (r + rows) % n_row * n_col + (c + cols) % n_col)
        for r in range(n_row)
        for c in range(n_col)
    ]
    return lax.ppermute(block, ("row", "col"), route)


def local(
    embedded,
    window_target_device,
    window_device_slot,
    cloud_mask_token,
    query_key_value_weight,
    projection_weight,
    up_weight,
    down_weight,
    bias_net_input_weight,
    bias_net_first_bias,
    bias_net_output_weight,
    temper,
    norm_gain_values,
):
    n_row, n_col = lax.axis_size("row"), lax.axis_size("col")
    n_heads, n_feat = temper.shape[1], cloud_mask_token.shape[0]
    slots = window_target_device.size // 2
    row, col = lax.axis_index("row"), lax.axis_index("col")
    place = jnp.stack([row, col, n_row - 1, n_col - 1]).astype(jnp.int32)
    me = (row * n_col + col).astype(jnp.int32).reshape(1)
    consts = constants(n_heads, n_feat)
    params = (
        bias_net_input_weight,
        bias_net_first_bias[:, None, :],
        bias_net_output_weight,
        query_key_value_weight,
        projection_weight,
        up_weight,
        down_weight,
        norm_gain_values,
    )
    code = jnp.where(
        window_target_device >= 0, window_target_device * slots + window_device_slot, -1
    )
    codes = lax.all_gather(code.reshape(1, -1), ("row", "col"), axis=0, tiled=True)
    mid0, mid1, left, right, send = first_layer(
        embedded, window_target_device, temper, cloud_mask_token[None, :], consts, params, n_row * n_col
    )
    pieces = (
        mid0,
        mid1,
        moved(mid1, 1, 0),
        moved(mid0, -1, 0),
        moved(right, 0, 1),
        moved(left, 0, -1),
        moved(right, 1, 1),
        moved(left, 1, -1),
        moved(right, -1, 1),
        moved(left, -1, -1),
    )
    arrived = lax.all_to_all(send, ("row", "col"), split_axis=0, concat_axis=0, tiled=True)
    features = second_layer(place, temper, pieces, consts, params)
    packed = pack_rows(me, codes, arrived, slots, CELLS * n_feat)
    return features, packed


def solution(mesh):
    in_specs = (P("row", "col"),) * 3 + (P(),) * 10
    out_specs = (P("row", "col"), P(("row", "col"), None))
    return jax.shard_map(local, mesh=mesh, in_specs=in_specs, out_specs=out_specs, check_vma=False)
```

```python
import functools
import math

import jax
import jax.numpy as jnp
import numpy as np
from jax import lax
from jax.experimental import pallas as pl
from jax.experimental.pallas import tpu as pltpu
from jax.sharding import PartitionSpec as P

WIN = 8
HALF = WIN // 2
CELLS = WIN * WIN
LOG2E = math.log2(math.e)
F32 = jnp.float32
BF16 = jnp.bfloat16
VMEM_BYTES = 60 * 2**20
SMEM = pl.BlockSpec(memory_space=pltpu.SMEM)
ANY = pl.BlockSpec(memory_space=pl.ANY)


def log_step(offset):
    scaled = np.abs(offset).astype(np.float32) * np.float32(8.0 / (WIN - 1))
    return np.sign(offset) * np.log2(scaled + 1.0) / 3.0


def offset_coords():
    lane = np.arange(128)
    across = np.maximum(WIN - 1 - lane // WIN, 1 - WIN)
    down = np.concatenate([-(lane % WIN), np.minimum(WIN - lane % WIN, WIN - 1)])
    return np.stack([log_step(down), log_step(np.tile(across, 2))], 1).astype(np.float32)


def head_blocks(rows, row_block, cols, col_block):
    same = (np.arange(rows) // row_block)[:, None] == (np.arange(cols) // col_block)[None, :]
    return same.astype(np.float32)


def constants(n_heads, n_feat):
    per_head = n_feat // n_heads
    return (
        jnp.asarray(offset_coords(), F32),
        jnp.asarray(head_blocks(n_feat, per_head, n_feat, per_head), BF16),
        jnp.asarray(head_blocks(n_heads * CELLS, CELLS, n_feat, per_head), BF16),
        jnp.asarray(head_blocks(n_heads, 1, n_feat, per_head), BF16),
    )


def dot(a, b):
    return jnp.dot(a, b, preferred_element_type=F32)


def dot_nt(a, b):
    return lax.dot_general(a, b, (((1,), (1,)), ((), ())), preferred_element_type=F32)


def bias_strips(coords_ref, net_in, net_first, net_out, strips_ref):
    coords = coords_ref[...]
    units = jnp.maximum(
        coords[:, 0:1] * net_in[0:1, :] + coords[:, 1:2] * net_in[1:2, :] + net_first, 0.0
    )
    logits = lax.dot_general(
        net_out, units, (((1,), (1,)), ((), ())),
        precision=lax.Precision.HIGHEST, preferred_element_type=F32,
    )
    n_heads = logits.shape[0]
    logits = jnp.concatenate([logits, jnp.zeros((8 - n_heads, 256), F32)], 0)
    table = 16.0 * LOG2E / (1.0 + jnp.exp(-logits))
    before, after = table[:, :128], table[:, 128:]
    cell = lax.broadcasted_iota(jnp.int32, (8, 128), 1) % WIN
    for u in range(WIN):
        strip = jnp.where(
            cell >= u,
            pltpu.roll(before, u, 1) if u else before,
            pltpu.roll(after, (u - WIN) % 128, 1),
        )
        strips_ref[:, u, :] = strip


def turned(strip):
    cell = lax.broadcasted_iota(jnp.int32, (WIN, 128), 1) % WIN
    strip = pltpu.roll(strip, HALF, 0)
    return jnp.where(cell < HALF, pltpu.roll(strip, 128 - HALF, 1), pltpu.roll(strip, HALF, 1))


def bias_rows(strips, w):
    lane = lax.broadcasted_iota(jnp.int32, (WIN, 128), 1)
    back = (WIN - 1 - w) * WIN
    parts = []
    for pair in range(len(strips) // 2):
        low = pltpu.roll(strips[2 * pair], (128 - back) % 128, 1)
        high = pltpu.roll(strips[2 * pair + 1], (192 - back) % 128, 1)
        parts.append(jnp.where(lane < CELLS, low, high))
    return jnp.concatenate(parts, 1)


def layer_norm(values, gain_row):
    row_mean = jnp.mean(values, -1, keepdims=True)
    centred = values - row_mean
    spread = jnp.mean(centred * centred, -1, keepdims=True)
    return centred * lax.rsqrt(spread + 1e-05) * gain_row


def unit_vectors(t, heads_ref):
    t = t.astype(BF16).astype(F32)
    squares = dot((t * t).astype(BF16), heads_ref[...])
    return t * lax.rsqrt(squares + 1e-06)


def temper_row(temper, layer, mask_ref):
    row = jnp.zeros((1, mask_ref.shape[1]), F32)
    for h in range(mask_ref.shape[0]):
        row = row + (temper[layer, h] * LOG2E) * mask_ref[h : h + 1, :].astype(F32)
    return row


def spread_heads(t, mask_ref):
    low = [t[:, :128] * mask_ref[h : h + 1, :128] for h in range(4)]
    high = [t[:, 128:] * mask_ref[h : h + 1, 128:] for h in range(4, 6)]
    return jnp.concatenate(low, 0), jnp.concatenate(high, 0)


def scores_of(q, k, mask_ref):
    low, high = spread_heads(k, mask_ref)
    return jnp.concatenate([dot_nt(q[:, :128], low), dot_nt(q[:, 128:], high)], 1)


def weighted(p, low, high):
    return jnp.concatenate([dot(p[:, :256], low), dot(p[:, 256:], high)], 1)


def totals_of(p, ones_ref):
    return weighted(p, ones_ref[:256, :128], ones_ref[256:, 128:])


def dense_tail(x, mixed, proj_ref, up_ref, down_ref, gain_ref):
    attended = dot(mixed.astype(BF16), proj_ref[...])
    hidden = (x + layer_norm(attended, gain_ref[0:1, :])).astype(BF16)
    raised = dot(hidden, up_ref[...])
    expanded = (0.5 * raised * (1.0 + lax.erf(raised * math.sqrt(0.5)))).astype(BF16)
    reduced = dot_nt(expanded, down_ref[...])
    return (hidden.astype(F32) + layer_norm(reduced, gain_ref[1:2, :])).astype(BF16)


def split_weights(qkv_ref, q_w, k_w, v_w):
    n_feat = q_w.shape[0]
    q_w[...] = qkv_ref[:, :n_feat]
    k_w[...] = qkv_ref[:, n_feat : 2 * n_feat]
    v_w[...] = qkv_ref[:, 2 * n_feat :]


def half_rows(tile, lower):
    first = lax.broadcasted_iota(jnp.int32, (WIN, tile.shape[1]), 0) < HALF
    pairs = []
    for pair in range(2):
        even = tile[2 * pair * WIN : (2 * pair + 1) * WIN]
        odd = tile[(2 * pair + 1) * WIN : (2 * pair + 2) * WIN]
        if lower:
            pairs.append(jnp.where(first, pltpu.roll(even, HALF, 0), odd))
        else:
            pairs.append(jnp.where(first, even, pltpu.roll(odd, HALF, 0)))
    return jnp.concatenate(pairs, 0)


def ring_tile(upper, lower):
    first = lax.broadcasted_iota(jnp.int32, (WIN, upper.shape[1]), 0) < HALF
    tiles = []
    for pair in range(2):
        rows = slice(pair * WIN, (pair + 1) * WIN)
        up, low = upper[rows], lower[rows]
        tiles.append(jnp.where(first, up, pltpu.roll(low, HALF, 0)))
        tiles.append(jnp.where(first, pltpu.roll(up, HALF, 0), low))
    return jnp.concatenate(tiles, 0)


def first_kernel(
    groups,
    targets, slots, temper, emb_ref, token_ref, coords_ref, heads_ref, ones_ref, mask_ref,
    net_in, net_first, net_out, qkv_ref, proj_ref, up_ref, down_ref, gain_ref,
    mid0_ref, mid1_ref, upper_ref, lower_ref, left_ref, right_ref, send_ref,
    bias_ref, strips_ref, q_w, k_w, v_w, p_ref, staging, blank, sems, blank_sems,
):
    step = pl.program_id(0)
    n_heads, n_feat = mask_ref.shape

    n_blank = blank.shape[0]
    blanks = [
        pltpu.make_async_copy(blank, send_ref.at[pl.ds(n * n_blank, n_blank)], blank_sems.at[n])
        for n in range(send_ref.shape[0] // n_blank)
    ]

    @pl.when(step == 0)
    def _():
        blank[...] = jnp.full(blank.shape, -1.0, BF16)
        for copy in blanks:
            copy.start()
        bias_strips(coords_ref, net_in, net_first[0:1, :], net_out[:, 0, :], strips_ref)
        strips = [strips_ref[h] for h in range(n_heads)]
        for w in range(WIN):
            bias_ref[w * WIN : (w + 1) * WIN, :] = bias_rows(strips, w)
        split_weights(qkv_ref, q_w, k_w, v_w)

    tiles = []
    for group in range(groups):
        slabs = []
        for w in range(WIN):
            at = (group * WIN + w) * n_feat
            slabs.append(emb_ref[:, at : at + n_feat].astype(F32))
        for i in range(2):
            tiles.append(jnp.concatenate([s[i * WIN : (i + 1) * WIN] for s in slabs], 0))
    x = jnp.concatenate(tiles, 0)
    xb = x.astype(BF16)
    q = (unit_vectors(dot(xb, q_w[...]), heads_ref) * temper_row(temper, 0, mask_ref)).astype(BF16)
    k = unit_vectors(dot(xb, k_w[...]), heads_ref).astype(BF16)
    v = dot(xb, v_w[...]).astype(BF16)
    bias = bias_ref[...]
    mixed = []
    for n in range(2 * groups):
        rows = slice(n * CELLS, (n + 1) * CELLS)
        p_ref[rows, :] = jnp.exp2(scores_of(q[rows], k[rows], mask_ref) + bias).astype(BF16)
    for n in range(2 * groups):
        rows = slice(n * CELLS, (n + 1) * CELLS)
        mixed.append(weighted(p_ref[rows, :], *spread_heads(v[rows], mask_ref)))
    mixed = jnp.concatenate(mixed, 0) / totals_of(p_ref[...], ones_ref)

    @pl.when(step == 0)
    def _():
        for copy in blanks:
            copy.wait()

    y = dense_tail(x, mixed, proj_ref, up_ref, down_ref, gain_ref).astype(F32)

    token = token_ref[...].astype(F32).reshape(1, n_feat)
    for group in range(groups):
        for i in range(2):
            n = 2 * group + i
            j = step * groups + group
            target = targets[i, j]
            tile = y[n * CELLS : (n + 1) * CELLS]
            kept = jnp.where(target >= 0, tile, token)
            rows = kept.astype(BF16)
            mid = (mid0_ref, mid1_ref)[i]
            mid[2 * group] = rows[:32]
            mid[2 * group + 1] = rows[32:]
            halves = [half_rows(kept[half * 32 : (half + 1) * 32], i).astype(BF16) for half in range(2)]
            outward = (upper_ref, lower_ref)[i]
            outward[1 + 2 * j] = halves[0]
            outward[2 + 2 * j] = halves[1]
            if group == 0:

                @pl.when(step == 0)
                def _(i=i, rows=rows, halves=halves):
                    left_ref[i * 32 : (i + 1) * 32] = rows[:32]
                    left_ref[64 + i * 16 : 80 + i * 16] = halves[0]

            if group == groups - 1:

                @pl.when(step == pl.num_programs(0) - 1)
                def _(i=i, rows=rows, halves=halves):
                    right_ref[i * 32 : (i + 1) * 32] = rows[32:]
                    right_ref[64 + i * 16 : 80 + i * 16] = halves[1]

            slot = j * 2 + i
            staging[slot, :64] = tile[:, :128].astype(BF16)
            tails = tile[:, 128:].reshape(4, 2, WIN, 64)
            joined = jnp.concatenate([tails[:, 0], tails[:, 1]], -1)
            staging[slot, 64:96] = joined.reshape(32, 128).astype(BF16)
            staging[slot, 96:] = jnp.full((8, 128), slots[i, j].astype(F32)).astype(BF16)

            @pl.when(target >= 0)
            def _(slot=slot, target=target):
                pltpu.make_async_copy(staging.at[slot], send_ref.at[target], sems.at[slot]).start()

    @pl.when(step == pl.num_programs(0) - 1)
    def _():
        def finish(slot, carry):
            target = targets[lax.rem(slot, 2), slot // 2]

            @pl.when(target >= 0)
            def _():
                pltpu.make_async_copy(staging.at[slot], send_ref.at[target], sems.at[slot]).wait()

            return carry

        lax.fori_loop(0, staging.shape[0], finish, 0)


def whole(array):
    zeros = (0,) * array.ndim
    return pl.BlockSpec(array.shape, lambda *_: zeros)


def layer_spec(array, position, layer):
    if position in (1, 2):
        return whole(array)
    rest = array.shape[1:]
    at = (layer,) + (0,) * len(rest)
    return pl.BlockSpec((None,) + rest, lambda *_: at)


def layer_scratch(n_heads, n_feat):
    square = pltpu.VMEM((n_feat, n_feat), BF16)
    return [pltpu.VMEM((8, WIN, 128), F32), square, square, square]


def first_layer(embedded, targets, slots, temper, token, consts, params, devices, groups=8):
    n_heads, n_feat = consts[3].shape
    columns = embedded.shape[1] // (WIN * n_feat)
    side = jax.ShapeDtypeStruct((96, n_feat), BF16)
    outward = jax.ShapeDtypeStruct((2 * columns + 2, 16, n_feat), BF16)
    mid = jax.ShapeDtypeStruct((2 * columns, 32, n_feat), BF16)
    mid_spec = pl.BlockSpec((2 * groups, 32, n_feat), lambda g: (g, 0, 0))
    return pl.pallas_call(
        functools.partial(first_kernel, groups),
        grid=(columns // groups,),
        out_shape=(mid, mid, outward, outward, side, side, jax.ShapeDtypeStruct((devices, 104, 128), BF16)),
        in_specs=[SMEM, SMEM, SMEM, pl.BlockSpec((2 * WIN, groups * WIN * n_feat), lambda g: (0, g))]
        + [whole(a) for a in (token,) + consts]
        + [layer_spec(a, n, 0) for n, a in enumerate(params)],
        out_specs=(mid_spec, mid_spec, whole(outward), whole(outward), whole(side), whole(side), ANY),
        scratch_shapes=[pltpu.VMEM((CELLS, n_heads * CELLS), F32)]
        + layer_scratch(n_heads, n_feat)
        + [
            pltpu.VMEM((groups * 2 * CELLS, n_heads * CELLS), BF16),
            pltpu.VMEM((2 * columns, 104, 128), BF16),
            pltpu.VMEM((devices // 8, 104, 128), BF16),
            pltpu.SemaphoreType.DMA((2 * columns,)),
            pltpu.SemaphoreType.DMA((8,)),
        ],
        compiler_params=pltpu.CompilerParams(vmem_limit_bytes=VMEM_BYTES),
        cost_estimate=pl.CostEstimate(flops=2 * 10**9, bytes_accessed=6 * 10**6, transcendentals=10**6),
        name="first_layer",
    )(targets, slots, temper, embedded, token, *consts, *params)


def corner_kernel(left_ref, right_ref, up_in, low_in, up_ref, low_ref, sems):
    del up_in, low_in
    end = up_ref.shape[0] - 1
    copies = [
        pltpu.make_async_copy(left_ref.at[pl.ds(64, 16)], up_ref.at[0], sems.at[0]),
        pltpu.make_async_copy(right_ref.at[pl.ds(64, 16)], up_ref.at[end], sems.at[1]),
        pltpu.make_async_copy(left_ref.at[pl.ds(80, 16)], low_ref.at[0], sems.at[2]),
        pltpu.make_async_copy(right_ref.at[pl.ds(80, 16)], low_ref.at[end], sems.at[3]),
    ]
    for copy in copies:
        copy.start()
    for copy in copies:
        copy.wait()


def add_corners(left, right, upper, lower):
    shape = jax.ShapeDtypeStruct(upper.shape, upper.dtype)
    return pl.pallas_call(
        corner_kernel,
        out_shape=(shape, shape),
        in_specs=[ANY] * 4,
        out_specs=(ANY, ANY),
        scratch_shapes=[pltpu.SemaphoreType.DMA((4,))],
        input_output_aliases={2: 0, 3: 1},
        name="add_corners",
    )(left, right, upper, lower)


def second_kernel(
    groups,
    place, temper, mid0_ref, mid1_ref, above_ref, below_ref, left_ref, right_ref,
    coords_ref, heads_ref, ones_ref, mask_ref,
    net_in, net_first, net_out, qkv_ref, proj_ref, up_ref, down_ref, gain_ref,
    out_ref,
    bias_ref, strips_ref, q_w, k_w, v_w, ext, upper_ring, lower_ring, p_ref, sems,
):
    step = pl.program_id(0)
    n_heads, n_feat = mask_ref.shape
    n_half = mid0_ref.shape[0]
    row, col, last_row, last_col = place[0], place[1], place[2], place[3]

    @pl.when(step == 0)
    def _():
        inner, every = pl.ds(1, n_half), pl.ds(0, n_half + 2)
        end = n_half + 1
        copies = [
            pltpu.make_async_copy(src, dst, sems.at[n])
            for n, (src, dst) in enumerate(
                [
                    (mid0_ref, ext.at[0, inner]),
                    (mid1_ref, ext.at[1, inner]),
                    (left_ref.at[pl.ds(0, 32)], ext.at[0, 0]),
                    (left_ref.at[pl.ds(32, 32)], ext.at[1, 0]),
                    (right_ref.at[pl.ds(0, 32)], ext.at[0, end]),
                    (right_ref.at[pl.ds(32, 32)], ext.at[1, end]),
                    (above_ref, lower_ring.at[every]),
                    (below_ref, upper_ring.at[every]),
                ]
            )
        ]
        for copy in copies:
            copy.start()
        for spare in range(n_half + 2, ext.shape[1]):
            ext[:, spare] = jnp.zeros((2, 32, n_feat), BF16)
            upper_ring[spare] = jnp.zeros((16, n_feat), BF16)
            lower_ring[spare] = jnp.zeros((16, n_feat), BF16)
        split_weights(qkv_ref, q_w, k_w, v_w)
        bias_strips(coords_ref, net_in, net_first[1:2, :], net_out[:, 1, :], strips_ref)
        strips = [turned(strips_ref[h]) for h in range(n_heads)]
        lane = lax.broadcasted_iota(jnp.int32, (WIN, n_heads * CELLS), 1)
        upper = lax.broadcasted_iota(jnp.int32, (WIN, n_heads * CELLS), 0) < HALF
        other_rows = upper != (lane % WIN < HALF)
        top, bottom = row == 0, row == last_row
        edge_rows = other_rows & ((upper & top) | (~upper & bottom))
        for w in range(WIN):
            other_cols = (lane % CELLS >= CELLS // 2) != (w >= HALF)
            rows = slice(w * WIN, (w + 1) * WIN)
            bias = bias_rows(strips, w)
            away = -100.0 * LOG2E
            bias_ref[0, rows, :] = bias
            bias_ref[1, rows, :] = bias + jnp.where(other_cols, away, 0.0)
            bias_ref[2, rows, :] = bias + jnp.where(edge_rows, away, 0.0)
            bias_ref[3, rows, :] = bias + jnp.where(edge_rows | other_cols, away, 0.0)
        for copy in copies:
            copy.wait()

    first_half = 2 * groups * step
    upper = lax.broadcasted_iota(jnp.int32, (CELLS, n_feat), 0) % WIN < HALF

    def tile_of(line, group):
        return jnp.concatenate(
            [ext[line, first_half + 2 * group], ext[line, first_half + 2 * group + 1]], 0
        )

    own, around = [], []
    for group in range(groups):
        own += [tile_of(0, group), tile_of(1, group)]
        for half in range(2):
            at = first_half + 2 * group + half
            around.append(
                ring_tile(upper_ring[at].astype(F32), lower_ring[at].astype(F32)).astype(BF16)
            )
    xb = jnp.concatenate(own, 0)
    xa = jnp.concatenate(around, 0)
    q = (unit_vectors(dot(xb, q_w[...]), heads_ref) * temper_row(temper, 1, mask_ref)).astype(BF16)
    keys = [unit_vectors(dot(t, k_w[...]), heads_ref).astype(BF16) for t in (xb, xa)]
    values = [dot(t, v_w[...]).astype(BF16) for t in (xb, xa)]

    def tiles(t, group):
        low = 2 * group * CELLS
        return t[low : low + CELLS], t[low + CELLS : low + 2 * CELLS]

    def three(parts, group):
        zero, one = tiles(parts[0], group)
        ring = parts[1][group * CELLS : (group + 1) * CELLS]
        return (
            jnp.where(upper, one, zero),
            jnp.where(upper, zero, ring),
            jnp.where(upper, ring, one),
        )

    upper_wide = lax.broadcasted_iota(jnp.int32, (CELLS, n_heads * CELLS), 0) % WIN < HALF
    for group in range(groups):
        zero, one = tiles(q, group)
        inside, over, under = three(keys, group)
        column = step * groups + group
        cut = ((column == 0) & (col == 0)) | ((column == n_half // 2) & (col == last_col))
        cut = cut.astype(jnp.int32)
        rows = slice(2 * group * CELLS, (2 * group + 1) * CELLS)
        scores = scores_of(jnp.where(upper, one, zero), inside, mask_ref)
        p_ref[rows, :] = jnp.exp2(scores + bias_ref[cut]).astype(BF16)
        edge = jnp.where(upper, zero, one)
        scores = jnp.where(
            upper_wide, scores_of(edge, over, mask_ref), scores_of(edge, under, mask_ref)
        )
        rows = slice((2 * group + 1) * CELLS, (2 * group + 2) * CELLS)
        p_ref[rows, :] = jnp.exp2(scores + bias_ref[2 + cut]).astype(BF16)
    totals = totals_of(p_ref[...], ones_ref)
    mixed = []
    for group in range(groups):
        inside, over, under = three(values, group)
        rows = slice(2 * group * CELLS, (2 * group + 1) * CELLS)
        middle = weighted(p_ref[rows, :], *spread_heads(inside, mask_ref)) / totals[rows]
        rows = slice((2 * group + 1) * CELLS, (2 * group + 2) * CELLS)
        p = p_ref[rows, :]
        edge = jnp.where(
            upper,
            weighted(p, *spread_heads(over, mask_ref)),
            weighted(p, *spread_heads(under, mask_ref)),
        ) / totals[rows]
        mixed += [jnp.where(upper, edge, middle), jnp.where(upper, middle, edge)]
    mixed = jnp.concatenate(mixed, 0)
    y = dense_tail(xb.astype(F32), mixed, proj_ref, up_ref, down_ref, gain_ref).astype(F32)

    for group in range(groups):
        zero, one = tiles(y, group)
        for half in range(2):
            slabs = []
            for w in range(half * HALF, (half + 1) * HALF):
                rows = slice(w * WIN, (w + 1) * WIN)
                slabs.append(jnp.concatenate([zero[rows], one[rows]], 0))
            strip = jnp.concatenate(slabs, 1).astype(BF16)
            at = first_half + 2 * group + half - 1

            @pl.when((at >= 0) & (at < n_half))
            def _(at=at, strip=strip):
                width = HALF * n_feat
                out_ref[:, pl.ds(pl.multiple_of(at * width, 128), width)] = strip


def second_layer(place, temper, pieces, consts, params, groups=6):
    n_heads, n_feat = consts[3].shape
    n_half = pieces[0].shape[0]
    steps = -(-(n_half // 2 + 1) // groups)
    out = jax.ShapeDtypeStruct((2 * WIN, n_half * HALF * n_feat), BF16)
    return pl.pallas_call(
        functools.partial(second_kernel, groups),
        grid=(steps,),
        out_shape=out,
        in_specs=[SMEM, SMEM]
        + [ANY] * len(pieces)
        + [whole(a) for a in consts]
        + [layer_spec(a, n, 1) for n, a in enumerate(params)],
        out_specs=whole(out),
        scratch_shapes=[pltpu.VMEM((4, CELLS, n_heads * CELLS), F32)]
        + layer_scratch(n_heads, n_feat)
        + [
            pltpu.VMEM((2, 2 * groups * steps, 32, n_feat), BF16),
            pltpu.VMEM((2 * groups * steps, 16, n_feat), BF16),
            pltpu.VMEM((2 * groups * steps, 16, n_feat), BF16),
            pltpu.VMEM((groups * 2 * CELLS, n_heads * CELLS), BF16),
            pltpu.SemaphoreType.DMA((8,)),
        ],
        compiler_params=pltpu.CompilerParams(vmem_limit_bytes=VMEM_BYTES),
        cost_estimate=pl.CostEstimate(flops=10**11, bytes_accessed=10**7, transcendentals=10**6),
        name="second_layer",
    )(place, temper, *pieces, *consts, *params)


def pack_kernel(entries_ref, out_ref, arrived_ref, sems):
    slots = out_ref.shape[0]
    part = arrived_ref.shape[0] // 8
    copies = [
        pltpu.make_async_copy(
            entries_ref.at[pl.ds(n * part, part)], arrived_ref.at[pl.ds(n * part, part)], sems.at[n]
        )
        for n in range(8)
    ]
    for copy in copies:
        copy.start()
    for copy in copies:
        copy.wait()
    marks = arrived_ref[:, 96:, :].astype(F32)
    lane = lax.broadcasted_iota(jnp.int32, marks.shape, 2).astype(F32)
    sender = lax.broadcasted_iota(jnp.int32, marks.shape, 0).astype(F32)
    found = jnp.max(jnp.where(marks == lane, sender, 0.0), 0).astype(jnp.int32)
    sources = [found[0, slot] for slot in range(slots)]
    lane = lax.broadcasted_iota(jnp.int32, (slots, 128), 1)

    def rows_of(at):
        rows = [arrived_ref[source, at : at + WIN, :].astype(F32) for source in sources]
        return jnp.swapaxes(jnp.stack(rows, 0), 0, 1)

    for pair in range(WIN // 2):
        even = rows_of(2 * pair * WIN)
        odd = rows_of((2 * pair + 1) * WIN)
        tails = rows_of(CELLS + pair * WIN)
        for u in range(WIN):
            moved = pltpu.roll(odd[u], 64, 1)
            joined = [
                even[u],
                jnp.where(lane < 64, tails[u], moved),
                jnp.where(lane < 64, moved, tails[u]),
            ]
            at = (u * WIN + 2 * pair) * 192
            out_ref[:, at : at + 384] = jnp.concatenate(joined, 1).astype(BF16)


def pack_rows(arrived, slots, width):
    return pl.pallas_call(
        pack_kernel,
        out_shape=jax.ShapeDtypeStruct((slots, width), BF16),
        in_specs=[ANY],
        out_specs=pl.BlockSpec(memory_space=pltpu.VMEM),
        scratch_shapes=[pltpu.VMEM(arrived.shape, BF16), pltpu.SemaphoreType.DMA((8,))],
        compiler_params=pltpu.CompilerParams(vmem_limit_bytes=VMEM_BYTES),
        name="pack_rows",
    )(arrived)


def moved(block, rows, cols):
    n_row, n_col = lax.axis_size("row"), lax.axis_size("col")
    route = [
        (r * n_col + c, (r + rows) % n_row * n_col + (c + cols) % n_col)
        for r in range(n_row)
        for c in range(n_col)
    ]
    return lax.ppermute(block, ("row", "col"), route)


def local(
    embedded,
    window_target_device,
    window_device_slot,
    cloud_mask_token,
    query_key_value_weight,
    projection_weight,
    up_weight,
    down_weight,
    bias_net_input_weight,
    bias_net_first_bias,
    bias_net_output_weight,
    temper,
    norm_gain_values,
):
    n_row, n_col = lax.axis_size("row"), lax.axis_size("col")
    n_heads, n_feat = temper.shape[1], cloud_mask_token.shape[0]
    slots = window_target_device.size // 2
    row, col = lax.axis_index("row"), lax.axis_index("col")
    place = jnp.stack([row, col, n_row - 1, n_col - 1]).astype(jnp.int32)
    consts = constants(n_heads, n_feat)
    params = (
        bias_net_input_weight,
        bias_net_first_bias,
        jnp.transpose(bias_net_output_weight, (2, 0, 1)),
        query_key_value_weight,
        projection_weight,
        up_weight,
        jnp.swapaxes(down_weight, 1, 2),
        norm_gain_values,
    )
    mid0, mid1, upper, lower, left, right, send = first_layer(
        embedded, window_target_device, window_device_slot, temper, cloud_mask_token, consts, params,
        n_row * n_col,
    )
    left, right = moved(right, 0, 1), moved(left, 0, -1)
    upper, lower = add_corners(left, right, upper, lower)
    send, upper, lower = lax.optimization_barrier((send, upper, lower))
    pieces = (mid0, mid1, moved(lower, 1, 0), moved(upper, -1, 0), left, right)
    arrived = lax.all_to_all(send, ("row", "col"), split_axis=0, concat_axis=0, tiled=True)
    features = second_layer(place, temper, pieces, consts, params)
    packed = pack_rows(arrived, slots, CELLS * n_feat)
    return features, packed


def solution(mesh):
    in_specs = (P("row", "col"),) * 3 + (P(),) * 10
    out_specs = (P("row", "col"), P(("row", "col"), None))
    return jax.shard_map(local, mesh=mesh, in_specs=in_specs, out_specs=out_specs, check_vma=False)
```

```python
import functools
import math

import jax
import jax.numpy as jnp
import numpy as np
from jax import lax
from jax.experimental import pallas as pl
from jax.experimental.pallas import tpu as pltpu
from jax.sharding import PartitionSpec as P

WIN = 8
HALF = WIN // 2
CELLS = WIN * WIN
LOG2E = math.log2(math.e)
F32 = jnp.float32
BF16 = jnp.bfloat16
VMEM_BYTES = 60 * 2**20
SMEM = pl.BlockSpec(memory_space=pltpu.SMEM)
ANY = pl.BlockSpec(memory_space=pl.ANY)
HBM = pl.BlockSpec(memory_space=pltpu.HBM)


def log_step(offset):
    scaled = np.abs(offset).astype(np.float32) * np.float32(8.0 / (WIN - 1))
    return np.sign(offset) * np.log2(scaled + 1.0) / 3.0


def offset_coords():
    lane = np.arange(128)
    across = np.maximum(WIN - 1 - lane // WIN, 1 - WIN)
    down = np.concatenate([-(lane % WIN), np.minimum(WIN - lane % WIN, WIN - 1)])
    return np.stack([log_step(down), log_step(np.tile(across, 2))], 1).astype(np.float32)


def head_blocks(rows, row_block, cols, col_block):
    same = (np.arange(rows) // row_block)[:, None] == (np.arange(cols) // col_block)[None, :]
    return same.astype(np.float32)


def constants(n_heads, n_feat):
    per_head = n_feat // n_heads
    return (
        jnp.asarray(offset_coords(), F32),
        jnp.asarray(head_blocks(n_feat, per_head, n_feat, per_head), BF16),
        jnp.asarray(head_blocks(n_heads * CELLS, CELLS, n_feat, per_head), BF16),
        jnp.asarray(head_blocks(n_heads, 1, n_feat, per_head), BF16),
    )


def dot(a, b):
    return jnp.dot(a, b, preferred_element_type=F32)


def dot_nt(a, b):
    return lax.dot_general(a, b, (((1,), (1,)), ((), ())), preferred_element_type=F32)


def bias_strips(coords_ref, net_in, net_first, net_out, strips_ref):
    coords = coords_ref[...]
    units = jnp.maximum(
        coords[:, 0:1] * net_in[0:1, :] + coords[:, 1:2] * net_in[1:2, :] + net_first, 0.0
    )
    logits = lax.dot_general(
        net_out, units, (((1,), (1,)), ((), ())),
        precision=lax.Precision.HIGHEST, preferred_element_type=F32,
    )
    n_heads = logits.shape[0]
    logits = jnp.concatenate([logits, jnp.zeros((8 - n_heads, 256), F32)], 0)
    table = 16.0 * LOG2E / (1.0 + jnp.exp(-logits))
    before, after = table[:, :128], table[:, 128:]
    cell = lax.broadcasted_iota(jnp.int32, (8, 128), 1) % WIN
    for u in range(WIN):
        strip = jnp.where(
            cell >= u,
            pltpu.roll(before, u, 1) if u else before,
            pltpu.roll(after, (u - WIN) % 128, 1),
        )
        strips_ref[:, u, :] = strip


def turned(strip):
    cell = lax.broadcasted_iota(jnp.int32, (WIN, 128), 1) % WIN
    strip = pltpu.roll(strip, HALF, 0)
    return jnp.where(cell < HALF, pltpu.roll(strip, 128 - HALF, 1), pltpu.roll(strip, HALF, 1))


def bias_rows(strips, w):
    lane = lax.broadcasted_iota(jnp.int32, (WIN, 128), 1)
    back = (WIN - 1 - w) * WIN
    parts = []
    for pair in range(len(strips) // 2):
        low = pltpu.roll(strips[2 * pair], (128 - back) % 128, 1)
        high = pltpu.roll(strips[2 * pair + 1], (192 - back) % 128, 1)
        parts.append(jnp.where(lane < CELLS, low, high))
    return jnp.concatenate(parts, 1)


def layer_norm(values, gain_row):
    row_mean = jnp.mean(values, -1, keepdims=True)
    centred = values - row_mean
    spread = jnp.mean(centred * centred, -1, keepdims=True)
    return centred * lax.rsqrt(spread + 1e-05) * gain_row


def unit_vectors(t, heads_ref):
    t = t.astype(BF16).astype(F32)
    squares = dot((t * t).astype(BF16), heads_ref[...])
    return t * lax.rsqrt(squares + 1e-06)


def temper_row(temper, layer, mask_ref):
    row = jnp.zeros((1, mask_ref.shape[1]), F32)
    for h in range(mask_ref.shape[0]):
        row = row + (temper[layer, h] * LOG2E) * mask_ref[h : h + 1, :].astype(F32)
    return row


def spread_heads(t, mask_ref):
    low = [t[:, :128] * mask_ref[h : h + 1, :128] for h in range(4)]
    high = [t[:, 128:] * mask_ref[h : h + 1, 128:] for h in range(4, 6)]
    return jnp.concatenate(low, 0), jnp.concatenate(high, 0)


def scores_of(q, k, mask_ref):
    low, high = spread_heads(k, mask_ref)
    return jnp.concatenate([dot_nt(q[:, :128], low), dot_nt(q[:, 128:], high)], 1)


def weighted(p, low, high):
    return jnp.concatenate([dot(p[:, :256], low), dot(p[:, 256:], high)], 1)


def totals_of(p, ones_ref):
    return weighted(p, ones_ref[:256, :128], ones_ref[256:, 128:])


def dense_tail(x, mixed, proj_ref, up_ref, down_ref, gain_ref):
    attended = dot(mixed.astype(BF16), proj_ref[...])
    hidden = (x + layer_norm(attended, gain_ref[0:1, :])).astype(BF16)
    raised = dot(hidden, up_ref[...])
    expanded = (0.5 * raised * (1.0 + lax.erf(raised * math.sqrt(0.5)))).astype(BF16)
    reduced = dot_nt(expanded, down_ref[...])
    return (hidden.astype(F32) + layer_norm(reduced, gain_ref[1:2, :])).astype(BF16)


def attend(x, q_w, k_w, v_w, temper, heads_ref, ones_ref, mask_ref, bias_of, p_ref):
    n_windows = x.shape[0] // CELLS
    q = (unit_vectors(dot(x, q_w[...]), heads_ref) * temper).astype(BF16)
    k = unit_vectors(dot(x, k_w[...]), heads_ref).astype(BF16)
    v = dot(x, v_w[...]).astype(BF16)
    mixed = []
    for n in range(n_windows):
        rows = slice(n * CELLS, (n + 1) * CELLS)
        p_ref[rows, :] = jnp.exp2(scores_of(q[rows], k[rows], mask_ref) + bias_of(n)).astype(BF16)
    for n in range(n_windows):
        rows = slice(n * CELLS, (n + 1) * CELLS)
        mixed.append(weighted(p_ref[rows, :], *spread_heads(v[rows], mask_ref)))
    return jnp.concatenate(mixed, 0) / totals_of(p_ref[...], ones_ref)


def split_weights(qkv_ref, q_w, k_w, v_w):
    n_feat = q_w.shape[0]
    q_w[...] = qkv_ref[:, :n_feat]
    k_w[...] = qkv_ref[:, n_feat : 2 * n_feat]
    v_w[...] = qkv_ref[:, 2 * n_feat :]


def half_rows(tile):
    first = lax.broadcasted_iota(jnp.int32, (WIN, tile.shape[1]), 0) < HALF
    pairs = []
    for pair in range(2):
        even = tile[2 * pair * WIN : (2 * pair + 1) * WIN]
        odd = tile[(2 * pair + 1) * WIN : (2 * pair + 2) * WIN]
        pairs.append(jnp.where(first, even, pltpu.roll(odd, HALF, 0)))
    return jnp.concatenate(pairs, 0)


def whole_rows(halves):
    tiles = []
    for pair in range(2):
        rows = halves[pair * WIN : (pair + 1) * WIN]
        tiles += [rows, pltpu.roll(rows, HALF, 0)]
    return jnp.concatenate(tiles, 0)


def first_kernel(
    groups,
    targets, slots, temper, emb_ref, token_ref, coords_ref, heads_ref, ones_ref, mask_ref,
    net_in, net_first, net_out, qkv_ref, proj_ref, up_ref, down_ref, gain_ref,
    mid0_ref, mid1_ref, upper_ref, left_ref, send_ref,
    bias_ref, strips_ref, q_w, k_w, v_w, p_ref, staging, blank, sems, blank_sems,
):
    step = pl.program_id(0)
    n_heads, n_feat = mask_ref.shape

    n_blank = blank.shape[0]
    blanks = [
        pltpu.make_async_copy(blank, send_ref.at[pl.ds(n * n_blank, n_blank)], blank_sems.at[n])
        for n in range(send_ref.shape[0] // n_blank)
    ]

    @pl.when(step == 0)
    def _():
        blank[...] = jnp.full(blank.shape, -1.0, BF16)
        for copy in blanks:
            copy.start()
        bias_strips(coords_ref, net_in, net_first[0:1, :], net_out[:, 0, :], strips_ref)
        strips = [strips_ref[h] for h in range(n_heads)]
        for w in range(WIN):
            bias_ref[w * WIN : (w + 1) * WIN, :] = bias_rows(strips, w)
        split_weights(qkv_ref, q_w, k_w, v_w)

    tiles = []
    for group in range(groups):
        slabs = []
        for w in range(WIN):
            at = (group * WIN + w) * n_feat
            slabs.append(emb_ref[:, at : at + n_feat].astype(F32))
        for i in range(2):
            tiles.append(jnp.concatenate([s[i * WIN : (i + 1) * WIN] for s in slabs], 0))
    x = jnp.concatenate(tiles, 0)
    mixed = attend(
        x.astype(BF16), q_w, k_w, v_w, temper_row(temper, 0, mask_ref), heads_ref, ones_ref, mask_ref,
        lambda n: bias_ref[...], p_ref,
    )

    @pl.when(step == 0)
    def _():
        for copy in blanks:
            copy.wait()

    y = dense_tail(x, mixed, proj_ref, up_ref, down_ref, gain_ref).astype(F32)

    token = token_ref[...].astype(F32).reshape(1, n_feat)
    for group in range(groups):
        for i in range(2):
            n = 2 * group + i
            j = step * groups + group
            target = targets[i, j]
            tile = y[n * CELLS : (n + 1) * CELLS]
            kept = jnp.where(target >= 0, tile, token)
            rows = kept.astype(BF16)
            mid = (mid0_ref, mid1_ref)[i]
            mid[2 * group] = rows[:32]
            mid[2 * group + 1] = rows[32:]
            if i == 0:
                halves = [half_rows(kept[half * 32 : (half + 1) * 32]).astype(BF16) for half in range(2)]
                upper_ref[2 * group] = halves[0]
                upper_ref[2 * group + 1] = halves[1]
            if group == 0:

                @pl.when(step == 0)
                def _(i=i, rows=rows, halves=halves):
                    left_ref[i * 32 : (i + 1) * 32] = rows[:32]
                    if i == 0:
                        left_ref[64:] = halves[0]

            slot = j * 2 + i
            staging[slot, :64] = tile[:, :128].astype(BF16)
            tails = tile[:, 128:].reshape(4, 2, WIN, 64)
            joined = jnp.concatenate([tails[:, 0], tails[:, 1]], -1)
            staging[slot, 64:96] = joined.reshape(32, 128).astype(BF16)
            staging[slot, 96:] = jnp.full((8, 128), slots[i, j].astype(F32)).astype(BF16)

            @pl.when(target >= 0)
            def _(slot=slot, target=target):
                pltpu.make_async_copy(staging.at[slot], send_ref.at[target], sems.at[slot]).start()

    @pl.when(step == pl.num_programs(0) - 1)
    def _():
        def finish(slot, carry):
            target = targets[lax.rem(slot, 2), slot // 2]

            @pl.when(target >= 0)
            def _():
                pltpu.make_async_copy(staging.at[slot], send_ref.at[target], sems.at[slot]).wait()

            return carry

        lax.fori_loop(0, staging.shape[0], finish, 0)


def whole(array):
    zeros = (0,) * array.ndim
    return pl.BlockSpec(array.shape, lambda *_: zeros)


def layer_spec(array, position, layer):
    if position in (1, 2):
        return whole(array)
    rest = array.shape[1:]
    at = (layer,) + (0,) * len(rest)
    return pl.BlockSpec((None,) + rest, lambda *_: at)


def layer_scratch(n_heads, n_feat):
    square = pltpu.VMEM((n_feat, n_feat), BF16)
    return [pltpu.VMEM((8, WIN, 128), F32), square, square, square]


def first_layer(embedded, targets, slots, temper, token, consts, params, devices, groups=8):
    n_heads, n_feat = consts[3].shape
    columns = embedded.shape[1] // (WIN * n_feat)
    side = jax.ShapeDtypeStruct((80, n_feat), BF16)
    upper = jax.ShapeDtypeStruct((2 * columns, 16, n_feat), BF16)
    mid = jax.ShapeDtypeStruct((2 * columns, 32, n_feat), BF16)
    mid_spec = pl.BlockSpec((2 * groups, 32, n_feat), lambda g: (g, 0, 0))
    return pl.pallas_call(
        functools.partial(first_kernel, groups),
        grid=(columns // groups,),
        out_shape=(mid, mid, upper, side, jax.ShapeDtypeStruct((devices, 104, 128), BF16)),
        in_specs=[SMEM, SMEM, SMEM, pl.BlockSpec((2 * WIN, groups * WIN * n_feat), lambda g: (0, g))]
        + [whole(a) for a in (token,) + consts]
        + [layer_spec(a, n, 0) for n, a in enumerate(params)],
        out_specs=(mid_spec, mid_spec, pl.BlockSpec((2 * groups, 16, n_feat), lambda g: (g, 0, 0)), whole(side), ANY),
        scratch_shapes=[pltpu.VMEM((CELLS, n_heads * CELLS), F32)]
        + layer_scratch(n_heads, n_feat)
        + [
            pltpu.VMEM((groups * 2 * CELLS, n_heads * CELLS), BF16),
            pltpu.VMEM((2 * columns, 104, 128), BF16),
            pltpu.VMEM((devices // 8, 104, 128), BF16),
            pltpu.SemaphoreType.DMA((2 * columns,)),
            pltpu.SemaphoreType.DMA((8,)),
        ],
        compiler_params=pltpu.CompilerParams(vmem_limit_bytes=VMEM_BYTES),
        cost_estimate=pl.CostEstimate(flops=2 * 10**9, bytes_accessed=6 * 10**6, transcendentals=10**6),
        name="first_layer",
    )(targets, slots, temper, embedded, token, *consts, *params)


def second_kernel(
    groups,
    place, temper, mid0_ref, mid1_ref, below_ref, right_ref, corner_ref,
    coords_ref, heads_ref, ones_ref, mask_ref,
    net_in, net_first, net_out, qkv_ref, proj_ref, up_ref, down_ref, gain_ref,
    out_ref, rows_ref, side_ref,
    bias_ref, strips_ref, q_w, k_w, v_w, ext, ring, p_ref, sems,
):
    step = pl.program_id(0)
    n_heads, n_feat = mask_ref.shape
    n_half = mid0_ref.shape[0]
    row, col, last_row, last_col = place[0], place[1], place[2], place[3]
    width = HALF * n_feat

    @pl.when(step == 0)
    def _():
        own = pl.ds(0, n_half)
        copies = [
            pltpu.make_async_copy(src, dst, sems.at[n])
            for n, (src, dst) in enumerate(
                [
                    (mid0_ref, ext.at[0, own]),
                    (mid1_ref, ext.at[1, own]),
                    (right_ref.at[pl.ds(0, 32)], ext.at[0, n_half]),
                    (right_ref.at[pl.ds(32, 32)], ext.at[1, n_half]),
                    (below_ref, ring.at[own]),
                    (corner_ref.at[pl.ds(64, 16)], ring.at[n_half]),
                ]
            )
        ]
        for copy in copies:
            copy.start()
        out_ref[:, :width] = jnp.zeros((2 * WIN, width), BF16)
        split_weights(qkv_ref, q_w, k_w, v_w)
        bias_strips(coords_ref, net_in, net_first[1:2, :], net_out[:, 1, :], strips_ref)
        strips = [turned(strips_ref[h]) for h in range(n_heads)]
        lane = lax.broadcasted_iota(jnp.int32, (WIN, n_heads * CELLS), 1)
        upper = lax.broadcasted_iota(jnp.int32, (WIN, n_heads * CELLS), 0) < HALF
        other_rows = upper != (lane % WIN < HALF)
        for w in range(WIN):
            other_cols = (lane % CELLS >= CELLS // 2) != (w >= HALF)
            rows = slice(w * WIN, (w + 1) * WIN)
            bias = bias_rows(strips, w)
            away = -100.0 * LOG2E
            bias_ref[0, rows, :] = bias
            bias_ref[1, rows, :] = bias + jnp.where(other_cols, away, 0.0)
            bias_ref[2, rows, :] = bias + jnp.where(other_rows, away, 0.0)
            bias_ref[3, rows, :] = bias + jnp.where(other_rows | other_cols, away, 0.0)
        for copy in copies:
            copy.wait()

    upper = lax.broadcasted_iota(jnp.int32, (CELLS, n_feat), 0) % WIN < HALF
    tiles = []
    for group in range(groups):
        at = 2 * (step * groups + group) + 1
        zero = jnp.concatenate([ext[0, at], ext[0, at + 1]], 0)
        one = jnp.concatenate([ext[1, at], ext[1, at + 1]], 0)
        two = jnp.concatenate([whole_rows(ring[at + half].astype(F32)) for half in range(2)], 0)
        tiles += [jnp.where(upper, one, zero), jnp.where(upper, two.astype(BF16), one)]
    x = jnp.concatenate(tiles, 0)
    low_cut = (row == last_row).astype(jnp.int32)

    def bias_of(n):
        column = step * groups + n // 2
        cut = ((col == last_col) & (column == n_half // 2 - 1)).astype(jnp.int32)
        return bias_ref[cut + 2 * low_cut * (n % 2)]

    mixed = attend(
        x, q_w, k_w, v_w, temper_row(temper, 1, mask_ref), heads_ref, ones_ref, mask_ref, bias_of, p_ref
    )
    y = dense_tail(x.astype(F32), mixed, proj_ref, up_ref, down_ref, gain_ref).astype(F32)

    for group in range(groups):
        first = y[2 * group * CELLS : (2 * group + 1) * CELLS]
        second = y[(2 * group + 1) * CELLS : (2 * group + 2) * CELLS]
        zero = jnp.where(upper, second, first)
        one = jnp.where(upper, first, second)
        for half in range(2):
            slabs = []
            for w in range(half * HALF, (half + 1) * HALF):
                rows = slice(w * WIN, (w + 1) * WIN)
                slabs.append(jnp.concatenate([zero[rows], one[rows]], 0))
            strip = jnp.concatenate(slabs, 1).astype(BF16)
            at = 2 * (step * groups + group) + 1 + half
            if half == 0 or group < groups - 1:
                out_ref[:, pl.ds(pl.multiple_of(at * width, 128), width)] = strip
            else:

                @pl.when(at < n_half)
                def _(at=at, strip=strip):
                    out_ref[:, pl.ds(pl.multiple_of(at * width, 128), width)] = strip

                @pl.when(at == n_half)
                def _(strip=strip):
                    side_ref[...] = strip

    @pl.when(step == pl.num_programs(0) - 1)
    def _():
        quarter = rows_ref.shape[1]
        first = lax.broadcasted_iota(jnp.int32, (WIN, quarter), 0) < HALF
        tops = [out_ref[:, n * quarter : (n + 1) * quarter][:WIN].astype(F32) for n in range(4)]
        pairs = [
            jnp.where(first, tops[2 * n], pltpu.roll(tops[2 * n + 1], HALF, 0)) for n in range(2)
        ]
        rows_ref[...] = jnp.concatenate(pairs, 0).astype(BF16)


def second_layer(place, temper, pieces, consts, params, groups=8):
    n_heads, n_feat = consts[3].shape
    n_half = pieces[0].shape[0]
    out = jax.ShapeDtypeStruct((2 * WIN, n_half * HALF * n_feat), BF16)
    rows = jax.ShapeDtypeStruct((2 * WIN, n_half * n_feat), BF16)
    side = jax.ShapeDtypeStruct((2 * WIN, HALF * n_feat), BF16)
    return pl.pallas_call(
        functools.partial(second_kernel, groups),
        grid=(n_half // 2 // groups,),
        out_shape=(out, rows, side),
        in_specs=[SMEM, SMEM]
        + [ANY] * len(pieces)
        + [whole(a) for a in consts]
        + [layer_spec(a, n, 1) for n, a in enumerate(params)],
        out_specs=(whole(out), whole(rows), whole(side)),
        scratch_shapes=[pltpu.VMEM((4, CELLS, n_heads * CELLS), F32)]
        + layer_scratch(n_heads, n_feat)
        + [
            pltpu.VMEM((2, n_half + 1, 32, n_feat), BF16),
            pltpu.VMEM((n_half + 1, 16, n_feat), BF16),
            pltpu.VMEM((groups * 2 * CELLS, n_heads * CELLS), BF16),
            pltpu.SemaphoreType.DMA((6,)),
        ],
        compiler_params=pltpu.CompilerParams(vmem_limit_bytes=VMEM_BYTES),
        cost_estimate=pl.CostEstimate(flops=10**11, bytes_accessed=10**7, transcendentals=10**6),
        name="second_layer",
    )(place, temper, *pieces, *consts, *params)


def merge_features(own_ref, rows_ref, side_ref, corner_ref, out_ref):
    quarter, width = rows_ref.shape[1], side_ref.shape[1]
    first = lax.broadcasted_iota(jnp.int32, (WIN, quarter), 0) < HALF
    for n in range(4):
        lanes = slice(n * quarter, (n + 1) * quarter)
        own = own_ref[:, lanes].astype(F32)
        top = rows_ref[...].astype(F32)[n // 2 * WIN : (n // 2 + 1) * WIN]
        top = pltpu.roll(top, HALF, 0) if n % 2 else top
        merged = jnp.concatenate([jnp.where(first, top, own[:WIN]), own[WIN:]], 0)
        out_ref[:, lanes] = merged.astype(BF16)
    corner = lax.broadcasted_iota(jnp.int32, (2 * WIN, width), 0) < HALF
    merged = jnp.where(corner, corner_ref[...].astype(F32), side_ref[...].astype(F32))
    out_ref[:, :width] = merged.astype(BF16)


def last_kernel(
    entries_ref, own_ref, rows_ref, side_ref, corner_ref, features_ref, packed_ref, arrived_ref, sems
):
    slots = packed_ref.shape[0]
    part = arrived_ref.shape[0] // 8
    copies = [
        pltpu.make_async_copy(
            entries_ref.at[pl.ds(n * part, part)], arrived_ref.at[pl.ds(n * part, part)], sems.at[n]
        )
        for n in range(8)
    ]
    for copy in copies:
        copy.start()
    merge_features(own_ref, rows_ref, side_ref, corner_ref, features_ref)
    for copy in copies:
        copy.wait()
    marks = arrived_ref[:, 96:, :].astype(F32)
    lane = lax.broadcasted_iota(jnp.int32, marks.shape, 2).astype(F32)
    sender = lax.broadcasted_iota(jnp.int32, marks.shape, 0).astype(F32)
    found = jnp.max(jnp.where(marks == lane, sender, 0.0), 0).astype(jnp.int32)
    sources = [found[0, slot] for slot in range(slots)]
    lane = lax.broadcasted_iota(jnp.int32, (slots, 128), 1)

    def rows_of(at):
        rows = [arrived_ref[source, at : at + WIN, :].astype(F32) for source in sources]
        return jnp.swapaxes(jnp.stack(rows, 0), 0, 1)

    for pair in range(WIN // 2):
        even = rows_of(2 * pair * WIN)
        odd = rows_of((2 * pair + 1) * WIN)
        tails = rows_of(CELLS + pair * WIN)
        for u in range(WIN):
            moved = pltpu.roll(odd[u], 64, 1)
            joined = [
                even[u],
                jnp.where(lane < 64, tails[u], moved),
                jnp.where(lane < 64, moved, tails[u]),
            ]
            at = (u * WIN + 2 * pair) * 192
            packed_ref[:, at : at + 384] = jnp.concatenate(joined, 1).astype(BF16)


def last_steps(arrived, own, rows, side, corner, slots, width):
    return pl.pallas_call(
        last_kernel,
        out_shape=(jax.ShapeDtypeStruct(own.shape, BF16), jax.ShapeDtypeStruct((slots, width), BF16)),
        in_specs=[HBM] + [pl.BlockSpec(memory_space=pltpu.VMEM)] * 4,
        out_specs=(pl.BlockSpec(memory_space=pltpu.VMEM),) * 2,
        scratch_shapes=[pltpu.VMEM(arrived.shape, BF16), pltpu.SemaphoreType.DMA((8,))],
        compiler_params=pltpu.CompilerParams(vmem_limit_bytes=VMEM_BYTES),
        name="last_steps",
    )(arrived, own, rows, side, corner)


def moved(block, rows, cols):
    n_row, n_col = lax.axis_size("row"), lax.axis_size("col")
    route = [
        (r * n_col + c, (r + rows) % n_row * n_col + (c + cols) % n_col)
        for r in range(n_row)
        for c in range(n_col)
    ]
    return lax.ppermute(block, ("row", "col"), route)


def local(
    embedded,
    window_target_device,
    window_device_slot,
    cloud_mask_token,
    query_key_value_weight,
    projection_weight,
    up_weight,
    down_weight,
    bias_net_input_weight,
    bias_net_first_bias,
    bias_net_output_weight,
    temper,
    norm_gain_values,
):
    n_row, n_col = lax.axis_size("row"), lax.axis_size("col")
    n_heads, n_feat = temper.shape[1], cloud_mask_token.shape[0]
    slots = window_target_device.size // 2
    row, col = lax.axis_index("row"), lax.axis_index("col")
    place = jnp.stack([row, col, n_row - 1, n_col - 1]).astype(jnp.int32)
    consts = constants(n_heads, n_feat)
    params = (
        bias_net_input_weight,
        bias_net_first_bias,
        jnp.transpose(bias_net_output_weight, (2, 0, 1)),
        query_key_value_weight,
        projection_weight,
        up_weight,
        jnp.swapaxes(down_weight, 1, 2),
        norm_gain_values,
    )
    mid0, mid1, upper, left, send = first_layer(
        embedded, window_target_device, window_device_slot, temper, cloud_mask_token, consts, params,
        n_row * n_col,
    )
    pieces = (mid0, mid1, moved(upper, -1, 0), moved(left, 0, -1), moved(left, -1, -1))
    arrived = lax.all_to_all(send, ("row", "col"), split_axis=0, concat_axis=0, tiled=True)
    own, rows, side = second_layer(place, temper, pieces, consts, params)
    return last_steps(
        arrived, own, moved(rows, 1, 0), moved(side, 0, 1), moved(side, 1, 1), slots, CELLS * n_feat
    )


def solution(mesh):
    in_specs = (P("row", "col"),) * 3 + (P(),) * 10
    out_specs = (P("row", "col"), P(("row", "col"), None))
    return jax.shard_map(local, mesh=mesh, in_specs=in_specs, out_specs=out_specs, check_vma=False)
```

```python
import functools
import math

import jax
import jax.numpy as jnp
import numpy as np
from jax import lax
from jax.experimental import pallas as pl
from jax.experimental.pallas import tpu as pltpu
from jax.sharding import PartitionSpec as P

WIN = 8
HALF = WIN // 2
CELLS = WIN * WIN
LOG2E = math.log2(math.e)
F32 = jnp.float32
BF16 = jnp.bfloat16
VMEM_BYTES = 60 * 2**20
LAST_BYTES = 62 * 2**20
SMEM = pl.BlockSpec(memory_space=pltpu.SMEM)
ANY = pl.BlockSpec(memory_space=pl.ANY)


def log_step(offset):
    scaled = np.abs(offset).astype(np.float32) * np.float32(8.0 / (WIN - 1))
    return np.sign(offset) * np.log2(scaled + 1.0) / 3.0


def offset_coords():
    lane = np.arange(128)
    across = np.maximum(WIN - 1 - lane // WIN, 1 - WIN)
    down = np.concatenate([-(lane % WIN), np.minimum(WIN - lane % WIN, WIN - 1)])
    return np.stack([log_step(down), log_step(np.tile(across, 2))], 1).astype(np.float32)


def head_blocks(rows, row_block, cols, col_block):
    same = (np.arange(rows) // row_block)[:, None] == (np.arange(cols) // col_block)[None, :]
    return same.astype(np.float32)


def constants(n_heads, n_feat):
    per_head = n_feat // n_heads
    return (
        jnp.asarray(offset_coords(), F32),
        jnp.asarray(head_blocks(n_feat, per_head, n_feat, per_head), BF16),
        jnp.asarray(head_blocks(n_heads * CELLS, CELLS, n_feat, per_head), BF16),
        jnp.asarray(head_blocks(n_heads, 1, n_feat, per_head), BF16),
    )


def dot(a, b):
    return jnp.dot(a, b, preferred_element_type=F32)


def dot_nt(a, b):
    return lax.dot_general(a, b, (((1,), (1,)), ((), ())), preferred_element_type=F32)


def bias_strips(coords_ref, net_in, net_first, net_out, strips_ref):
    coords = coords_ref[...]
    units = jnp.maximum(
        coords[:, 0:1] * net_in[0:1, :] + coords[:, 1:2] * net_in[1:2, :] + net_first, 0.0
    )
    logits = lax.dot_general(
        net_out, units, (((1,), (1,)), ((), ())),
        precision=lax.Precision.HIGHEST, preferred_element_type=F32,
    )
    n_heads = logits.shape[0]
    logits = jnp.concatenate([logits, jnp.zeros((8 - n_heads, 256), F32)], 0)
    table = 16.0 * LOG2E / (1.0 + jnp.exp(-logits))
    before, after = table[:, :128], table[:, 128:]
    cell = lax.broadcasted_iota(jnp.int32, (8, 128), 1) % WIN
    for u in range(WIN):
        strip = jnp.where(
            cell >= u,
            pltpu.roll(before, u, 1) if u else before,
            pltpu.roll(after, (u - WIN) % 128, 1),
        )
        strips_ref[:, u, :] = strip


def turned(strip):
    cell = lax.broadcasted_iota(jnp.int32, (WIN, 128), 1) % WIN
    strip = pltpu.roll(strip, HALF, 0)
    return jnp.where(cell < HALF, pltpu.roll(strip, 128 - HALF, 1), pltpu.roll(strip, HALF, 1))


def bias_rows(strips, w):
    lane = lax.broadcasted_iota(jnp.int32, (WIN, 128), 1)
    back = (WIN - 1 - w) * WIN
    parts = []
    for pair in range(len(strips) // 2):
        low = pltpu.roll(strips[2 * pair], (128 - back) % 128, 1)
        high = pltpu.roll(strips[2 * pair + 1], (192 - back) % 128, 1)
        parts.append(jnp.where(lane < CELLS, low, high))
    return jnp.concatenate(parts, 1)


def layer_norm(values, gain_row):
    row_mean = jnp.mean(values, -1, keepdims=True)
    centred = values - row_mean
    spread = jnp.mean(centred * centred, -1, keepdims=True)
    return centred * lax.rsqrt(spread + 1e-05) * gain_row


def unit_vectors(t, heads_ref):
    t = t.astype(BF16).astype(F32)
    squares = dot((t * t).astype(BF16), heads_ref[...])
    return t * lax.rsqrt(squares + 1e-06)


def temper_row(temper, layer, mask_ref):
    row = jnp.zeros((1, mask_ref.shape[1]), F32)
    for h in range(mask_ref.shape[0]):
        row = row + (temper[layer, h] * LOG2E) * mask_ref[h : h + 1, :].astype(F32)
    return row


def spread_heads(t, mask_ref):
    low = [t[:, :128] * mask_ref[h : h + 1, :128] for h in range(4)]
    high = [t[:, 128:] * mask_ref[h : h + 1, 128:] for h in range(4, 6)]
    return jnp.concatenate(low, 0), jnp.concatenate(high, 0)


def scores_of(q, k, mask_ref):
    low, high = spread_heads(k, mask_ref)
    return jnp.concatenate([dot_nt(q[:, :128], low), dot_nt(q[:, 128:], high)], 1)


def weighted(p, low, high):
    return jnp.concatenate([dot(p[:, :256], low), dot(p[:, 256:], high)], 1)


def totals_of(p, ones_ref):
    return weighted(p, ones_ref[:256, :128], ones_ref[256:, 128:])


def dense_tail(x, mixed, proj_ref, up_ref, down_ref, gain_ref):
    attended = dot(mixed.astype(BF16), proj_ref[...])
    hidden = (x + layer_norm(attended, gain_ref[0:1, :])).astype(BF16)
    raised = dot(hidden, up_ref[...])
    expanded = (0.5 * raised * (1.0 + lax.erf(raised * math.sqrt(0.5)))).astype(BF16)
    reduced = dot_nt(expanded, down_ref[...])
    return (hidden.astype(F32) + layer_norm(reduced, gain_ref[1:2, :])).astype(BF16)


def attend(x, q_w, k_w, v_w, temper, heads_ref, ones_ref, mask_ref, bias_of, p_ref):
    n_windows = x.shape[0] // CELLS
    q = (unit_vectors(dot(x, q_w[...]), heads_ref) * temper).astype(BF16)
    k = unit_vectors(dot(x, k_w[...]), heads_ref).astype(BF16)
    v = dot(x, v_w[...]).astype(BF16)
    mixed = []
    for n in range(n_windows):
        rows = slice(n * CELLS, (n + 1) * CELLS)
        p_ref[rows, :] = jnp.exp2(scores_of(q[rows], k[rows], mask_ref) + bias_of(n)).astype(BF16)
    for n in range(n_windows):
        rows = slice(n * CELLS, (n + 1) * CELLS)
        mixed.append(weighted(p_ref[rows, :], *spread_heads(v[rows], mask_ref)))
    return jnp.concatenate(mixed, 0) / totals_of(p_ref[...], ones_ref)


def split_weights(qkv_ref, q_w, k_w, v_w):
    n_feat = q_w.shape[0]
    q_w[...] = qkv_ref[:, :n_feat]
    k_w[...] = qkv_ref[:, n_feat : 2 * n_feat]
    v_w[...] = qkv_ref[:, 2 * n_feat :]


def half_rows(tile):
    first = lax.broadcasted_iota(jnp.int32, (WIN, tile.shape[1]), 0) < HALF
    pairs = []
    for pair in range(2):
        even = tile[2 * pair * WIN : (2 * pair + 1) * WIN]
        odd = tile[(2 * pair + 1) * WIN : (2 * pair + 2) * WIN]
        pairs.append(jnp.where(first, even, pltpu.roll(odd, HALF, 0)))
    return jnp.concatenate(pairs, 0)


def whole_rows(halves):
    tiles = []
    for pair in range(2):
        rows = halves[pair * WIN : (pair + 1) * WIN]
        tiles += [rows, pltpu.roll(rows, HALF, 0)]
    return jnp.concatenate(tiles, 0)


def first_kernel(
    groups,
    targets, slots, temper, emb_ref, token_ref, coords_ref, heads_ref, ones_ref, mask_ref,
    net_in, net_first, net_out, qkv_ref, proj_ref, up_ref, down_ref, gain_ref,
    mid0_ref, mid1_ref, upper_ref, left_ref, send_ref,
    bias_ref, strips_ref, q_w, k_w, v_w, p_ref, staging, blank, sems, blank_sem,
):
    step = pl.program_id(0)
    n_heads, n_feat = mask_ref.shape

    no_slots = pltpu.make_async_copy(blank, send_ref.at[:, pl.ds(96, 8)], blank_sem)

    @pl.when(step == 0)
    def _():
        blank[...] = jnp.full(blank.shape, -1.0, BF16)
        no_slots.start()
        bias_strips(coords_ref, net_in, net_first[0:1, :], net_out[:, 0, :], strips_ref)
        strips = [strips_ref[h] for h in range(n_heads)]
        for w in range(WIN):
            bias_ref[w * WIN : (w + 1) * WIN, :] = bias_rows(strips, w)
        split_weights(qkv_ref, q_w, k_w, v_w)

    tiles = []
    for group in range(groups):
        slabs = []
        for w in range(WIN):
            at = (group * WIN + w) * n_feat
            slabs.append(emb_ref[:, at : at + n_feat].astype(F32))
        for i in range(2):
            tiles.append(jnp.concatenate([s[i * WIN : (i + 1) * WIN] for s in slabs], 0))
    x = jnp.concatenate(tiles, 0)
    mixed = attend(
        x.astype(BF16), q_w, k_w, v_w, temper_row(temper, 0, mask_ref), heads_ref, ones_ref, mask_ref,
        lambda n: bias_ref[...], p_ref,
    )

    @pl.when(step == 0)
    def _():
        no_slots.wait()

    y = jnp.concatenate(
        [
            dense_tail(x[n : n + 256], mixed[n : n + 256], proj_ref, up_ref, down_ref, gain_ref)
            for n in range(0, x.shape[0], 256)
        ],
        0,
    ).astype(F32)

    token = token_ref[...].astype(F32).reshape(1, n_feat)
    for group in range(groups):
        for i in range(2):
            n = 2 * group + i
            j = step * groups + group
            target = targets[i, j]
            tile = y[n * CELLS : (n + 1) * CELLS]
            kept = jnp.where(target >= 0, tile, token)
            rows = kept.astype(BF16)
            mid = (mid0_ref, mid1_ref)[i]
            mid[2 * group] = rows[:32]
            mid[2 * group + 1] = rows[32:]
            if i == 0:
                halves = [half_rows(kept[half * 32 : (half + 1) * 32]).astype(BF16) for half in range(2)]
                upper_ref[2 * group] = halves[0]
                upper_ref[2 * group + 1] = halves[1]
            if group == 0:

                @pl.when(step == 0)
                def _(i=i, rows=rows, halves=halves):
                    left_ref[i * 32 : (i + 1) * 32] = rows[:32]
                    if i == 0:
                        left_ref[64:] = halves[0]

            slot = j * 2 + i
            staging[slot, :64] = tile[:, :128].astype(BF16)
            tails = tile[:, 128:].reshape(4, 2, WIN, 64)
            joined = jnp.concatenate([tails[:, 0], tails[:, 1]], -1)
            staging[slot, 64:96] = joined.reshape(32, 128).astype(BF16)
            staging[slot, 96:] = jnp.full((8, 128), slots[i, j].astype(F32)).astype(BF16)

            @pl.when(target >= 0)
            def _(slot=slot, target=target):
                pltpu.make_async_copy(staging.at[slot], send_ref.at[target], sems.at[slot]).start()

    @pl.when(step == pl.num_programs(0) - 1)
    def _():
        def finish(slot, carry):
            target = targets[lax.rem(slot, 2), slot // 2]

            @pl.when(target >= 0)
            def _():
                pltpu.make_async_copy(staging.at[slot], send_ref.at[target], sems.at[slot]).wait()

            return carry

        lax.fori_loop(0, staging.shape[0], finish, 0)


def whole(array):
    zeros = (0,) * array.ndim
    return pl.BlockSpec(array.shape, lambda *_: zeros)


def layer_spec(array, position, layer):
    if position in (1, 2):
        return whole(array)
    rest = array.shape[1:]
    at = (layer,) + (0,) * len(rest)
    return pl.BlockSpec((None,) + rest, lambda *_: at)


def layer_scratch(n_heads, n_feat):
    square = pltpu.VMEM((n_feat, n_feat), BF16)
    return [pltpu.VMEM((8, WIN, 128), F32), square, square, square]


def first_layer(embedded, targets, slots, temper, token, consts, params, devices, groups=16):
    n_heads, n_feat = consts[3].shape
    columns = embedded.shape[1] // (WIN * n_feat)
    side = jax.ShapeDtypeStruct((80, n_feat), BF16)
    upper = jax.ShapeDtypeStruct((2 * columns, 16, n_feat), BF16)
    mid = jax.ShapeDtypeStruct((2 * columns, 32, n_feat), BF16)
    mid_spec = pl.BlockSpec((2 * groups, 32, n_feat), lambda g: (g, 0, 0))
    return pl.pallas_call(
        functools.partial(first_kernel, groups),
        grid=(columns // groups,),
        out_shape=(mid, mid, upper, side, jax.ShapeDtypeStruct((devices, 104, 128), BF16)),
        in_specs=[SMEM, SMEM, SMEM, pl.BlockSpec((2 * WIN, groups * WIN * n_feat), lambda g: (0, g))]
        + [whole(a) for a in (token,) + consts]
        + [layer_spec(a, n, 0) for n, a in enumerate(params)],
        out_specs=(mid_spec, mid_spec, pl.BlockSpec((2 * groups, 16, n_feat), lambda g: (g, 0, 0)), whole(side), ANY),
        scratch_shapes=[pltpu.VMEM((CELLS, n_heads * CELLS), F32)]
        + layer_scratch(n_heads, n_feat)
        + [
            pltpu.VMEM((groups * 2 * CELLS, n_heads * CELLS), BF16),
            pltpu.VMEM((2 * columns, 104, 128), BF16),
            pltpu.VMEM((devices, 8, 128), BF16),
            pltpu.SemaphoreType.DMA((2 * columns,)),
            pltpu.SemaphoreType.DMA,
        ],
        compiler_params=pltpu.CompilerParams(vmem_limit_bytes=VMEM_BYTES),
        cost_estimate=pl.CostEstimate(flops=2 * 10**9, bytes_accessed=6 * 10**6, transcendentals=10**6),
        name="first_layer",
    )(targets, slots, temper, embedded, token, *consts, *params)


def second_kernel(
    groups,
    place, temper, mid0_ref, mid1_ref, below_ref, right_ref, corner_ref,
    coords_ref, heads_ref, ones_ref, mask_ref,
    net_in, net_first, net_out, qkv_ref, proj_ref, up_ref, down_ref, gain_ref,
    out_ref, rows_ref, side_ref,
    bias_ref, strips_ref, q_w, k_w, v_w, ext, ring, p_ref, sems,
):
    step = pl.program_id(0)
    n_heads, n_feat = mask_ref.shape
    n_half = mid0_ref.shape[0]
    row, col, last_row, last_col = place[0], place[1], place[2], place[3]
    width = HALF * n_feat

    @pl.when(step == 0)
    def _():
        own = pl.ds(0, n_half)
        copies = [
            pltpu.make_async_copy(src, dst, sems.at[n])
            for n, (src, dst) in enumerate(
                [
                    (mid0_ref, ext.at[0, own]),
                    (mid1_ref, ext.at[1, own]),
                    (right_ref.at[pl.ds(0, 32)], ext.at[0, n_half]),
                    (right_ref.at[pl.ds(32, 32)], ext.at[1, n_half]),
                    (below_ref, ring.at[own]),
                    (corner_ref.at[pl.ds(64, 16)], ring.at[n_half]),
                ]
            )
        ]
        for copy in copies:
            copy.start()
        out_ref[:, :width] = jnp.zeros((2 * WIN, width), BF16)
        split_weights(qkv_ref, q_w, k_w, v_w)
        bias_strips(coords_ref, net_in, net_first[1:2, :], net_out[:, 1, :], strips_ref)
        strips = [turned(strips_ref[h]) for h in range(n_heads)]
        lane = lax.broadcasted_iota(jnp.int32, (WIN, n_heads * CELLS), 1)
        upper = lax.broadcasted_iota(jnp.int32, (WIN, n_heads * CELLS), 0) < HALF
        other_rows = upper != (lane % WIN < HALF)
        for w in range(WIN):
            other_cols = (lane % CELLS >= CELLS // 2) != (w >= HALF)
            rows = slice(w * WIN, (w + 1) * WIN)
            bias = bias_rows(strips, w)
            away = -100.0 * LOG2E
            bias_ref[0, rows, :] = bias
            bias_ref[1, rows, :] = bias + jnp.where(other_cols, away, 0.0)
            bias_ref[2, rows, :] = bias + jnp.where(other_rows, away, 0.0)
            bias_ref[3, rows, :] = bias + jnp.where(other_rows | other_cols, away, 0.0)
        for copy in copies:
            copy.wait()

    upper = lax.broadcasted_iota(jnp.int32, (CELLS, n_feat), 0) % WIN < HALF
    tiles = []
    for group in range(groups):
        at = 2 * (step * groups + group) + 1
        zero = jnp.concatenate([ext[0, at], ext[0, at + 1]], 0)
        one = jnp.concatenate([ext[1, at], ext[1, at + 1]], 0)
        two = jnp.concatenate([whole_rows(ring[at + half].astype(F32)) for half in range(2)], 0)
        tiles += [jnp.where(upper, one, zero), jnp.where(upper, two.astype(BF16), one)]
    x = jnp.concatenate(tiles, 0)
    low_cut = (row == last_row).astype(jnp.int32)

    def bias_of(n):
        column = step * groups + n // 2
        cut = ((col == last_col) & (column == n_half // 2 - 1)).astype(jnp.int32)
        return bias_ref[cut + 2 * low_cut * (n % 2)]

    mixed = attend(
        x, q_w, k_w, v_w, temper_row(temper, 1, mask_ref), heads_ref, ones_ref, mask_ref, bias_of, p_ref
    )
    y = dense_tail(x.astype(F32), mixed, proj_ref, up_ref, down_ref, gain_ref).astype(F32)

    for group in range(groups):
        first = y[2 * group * CELLS : (2 * group + 1) * CELLS]
        second = y[(2 * group + 1) * CELLS : (2 * group + 2) * CELLS]
        zero = jnp.where(upper, second, first)
        one = jnp.where(upper, first, second)
        for half in range(2):
            slabs = []
            for w in range(half * HALF, (half + 1) * HALF):
                rows = slice(w * WIN, (w + 1) * WIN)
                slabs.append(jnp.concatenate([zero[rows], one[rows]], 0))
            strip = jnp.concatenate(slabs, 1).astype(BF16)
            at = 2 * (step * groups + group) + 1 + half
            if half == 0 or group < groups - 1:
                out_ref[:, pl.ds(pl.multiple_of(at * width, 128), width)] = strip
            else:

                @pl.when(at < n_half)
                def _(at=at, strip=strip):
                    out_ref[:, pl.ds(pl.multiple_of(at * width, 128), width)] = strip

                @pl.when(at == n_half)
                def _(strip=strip):
                    side_ref[...] = strip

    @pl.when(step == pl.num_programs(0) - 1)
    def _():
        quarter = rows_ref.shape[1]
        first = lax.broadcasted_iota(jnp.int32, (WIN, quarter), 0) < HALF
        tops = [out_ref[:, n * quarter : (n + 1) * quarter][:WIN].astype(F32) for n in range(4)]
        pairs = [
            jnp.where(first, tops[2 * n], pltpu.roll(tops[2 * n + 1], HALF, 0)) for n in range(2)
        ]
        rows_ref[...] = jnp.concatenate(pairs, 0).astype(BF16)


def second_layer(place, temper, pieces, consts, params, groups=8):
    n_heads, n_feat = consts[3].shape
    n_half = pieces[0].shape[0]
    out = jax.ShapeDtypeStruct((2 * WIN, n_half * HALF * n_feat), BF16)
    rows = jax.ShapeDtypeStruct((2 * WIN, n_half * n_feat), BF16)
    side = jax.ShapeDtypeStruct((2 * WIN, HALF * n_feat), BF16)
    return pl.pallas_call(
        functools.partial(second_kernel, groups),
        grid=(n_half // 2 // groups,),
        out_shape=(out, rows, side),
        in_specs=[SMEM, SMEM]
        + [ANY] * len(pieces)
        + [whole(a) for a in consts]
        + [layer_spec(a, n, 1) for n, a in enumerate(params)],
        out_specs=(whole(out), whole(rows), whole(side)),
        scratch_shapes=[pltpu.VMEM((4, CELLS, n_heads * CELLS), F32)]
        + layer_scratch(n_heads, n_feat)
        + [
            pltpu.VMEM((2, n_half + 1, 32, n_feat), BF16),
            pltpu.VMEM((n_half + 1, 16, n_feat), BF16),
            pltpu.VMEM((groups * 2 * CELLS, n_heads * CELLS), BF16),
            pltpu.SemaphoreType.DMA((6,)),
        ],
        compiler_params=pltpu.CompilerParams(vmem_limit_bytes=VMEM_BYTES),
        cost_estimate=pl.CostEstimate(flops=10**11, bytes_accessed=10**7, transcendentals=10**6),
        name="second_layer",
    )(place, temper, *pieces, *consts, *params)


def merge_features(own_ref, rows_ref, side_ref, corner_ref, out_ref):
    quarter, width = rows_ref.shape[1], side_ref.shape[1]
    first = lax.broadcasted_iota(jnp.int32, (WIN, quarter), 0) < HALF
    for n in range(4):
        lanes = slice(n * quarter, (n + 1) * quarter)
        own = own_ref[:, lanes].astype(F32)
        top = rows_ref[...].astype(F32)[n // 2 * WIN : (n // 2 + 1) * WIN]
        top = pltpu.roll(top, HALF, 0) if n % 2 else top
        merged = jnp.concatenate([jnp.where(first, top, own[:WIN]), own[WIN:]], 0)
        out_ref[:, lanes] = merged.astype(BF16)
    corner = lax.broadcasted_iota(jnp.int32, (2 * WIN, width), 0) < HALF
    merged = jnp.where(corner, corner_ref[...].astype(F32), side_ref[...].astype(F32))
    out_ref[:, :width] = merged.astype(BF16)


def last_kernel(
    entries_ref, own_hbm, rows_ref, side_ref, corner_ref, features_ref, packed_ref,
    marks_ref, held, own_ref, sems, slot_sems,
):
    slots = packed_ref.shape[0]
    marks_copy = pltpu.make_async_copy(entries_ref.at[:, pl.ds(96, 8)], marks_ref, sems.at[0])
    own_copy = pltpu.make_async_copy(own_hbm, own_ref, sems.at[1])
    marks_copy.start()
    own_copy.start()
    marks_copy.wait()
    marks = marks_ref[...].astype(F32)
    lane = lax.broadcasted_iota(jnp.int32, marks.shape, 2).astype(F32)
    sender = lax.broadcasted_iota(jnp.int32, marks.shape, 0).astype(F32)
    found = jnp.max(jnp.where(marks == lane, sender, 0.0), 0).astype(jnp.int32)
    windows = [
        pltpu.make_async_copy(entries_ref.at[found[0, slot]], held.at[slot], slot_sems.at[slot])
        for slot in range(slots)
    ]
    for copy in windows:
        copy.start()
    own_copy.wait()
    merge_features(own_ref, rows_ref, side_ref, corner_ref, features_ref)
    for copy in windows:
        copy.wait()
    lane = lax.broadcasted_iota(jnp.int32, (slots, 128), 1)

    def rows_of(at):
        return jnp.swapaxes(held[:, at : at + WIN, :].astype(F32), 0, 1)

    for pair in range(WIN // 2):
        even = rows_of(2 * pair * WIN)
        odd = rows_of((2 * pair + 1) * WIN)
        tails = rows_of(CELLS + pair * WIN)
        for u in range(WIN):
            moved = pltpu.roll(odd[u], 64, 1)
            joined = [
                even[u],
                jnp.where(lane < 64, tails[u], moved),
                jnp.where(lane < 64, moved, tails[u]),
            ]
            at = (u * WIN + 2 * pair) * 192
            packed_ref[:, at : at + 384] = jnp.concatenate(joined, 1).astype(BF16)


def last_steps(arrived, own, rows, side, corner, slots, width):
    return pl.pallas_call(
        last_kernel,
        out_shape=(jax.ShapeDtypeStruct(own.shape, BF16), jax.ShapeDtypeStruct((slots, width), BF16)),
        in_specs=[ANY, ANY] + [pl.BlockSpec(memory_space=pltpu.VMEM)] * 3,
        out_specs=(pl.BlockSpec(memory_space=pltpu.VMEM),) * 2,
        scratch_shapes=[
            pltpu.VMEM((arrived.shape[0], 8, 128), BF16),
            pltpu.VMEM((slots,) + arrived.shape[1:], BF16),
        ]
        + [pltpu.VMEM(own.shape, BF16), pltpu.SemaphoreType.DMA((2,)), pltpu.SemaphoreType.DMA((slots,))],
        compiler_params=pltpu.CompilerParams(vmem_limit_bytes=LAST_BYTES),
        name="last_steps",
    )(arrived, own, rows, side, corner)


def moved(block, rows, cols):
    n_row, n_col = lax.axis_size("row"), lax.axis_size("col")
    route = [
        (r * n_col + c, (r + rows) % n_row * n_col + (c + cols) % n_col)
        for r in range(n_row)
        for c in range(n_col)
    ]
    return lax.ppermute(block, ("row", "col"), route)


def local(
    embedded,
    window_target_device,
    window_device_slot,
    cloud_mask_token,
    query_key_value_weight,
    projection_weight,
    up_weight,
    down_weight,
    bias_net_input_weight,
    bias_net_first_bias,
    bias_net_output_weight,
    temper,
    norm_gain_values,
):
    n_row, n_col = lax.axis_size("row"), lax.axis_size("col")
    n_heads, n_feat = temper.shape[1], cloud_mask_token.shape[0]
    slots = window_target_device.size // 2
    row, col = lax.axis_index("row"), lax.axis_index("col")
    place = jnp.stack([row, col, n_row - 1, n_col - 1]).astype(jnp.int32)
    consts = constants(n_heads, n_feat)
    params = (
        bias_net_input_weight,
        bias_net_first_bias,
        jnp.transpose(bias_net_output_weight, (2, 0, 1)),
        query_key_value_weight,
        projection_weight,
        up_weight,
        jnp.swapaxes(down_weight, 1, 2),
        norm_gain_values,
    )
    mid0, mid1, upper, left, send = first_layer(
        embedded, window_target_device, window_device_slot, temper, cloud_mask_token, consts, params,
        n_row * n_col,
    )
    pieces = (mid0, mid1, moved(upper, -1, 0), moved(left, 0, -1), moved(left, -1, -1))
    arrived = lax.all_to_all(send, ("row", "col"), split_axis=0, concat_axis=0, tiled=True)
    own, rows, side = second_layer(place, temper, pieces, consts, params)
    return last_steps(
        arrived, own, moved(rows, 1, 0), moved(side, 0, 1), moved(side, 1, 1), slots, CELLS * n_feat
    )


def solution(mesh):
    in_specs = (P("row", "col"),) * 3 + (P(),) * 10
    out_specs = (P("row", "col"), P(("row", "col"), None))
    return jax.shard_map(local, mesh=mesh, in_specs=in_specs, out_specs=out_specs, check_vma=False)
```

```python
import functools
import math

import jax
import jax.numpy as jnp
import numpy as np
from jax import lax
from jax.experimental import pallas as pl
from jax.experimental.pallas import tpu as pltpu
from jax.sharding import PartitionSpec as P

WIN = 8
HALF = WIN // 2
CELLS = WIN * WIN
LOG2E = math.log2(math.e)
F32 = jnp.float32
BF16 = jnp.bfloat16
VMEM_BYTES = 60 * 2**20
LAST_BYTES = 62 * 2**20
SMEM = pl.BlockSpec(memory_space=pltpu.SMEM)
ANY = pl.BlockSpec(memory_space=pl.ANY)


def log_step(offset):
    scaled = np.abs(offset).astype(np.float32) * np.float32(8.0 / (WIN - 1))
    return np.sign(offset) * np.log2(scaled + 1.0) / 3.0


def offset_coords():
    lane = np.arange(128)
    across = np.maximum(WIN - 1 - lane // WIN, 1 - WIN)
    down = np.concatenate([-(lane % WIN), np.minimum(WIN - lane % WIN, WIN - 1)])
    return np.stack([log_step(down), log_step(np.tile(across, 2))], 1).astype(np.float32)


def head_blocks(rows, row_block, cols, col_block):
    same = (np.arange(rows) // row_block)[:, None] == (np.arange(cols) // col_block)[None, :]
    return same.astype(np.float32)


def constants(n_heads, n_feat):
    per_head = n_feat // n_heads
    return (
        jnp.asarray(offset_coords(), F32),
        jnp.asarray(head_blocks(n_feat, per_head, n_feat, per_head), BF16),
        jnp.asarray(head_blocks(n_heads * CELLS, CELLS, n_feat, per_head), BF16),
        jnp.asarray(head_blocks(n_heads, 1, n_feat, per_head), BF16),
    )


def dot(a, b):
    return jnp.dot(a, b, preferred_element_type=F32)


def dot_nt(a, b):
    return lax.dot_general(a, b, (((1,), (1,)), ((), ())), preferred_element_type=F32)


def bias_strips(coords_ref, net_in, net_first, net_out, strips_ref):
    coords = coords_ref[...]
    units = jnp.maximum(
        coords[:, 0:1] * net_in[0:1, :] + coords[:, 1:2] * net_in[1:2, :] + net_first, 0.0
    )
    logits = lax.dot_general(
        net_out, units, (((1,), (1,)), ((), ())),
        precision=lax.Precision.HIGHEST, preferred_element_type=F32,
    )
    n_heads = logits.shape[0]
    logits = jnp.concatenate([logits, jnp.zeros((8 - n_heads, 256), F32)], 0)
    table = 16.0 * LOG2E / (1.0 + jnp.exp(-logits))
    before, after = table[:, :128], table[:, 128:]
    cell = lax.broadcasted_iota(jnp.int32, (8, 128), 1) % WIN
    for u in range(WIN):
        strip = jnp.where(
            cell >= u,
            pltpu.roll(before, u, 1) if u else before,
            pltpu.roll(after, (u - WIN) % 128, 1),
        )
        strips_ref[:, u, :] = strip


def turned(strip):
    cell = lax.broadcasted_iota(jnp.int32, (WIN, 128), 1) % WIN
    strip = pltpu.roll(strip, HALF, 0)
    return jnp.where(cell < HALF, pltpu.roll(strip, 128 - HALF, 1), pltpu.roll(strip, HALF, 1))


def bias_rows(strips, w):
    lane = lax.broadcasted_iota(jnp.int32, (WIN, 128), 1)
    back = (WIN - 1 - w) * WIN
    parts = []
    for pair in range(len(strips) // 2):
        low = pltpu.roll(strips[2 * pair], (128 - back) % 128, 1)
        high = pltpu.roll(strips[2 * pair + 1], (192 - back) % 128, 1)
        parts.append(jnp.where(lane < CELLS, low, high))
    return jnp.concatenate(parts, 1)


def layer_norm(values, gain_row):
    row_mean = jnp.mean(values, -1, keepdims=True)
    centred = values - row_mean
    spread = jnp.mean(centred * centred, -1, keepdims=True)
    return centred * lax.rsqrt(spread + 1e-05) * gain_row


def unit_vectors(t, heads_ref):
    t = t.astype(BF16).astype(F32)
    squares = dot((t * t).astype(BF16), heads_ref[...])
    return t * lax.rsqrt(squares + 1e-06)


def temper_row(temper, layer, mask_ref):
    row = jnp.zeros((1, mask_ref.shape[1]), F32)
    for h in range(mask_ref.shape[0]):
        row = row + (temper[layer, h] * LOG2E) * mask_ref[h : h + 1, :].astype(F32)
    return row


def spread_heads(t, mask_ref):
    low = [t[:, :128] * mask_ref[h : h + 1, :128] for h in range(4)]
    high = [t[:, 128:] * mask_ref[h : h + 1, 128:] for h in range(4, 6)]
    return jnp.concatenate(low, 0), jnp.concatenate(high, 0)


def scores_of(q, k, mask_ref):
    low, high = spread_heads(k, mask_ref)
    return jnp.concatenate([dot_nt(q[:, :128], low), dot_nt(q[:, 128:], high)], 1)


def weighted(p, low, high):
    return jnp.concatenate([dot(p[:, :256], low), dot(p[:, 256:], high)], 1)


def totals_of(p, ones_ref):
    return weighted(p, ones_ref[:256, :128], ones_ref[256:, 128:])


def dense_tail(x, mixed, proj_ref, up_ref, down_ref, gain_ref):
    attended = dot(mixed.astype(BF16), proj_ref[...])
    hidden = (x + layer_norm(attended, gain_ref[0:1, :])).astype(BF16)
    raised = dot(hidden, up_ref[...])
    expanded = (0.5 * raised * (1.0 + lax.erf(raised * math.sqrt(0.5)))).astype(BF16)
    reduced = dot_nt(expanded, down_ref[...])
    return (hidden.astype(F32) + layer_norm(reduced, gain_ref[1:2, :])).astype(BF16)


def attend(x, q_w, k_w, v_w, temper, heads_ref, ones_ref, mask_ref, bias_of, p_ref):
    n_windows = x.shape[0] // CELLS
    q = (unit_vectors(dot(x, q_w[...]), heads_ref) * temper).astype(BF16)
    k = unit_vectors(dot(x, k_w[...]), heads_ref).astype(BF16)
    v = dot(x, v_w[...]).astype(BF16)
    mixed = []
    for n in range(n_windows):
        rows = slice(n * CELLS, (n + 1) * CELLS)
        p_ref[rows, :] = jnp.exp2(scores_of(q[rows], k[rows], mask_ref) + bias_of(n)).astype(BF16)
    for n in range(n_windows):
        rows = slice(n * CELLS, (n + 1) * CELLS)
        mixed.append(weighted(p_ref[rows, :], *spread_heads(v[rows], mask_ref)))
    return jnp.concatenate(mixed, 0) / totals_of(p_ref[...], ones_ref)


def split_weights(qkv_ref, q_w, k_w, v_w):
    n_feat = q_w.shape[0]
    q_w[...] = qkv_ref[:, :n_feat]
    k_w[...] = qkv_ref[:, n_feat : 2 * n_feat]
    v_w[...] = qkv_ref[:, 2 * n_feat :]


def half_rows(tile):
    first = lax.broadcasted_iota(jnp.int32, (WIN, tile.shape[1]), 0) < HALF
    pairs = []
    for pair in range(2):
        even = tile[2 * pair * WIN : (2 * pair + 1) * WIN]
        odd = tile[(2 * pair + 1) * WIN : (2 * pair + 2) * WIN]
        pairs.append(jnp.where(first, even, pltpu.roll(odd, HALF, 0)))
    return jnp.concatenate(pairs, 0)


def whole_rows(halves):
    tiles = []
    for pair in range(2):
        rows = halves[pair * WIN : (pair + 1) * WIN]
        tiles += [rows, pltpu.roll(rows, HALF, 0)]
    return jnp.concatenate(tiles, 0)


def first_kernel(
    groups,
    targets, slots, temper, emb_ref, token_ref, coords_ref, heads_ref, ones_ref, mask_ref,
    net_in, net_first, net_out, qkv_ref, proj_ref, up_ref, down_ref, gain_ref,
    mid0_ref, mid1_ref, upper_ref, left_ref, send_ref,
    bias_ref, strips_ref, q_w, k_w, v_w, p_ref, staging, blank, sems, blank_sem,
):
    step = pl.program_id(0)
    n_heads, n_feat = mask_ref.shape

    no_slots = pltpu.make_async_copy(blank, send_ref.at[:, pl.ds(96, 8)], blank_sem)

    @pl.when(step == 0)
    def _():
        blank[...] = jnp.full(blank.shape, -1.0, BF16)
        no_slots.start()
        bias_strips(coords_ref, net_in, net_first[0:1, :], net_out[:, 0, :], strips_ref)
        strips = [strips_ref[h] for h in range(n_heads)]
        for w in range(WIN):
            bias_ref[w * WIN : (w + 1) * WIN, :] = bias_rows(strips, w)
        split_weights(qkv_ref, q_w, k_w, v_w)

    tiles = []
    for group in range(groups):
        slabs = []
        for w in range(WIN):
            at = (group * WIN + w) * n_feat
            slabs.append(emb_ref[:, at : at + n_feat].astype(F32))
        for i in range(2):
            tiles.append(jnp.concatenate([s[i * WIN : (i + 1) * WIN] for s in slabs], 0))
    x = jnp.concatenate(tiles, 0)
    mixed = attend(
        x.astype(BF16), q_w, k_w, v_w, temper_row(temper, 0, mask_ref), heads_ref, ones_ref, mask_ref,
        lambda n: bias_ref[...], p_ref,
    )

    @pl.when(step == 0)
    def _():
        no_slots.wait()

    y = jnp.concatenate(
        [
            dense_tail(x[n : n + 512], mixed[n : n + 512], proj_ref, up_ref, down_ref, gain_ref)
            for n in range(0, x.shape[0], 512)
        ],
        0,
    ).astype(F32)

    token = token_ref[...].astype(F32).reshape(1, n_feat)
    for group in range(groups):
        for i in range(2):
            n = 2 * group + i
            j = step * groups + group
            target = targets[i, j]
            tile = y[n * CELLS : (n + 1) * CELLS]
            kept = jnp.where(target >= 0, tile, token)
            rows = kept.astype(BF16)
            mid = (mid0_ref, mid1_ref)[i]
            mid[2 * group] = rows[:32]
            mid[2 * group + 1] = rows[32:]
            if i == 0:
                halves = [half_rows(kept[half * 32 : (half + 1) * 32]).astype(BF16) for half in range(2)]
                upper_ref[2 * group] = halves[0]
                upper_ref[2 * group + 1] = halves[1]
            if group == 0:

                @pl.when(step == 0)
                def _(i=i, rows=rows, halves=halves):
                    left_ref[i * 32 : (i + 1) * 32] = rows[:32]
                    if i == 0:
                        left_ref[64:] = halves[0]

            slot = j * 2 + i
            staging[slot, :64] = tile[:, :128].astype(BF16)
            tails = tile[:, 128:].reshape(4, 2, WIN, 64)
            joined = jnp.concatenate([tails[:, 0], tails[:, 1]], -1)
            staging[slot, 64:96] = joined.reshape(32, 128).astype(BF16)
            staging[slot, 96:] = jnp.full((8, 128), slots[i, j].astype(F32)).astype(BF16)

            @pl.when(target >= 0)
            def _(slot=slot, target=target):
                pltpu.make_async_copy(staging.at[slot], send_ref.at[target], sems.at[slot]).start()

    @pl.when(step == pl.num_programs(0) - 1)
    def _():
        def finish(slot, carry):
            target = targets[lax.rem(slot, 2), slot // 2]

            @pl.when(target >= 0)
            def _():
                pltpu.make_async_copy(staging.at[slot], send_ref.at[target], sems.at[slot]).wait()

            return carry

        lax.fori_loop(0, staging.shape[0], finish, 0)


def whole(array):
    zeros = (0,) * array.ndim
    return pl.BlockSpec(array.shape, lambda *_: zeros)


def layer_spec(array, position, layer):
    if position in (1, 2):
        return whole(array)
    rest = array.shape[1:]
    at = (layer,) + (0,) * len(rest)
    return pl.BlockSpec((None,) + rest, lambda *_: at)


def layer_scratch(n_heads, n_feat):
    square = pltpu.VMEM((n_feat, n_feat), BF16)
    return [pltpu.VMEM((8, WIN, 128), F32), square, square, square]


def first_layer(embedded, targets, slots, temper, token, consts, params, devices, groups=16):
    n_heads, n_feat = consts[3].shape
    columns = embedded.shape[1] // (WIN * n_feat)
    side = jax.ShapeDtypeStruct((80, n_feat), BF16)
    upper = jax.ShapeDtypeStruct((2 * columns, 16, n_feat), BF16)
    mid = jax.ShapeDtypeStruct((2 * columns, 32, n_feat), BF16)
    mid_spec = pl.BlockSpec((2 * groups, 32, n_feat), lambda g: (g, 0, 0))
    return pl.pallas_call(
        functools.partial(first_kernel, groups),
        grid=(columns // groups,),
        out_shape=(mid, mid, upper, side, jax.ShapeDtypeStruct((devices, 104, 128), BF16)),
        in_specs=[SMEM, SMEM, SMEM, pl.BlockSpec((2 * WIN, groups * WIN * n_feat), lambda g: (0, g))]
        + [whole(a) for a in (token,) + consts]
        + [layer_spec(a, n, 0) for n, a in enumerate(params)],
        out_specs=(mid_spec, mid_spec, pl.BlockSpec((2 * groups, 16, n_feat), lambda g: (g, 0, 0)), whole(side), ANY),
        scratch_shapes=[pltpu.VMEM((CELLS, n_heads * CELLS), F32)]
        + layer_scratch(n_heads, n_feat)
        + [
            pltpu.VMEM((groups * 2 * CELLS, n_heads * CELLS), BF16),
            pltpu.VMEM((2 * columns, 104, 128), BF16),
            pltpu.VMEM((devices, 8, 128), BF16),
            pltpu.SemaphoreType.DMA((2 * columns,)),
            pltpu.SemaphoreType.DMA,
        ],
        compiler_params=pltpu.CompilerParams(vmem_limit_bytes=VMEM_BYTES),
        cost_estimate=pl.CostEstimate(flops=2 * 10**9, bytes_accessed=6 * 10**6, transcendentals=10**6),
        name="first_layer",
    )(targets, slots, temper, embedded, token, *consts, *params)


def second_kernel(
    groups,
    place, temper, mid0_ref, mid1_ref, below_ref, right_ref, corner_ref,
    coords_ref, heads_ref, ones_ref, mask_ref,
    net_in, net_first, net_out, qkv_ref, proj_ref, up_ref, down_ref, gain_ref,
    out_ref, rows_ref, side_ref,
    bias_ref, strips_ref, q_w, k_w, v_w, ext, ring, p_ref, sems,
):
    step = pl.program_id(0)
    n_heads, n_feat = mask_ref.shape
    n_half = mid0_ref.shape[0]
    row, col, last_row, last_col = place[0], place[1], place[2], place[3]
    width = HALF * n_feat

    @pl.when(step == 0)
    def _():
        own = pl.ds(0, n_half)
        copies = [
            pltpu.make_async_copy(src, dst, sems.at[n])
            for n, (src, dst) in enumerate(
                [
                    (mid0_ref, ext.at[0, own]),
                    (mid1_ref, ext.at[1, own]),
                    (right_ref.at[pl.ds(0, 32)], ext.at[0, n_half]),
                    (right_ref.at[pl.ds(32, 32)], ext.at[1, n_half]),
                    (below_ref, ring.at[own]),
                    (corner_ref.at[pl.ds(64, 16)], ring.at[n_half]),
                ]
            )
        ]
        for copy in copies:
            copy.start()
        out_ref[:, :width] = jnp.zeros((2 * WIN, width), BF16)
        split_weights(qkv_ref, q_w, k_w, v_w)
        bias_strips(coords_ref, net_in, net_first[1:2, :], net_out[:, 1, :], strips_ref)
        strips = [turned(strips_ref[h]) for h in range(n_heads)]
        lane = lax.broadcasted_iota(jnp.int32, (WIN, n_heads * CELLS), 1)
        upper = lax.broadcasted_iota(jnp.int32, (WIN, n_heads * CELLS), 0) < HALF
        other_rows = upper != (lane % WIN < HALF)
        for w in range(WIN):
            other_cols = (lane % CELLS >= CELLS // 2) != (w >= HALF)
            rows = slice(w * WIN, (w + 1) * WIN)
            bias = bias_rows(strips, w)
            away = -100.0 * LOG2E
            bias_ref[0, rows, :] = bias
            bias_ref[1, rows, :] = bias + jnp.where(other_cols, away, 0.0)
            bias_ref[2, rows, :] = bias + jnp.where(other_rows, away, 0.0)
            bias_ref[3, rows, :] = bias + jnp.where(other_rows | other_cols, away, 0.0)
        for copy in copies:
            copy.wait()

    upper = lax.broadcasted_iota(jnp.int32, (CELLS, n_feat), 0) % WIN < HALF
    tiles = []
    for group in range(groups):
        at = 2 * (step * groups + group) + 1
        zero = jnp.concatenate([ext[0, at], ext[0, at + 1]], 0)
        one = jnp.concatenate([ext[1, at], ext[1, at + 1]], 0)
        two = jnp.concatenate([whole_rows(ring[at + half].astype(F32)) for half in range(2)], 0)
        tiles += [jnp.where(upper, one, zero), jnp.where(upper, two.astype(BF16), one)]
    x = jnp.concatenate(tiles, 0)
    low_cut = (row == last_row).astype(jnp.int32)

    def bias_of(n):
        column = step * groups + n // 2
        cut = ((col == last_col) & (column == n_half // 2 - 1)).astype(jnp.int32)
        return bias_ref[cut + 2 * low_cut * (n % 2)]

    mixed = attend(
        x, q_w, k_w, v_w, temper_row(temper, 1, mask_ref), heads_ref, ones_ref, mask_ref, bias_of, p_ref
    )
    y = dense_tail(x.astype(F32), mixed, proj_ref, up_ref, down_ref, gain_ref).astype(F32)

    for group in range(groups):
        first = y[2 * group * CELLS : (2 * group + 1) * CELLS]
        second = y[(2 * group + 1) * CELLS : (2 * group + 2) * CELLS]
        zero = jnp.where(upper, second, first)
        one = jnp.where(upper, first, second)
        for half in range(2):
            slabs = []
            for w in range(half * HALF, (half + 1) * HALF):
                rows = slice(w * WIN, (w + 1) * WIN)
                slabs.append(jnp.concatenate([zero[rows], one[rows]], 0))
            strip = jnp.concatenate(slabs, 1).astype(BF16)
            at = 2 * (step * groups + group) + 1 + half
            if half == 0 or group < groups - 1:
                out_ref[:, pl.ds(pl.multiple_of(at * width, 128), width)] = strip
            else:

                @pl.when(at < n_half)
                def _(at=at, strip=strip):
                    out_ref[:, pl.ds(pl.multiple_of(at * width, 128), width)] = strip

                @pl.when(at == n_half)
                def _(strip=strip):
                    side_ref[...] = strip

    @pl.when(step == pl.num_programs(0) - 1)
    def _():
        quarter = rows_ref.shape[1]
        first = lax.broadcasted_iota(jnp.int32, (WIN, quarter), 0) < HALF
        tops = [out_ref[:, n * quarter : (n + 1) * quarter][:WIN].astype(F32) for n in range(4)]
        pairs = [
            jnp.where(first, tops[2 * n], pltpu.roll(tops[2 * n + 1], HALF, 0)) for n in range(2)
        ]
        rows_ref[...] = jnp.concatenate(pairs, 0).astype(BF16)


def second_layer(place, temper, pieces, consts, params, groups=8):
    n_heads, n_feat = consts[3].shape
    n_half = pieces[0].shape[0]
    out = jax.ShapeDtypeStruct((2 * WIN, n_half * HALF * n_feat), BF16)
    rows = jax.ShapeDtypeStruct((2 * WIN, n_half * n_feat), BF16)
    side = jax.ShapeDtypeStruct((2 * WIN, HALF * n_feat), BF16)
    return pl.pallas_call(
        functools.partial(second_kernel, groups),
        grid=(n_half // 2 // groups,),
        out_shape=(out, rows, side),
        in_specs=[SMEM, SMEM]
        + [ANY] * len(pieces)
        + [whole(a) for a in consts]
        + [layer_spec(a, n, 1) for n, a in enumerate(params)],
        out_specs=(whole(out), whole(rows), whole(side)),
        scratch_shapes=[pltpu.VMEM((4, CELLS, n_heads * CELLS), F32)]
        + layer_scratch(n_heads, n_feat)
        + [
            pltpu.VMEM((2, n_half + 1, 32, n_feat), BF16),
            pltpu.VMEM((n_half + 1, 16, n_feat), BF16),
            pltpu.VMEM((groups * 2 * CELLS, n_heads * CELLS), BF16),
            pltpu.SemaphoreType.DMA((6,)),
        ],
        compiler_params=pltpu.CompilerParams(vmem_limit_bytes=VMEM_BYTES),
        cost_estimate=pl.CostEstimate(flops=10**11, bytes_accessed=10**7, transcendentals=10**6),
        name="second_layer",
    )(place, temper, *pieces, *consts, *params)


def merge_features(own_ref, rows_ref, side_ref, corner_ref, out_ref):
    quarter, width = rows_ref.shape[1], side_ref.shape[1]
    first = lax.broadcasted_iota(jnp.int32, (WIN, quarter), 0) < HALF
    for n in range(4):
        lanes = slice(n * quarter, (n + 1) * quarter)
        own = own_ref[:, lanes].astype(F32)
        top = rows_ref[...].astype(F32)[n // 2 * WIN : (n // 2 + 1) * WIN]
        top = pltpu.roll(top, HALF, 0) if n % 2 else top
        merged = jnp.concatenate([jnp.where(first, top, own[:WIN]), own[WIN:]], 0)
        out_ref[:, lanes] = merged.astype(BF16)
    corner = lax.broadcasted_iota(jnp.int32, (2 * WIN, width), 0) < HALF
    merged = jnp.where(corner, corner_ref[...].astype(F32), side_ref[...].astype(F32))
    out_ref[:, :width] = merged.astype(BF16)


def last_kernel(
    entries_ref, own_hbm, rows_ref, side_ref, corner_ref, features_hbm, packed_ref,
    marks_ref, held, own_ref, features_ref, sems, slot_sems,
):
    slots = packed_ref.shape[0]
    marks_copy = pltpu.make_async_copy(entries_ref.at[:, pl.ds(96, 8)], marks_ref, sems.at[0])
    own_copy = pltpu.make_async_copy(own_hbm, own_ref, sems.at[1])
    marks_copy.start()
    own_copy.start()
    marks_copy.wait()
    marks = marks_ref[...].astype(F32)
    lane = lax.broadcasted_iota(jnp.int32, marks.shape, 2).astype(F32)
    sender = lax.broadcasted_iota(jnp.int32, marks.shape, 0).astype(F32)
    found = jnp.max(jnp.where(marks == lane, sender, 0.0), 0).astype(jnp.int32)
    windows = [
        pltpu.make_async_copy(entries_ref.at[found[0, slot]], held.at[slot], slot_sems.at[slot])
        for slot in range(slots)
    ]
    for copy in windows:
        copy.start()
    own_copy.wait()
    merge_features(own_ref, rows_ref, side_ref, corner_ref, features_ref)
    leave = pltpu.make_async_copy(features_ref, features_hbm, sems.at[2])
    leave.start()
    for copy in windows:
        copy.wait()
    lane = lax.broadcasted_iota(jnp.int32, (slots, 128), 1)

    def rows_of(at):
        return jnp.swapaxes(held[:, at : at + WIN, :].astype(F32), 0, 1)

    for pair in range(WIN // 2):
        even = rows_of(2 * pair * WIN)
        odd = rows_of((2 * pair + 1) * WIN)
        tails = rows_of(CELLS + pair * WIN)
        for u in range(WIN):
            moved = pltpu.roll(odd[u], 64, 1)
            joined = [
                even[u],
                jnp.where(lane < 64, tails[u], moved),
                jnp.where(lane < 64, moved, tails[u]),
            ]
            at = (u * WIN + 2 * pair) * 192
            packed_ref[:, at : at + 384] = jnp.concatenate(joined, 1).astype(BF16)
    leave.wait()


def last_steps(arrived, own, rows, side, corner, slots, width):
    return pl.pallas_call(
        last_kernel,
        out_shape=(jax.ShapeDtypeStruct(own.shape, BF16), jax.ShapeDtypeStruct((slots, width), BF16)),
        in_specs=[ANY, ANY] + [pl.BlockSpec(memory_space=pltpu.VMEM)] * 3,
        out_specs=(ANY, pl.BlockSpec(memory_space=pltpu.VMEM)),
        scratch_shapes=[
            pltpu.VMEM((arrived.shape[0], 8, 128), BF16),
            pltpu.VMEM((slots,) + arrived.shape[1:], BF16),
        ]
        + [pltpu.VMEM(own.shape, BF16)] * 2
        + [pltpu.SemaphoreType.DMA((3,)), pltpu.SemaphoreType.DMA((slots,))],
        compiler_params=pltpu.CompilerParams(vmem_limit_bytes=LAST_BYTES),
        name="last_steps",
    )(arrived, own, rows, side, corner)


def moved(block, rows, cols):
    n_row, n_col = lax.axis_size("row"), lax.axis_size("col")
    route = [
        (r * n_col + c, (r + rows) % n_row * n_col + (c + cols) % n_col)
        for r in range(n_row)
        for c in range(n_col)
    ]
    return lax.ppermute(block, ("row", "col"), route)


def local(
    embedded,
    window_target_device,
    window_device_slot,
    cloud_mask_token,
    query_key_value_weight,
    projection_weight,
    up_weight,
    down_weight,
    bias_net_input_weight,
    bias_net_first_bias,
    bias_net_output_weight,
    temper,
    norm_gain_values,
):
    n_row, n_col = lax.axis_size("row"), lax.axis_size("col")
    n_heads, n_feat = temper.shape[1], cloud_mask_token.shape[0]
    slots = window_target_device.size // 2
    row, col = lax.axis_index("row"), lax.axis_index("col")
    place = jnp.stack([row, col, n_row - 1, n_col - 1]).astype(jnp.int32)
    consts = constants(n_heads, n_feat)
    params = (
        bias_net_input_weight,
        bias_net_first_bias,
        jnp.transpose(bias_net_output_weight, (2, 0, 1)),
        query_key_value_weight,
        projection_weight,
        up_weight,
        jnp.swapaxes(down_weight, 1, 2),
        norm_gain_values,
    )
    mid0, mid1, upper, left, send = first_layer(
        embedded, window_target_device, window_device_slot, temper, cloud_mask_token, consts, params,
        n_row * n_col,
    )
    pieces = (mid0, mid1, moved(upper, -1, 0), moved(left, 0, -1), moved(left, -1, -1))
    arrived = lax.all_to_all(send, ("row", "col"), split_axis=0, concat_axis=0, tiled=True)
    own, rows, side = second_layer(place, temper, pieces, consts, params)
    return last_steps(
        arrived, own, moved(rows, 1, 0), moved(side, 0, 1), moved(side, 1, 1), slots, CELLS * n_feat
    )


def solution(mesh):
    in_specs = (P("row", "col"),) * 3 + (P(),) * 10
    out_specs = (P("row", "col"), P(("row", "col"), None))
    return jax.shard_map(local, mesh=mesh, in_specs=in_specs, out_specs=out_specs, check_vma=False)
```

```python
import functools
import math

import jax
import jax.numpy as jnp
import numpy as np
from jax import lax
from jax.experimental import pallas as pl
from jax.experimental.pallas import tpu as pltpu
from jax.sharding import PartitionSpec as P

WIN = 8
HALF = WIN // 2
CELLS = WIN * WIN
LOG2E = math.log2(math.e)
F32 = jnp.float32
BF16 = jnp.bfloat16
VMEM_BYTES = 60 * 2**20
LAST_BYTES = 62 * 2**20
SMEM = pl.BlockSpec(memory_space=pltpu.SMEM)
ANY = pl.BlockSpec(memory_space=pl.ANY)


def log_step(offset):
    scaled = np.abs(offset).astype(np.float32) * np.float32(8.0 / (WIN - 1))
    return np.sign(offset) * np.log2(scaled + 1.0) / 3.0


def offset_coords():
    lane = np.arange(128)
    across = np.maximum(WIN - 1 - lane // WIN, 1 - WIN)
    down = np.concatenate([-(lane % WIN), np.minimum(WIN - lane % WIN, WIN - 1)])
    return np.stack([log_step(down), log_step(np.tile(across, 2))], 1).astype(np.float32)


def head_blocks(rows, row_block, cols, col_block):
    same = (np.arange(rows) // row_block)[:, None] == (np.arange(cols) // col_block)[None, :]
    return same.astype(np.float32)


def constants(n_heads, n_feat):
    per_head = n_feat // n_heads
    return (
        jnp.asarray(offset_coords(), F32),
        jnp.asarray(head_blocks(n_feat, per_head, n_feat, per_head), BF16),
        jnp.asarray(head_blocks(n_heads * CELLS, CELLS, n_feat, per_head), BF16),
        jnp.asarray(head_blocks(n_heads, 1, n_feat, per_head), BF16),
    )


def dot(a, b):
    return jnp.dot(a, b, preferred_element_type=F32)


def dot_nt(a, b):
    return lax.dot_general(a, b, (((1,), (1,)), ((), ())), preferred_element_type=F32)


def bias_strips(coords_ref, net_in, net_first, net_out, strips_ref):
    coords = coords_ref[...]
    units = jnp.maximum(
        coords[:, 0:1] * net_in[0:1, :] + coords[:, 1:2] * net_in[1:2, :] + net_first, 0.0
    )
    logits = lax.dot_general(
        net_out, units, (((1,), (1,)), ((), ())),
        precision=lax.Precision.HIGHEST, preferred_element_type=F32,
    )
    n_heads = logits.shape[0]
    logits = jnp.concatenate([logits, jnp.zeros((8 - n_heads, 256), F32)], 0)
    table = 16.0 * LOG2E / (1.0 + jnp.exp(-logits))
    before, after = table[:, :128], table[:, 128:]
    cell = lax.broadcasted_iota(jnp.int32, (8, 128), 1) % WIN
    for u in range(WIN):
        strip = jnp.where(
            cell >= u,
            pltpu.roll(before, u, 1) if u else before,
            pltpu.roll(after, (u - WIN) % 128, 1),
        )
        strips_ref[:, u, :] = strip


def turned(strip):
    cell = lax.broadcasted_iota(jnp.int32, (WIN, 128), 1) % WIN
    strip = pltpu.roll(strip, HALF, 0)
    return jnp.where(cell < HALF, pltpu.roll(strip, 128 - HALF, 1), pltpu.roll(strip, HALF, 1))


def bias_rows(strips, w):
    lane = lax.broadcasted_iota(jnp.int32, (WIN, 128), 1)
    back = (WIN - 1 - w) * WIN
    parts = []
    for pair in range(len(strips) // 2):
        low = pltpu.roll(strips[2 * pair], (128 - back) % 128, 1)
        high = pltpu.roll(strips[2 * pair + 1], (192 - back) % 128, 1)
        parts.append(jnp.where(lane < CELLS, low, high))
    return jnp.concatenate(parts, 1)


def layer_norm(values, gain_row):
    row_mean = jnp.mean(values, -1, keepdims=True)
    centred = values - row_mean
    spread = jnp.mean(centred * centred, -1, keepdims=True)
    return centred * lax.rsqrt(spread + 1e-05) * gain_row


def unit_vectors(t, heads_ref):
    t = t.astype(BF16).astype(F32)
    squares = dot((t * t).astype(BF16), heads_ref[...])
    return t * lax.rsqrt(squares + 1e-06)


def temper_row(temper, layer, mask_ref):
    row = jnp.zeros((1, mask_ref.shape[1]), F32)
    for h in range(mask_ref.shape[0]):
        row = row + (temper[layer, h] * LOG2E) * mask_ref[h : h + 1, :].astype(F32)
    return row


def spread_heads(t, mask_ref):
    low = [t[:, :128] * mask_ref[h : h + 1, :128] for h in range(4)]
    high = [t[:, 128:] * mask_ref[h : h + 1, 128:] for h in range(4, 6)]
    return jnp.concatenate(low, 0), jnp.concatenate(high, 0)


def scores_of(q, k, mask_ref):
    low, high = spread_heads(k, mask_ref)
    return jnp.concatenate([dot_nt(q[:, :128], low), dot_nt(q[:, 128:], high)], 1)


def weighted(p, low, high):
    return jnp.concatenate([dot(p[:, :256], low), dot(p[:, 256:], high)], 1)


def totals_of(p, ones_ref):
    return weighted(p, ones_ref[:256, :128], ones_ref[256:, 128:])


def dense_tail(x, mixed, proj_ref, up_ref, down_ref, gain_ref):
    attended = dot(mixed.astype(BF16), proj_ref[...])
    hidden = (x + layer_norm(attended, gain_ref[0:1, :])).astype(BF16)
    raised = dot(hidden, up_ref[...])
    expanded = (0.5 * raised * (1.0 + lax.erf(raised * math.sqrt(0.5)))).astype(BF16)
    reduced = dot_nt(expanded, down_ref[...])
    return (hidden.astype(F32) + layer_norm(reduced, gain_ref[1:2, :])).astype(BF16)


def attend(x, q_w, k_w, v_w, temper, heads_ref, ones_ref, mask_ref, bias_of, p_ref):
    n_windows = x.shape[0] // CELLS
    q = (unit_vectors(dot(x, q_w[...]), heads_ref) * temper).astype(BF16)
    k = unit_vectors(dot(x, k_w[...]), heads_ref).astype(BF16)
    v = dot(x, v_w[...]).astype(BF16)
    mixed = []
    for n in range(n_windows):
        rows = slice(n * CELLS, (n + 1) * CELLS)
        p_ref[rows, :] = jnp.exp2(scores_of(q[rows], k[rows], mask_ref) + bias_of(n)).astype(BF16)
    for n in range(n_windows):
        rows = slice(n * CELLS, (n + 1) * CELLS)
        mixed.append(weighted(p_ref[rows, :], *spread_heads(v[rows], mask_ref)))
    return jnp.concatenate(mixed, 0) / totals_of(p_ref[...], ones_ref)


def split_weights(qkv_ref, q_w, k_w, v_w):
    n_feat = q_w.shape[0]
    q_w[...] = qkv_ref[:, :n_feat]
    k_w[...] = qkv_ref[:, n_feat : 2 * n_feat]
    v_w[...] = qkv_ref[:, 2 * n_feat :]


def half_rows(tile):
    first = lax.broadcasted_iota(jnp.int32, (WIN, tile.shape[1]), 0) < HALF
    pairs = []
    for pair in range(2):
        even = tile[2 * pair * WIN : (2 * pair + 1) * WIN]
        odd = tile[(2 * pair + 1) * WIN : (2 * pair + 2) * WIN]
        pairs.append(jnp.where(first, even, pltpu.roll(odd, HALF, 0)))
    return jnp.concatenate(pairs, 0)


def whole_rows(halves):
    tiles = []
    for pair in range(2):
        rows = halves[pair * WIN : (pair + 1) * WIN]
        tiles += [rows, pltpu.roll(rows, HALF, 0)]
    return jnp.concatenate(tiles, 0)


def first_kernel(
    groups,
    targets, slots, temper, emb_ref, token_ref, coords_ref, heads_ref, ones_ref, mask_ref,
    net_in, net_first, net_out, qkv_ref, proj_ref, up_ref, down_ref, gain_ref,
    mid0_ref, mid1_ref, upper_ref, left_ref, send_ref,
    bias_ref, strips_ref, q_w, k_w, v_w, p_ref, staging, blank, sems, blank_sem,
):
    step = pl.program_id(0)
    n_heads, n_feat = mask_ref.shape

    no_slots = pltpu.make_async_copy(blank, send_ref.at[:, pl.ds(24, 1)], blank_sem)

    @pl.when(step == 0)
    def _():
        blank[...] = jnp.full(blank.shape, -1.0, BF16)
        no_slots.start()
        bias_strips(coords_ref, net_in, net_first[0:1, :], net_out[:, 0, :], strips_ref)
        strips = [strips_ref[h] for h in range(n_heads)]
        for w in range(WIN):
            bias_ref[w * WIN : (w + 1) * WIN, :] = bias_rows(strips, w)
        split_weights(qkv_ref, q_w, k_w, v_w)

    tiles = []
    for group in range(groups):
        slabs = []
        for w in range(WIN):
            at = (group * WIN + w) * n_feat
            slabs.append(emb_ref[:, at : at + n_feat].astype(F32))
        for i in range(2):
            tiles.append(jnp.concatenate([s[i * WIN : (i + 1) * WIN] for s in slabs], 0))
    x = jnp.concatenate(tiles, 0)
    mixed = attend(
        x.astype(BF16), q_w, k_w, v_w, temper_row(temper, 0, mask_ref), heads_ref, ones_ref, mask_ref,
        lambda n: bias_ref[...], p_ref,
    )

    @pl.when(step == 0)
    def _():
        no_slots.wait()

    y = jnp.concatenate(
        [
            dense_tail(x[n : n + 512], mixed[n : n + 512], proj_ref, up_ref, down_ref, gain_ref)
            for n in range(0, x.shape[0], 512)
        ],
        0,
    ).astype(F32)

    token = token_ref[...].astype(F32).reshape(1, n_feat)
    for group in range(groups):
        for i in range(2):
            n = 2 * group + i
            j = step * groups + group
            target = targets[i, j]
            tile = y[n * CELLS : (n + 1) * CELLS]
            kept = jnp.where(target >= 0, tile, token)
            rows = kept.astype(BF16)
            mid = (mid0_ref, mid1_ref)[i]
            mid[2 * group] = rows[:32]
            mid[2 * group + 1] = rows[32:]
            if i == 0:
                halves = [half_rows(kept[half * 32 : (half + 1) * 32]).astype(BF16) for half in range(2)]
                upper_ref[2 * group] = halves[0]
                upper_ref[2 * group + 1] = halves[1]
            if group == 0:

                @pl.when(step == 0)
                def _(i=i, rows=rows, halves=halves):
                    left_ref[i * 32 : (i + 1) * 32] = rows[:32]
                    if i == 0:
                        left_ref[64:] = halves[0]

            slot = j * 2 + i
            staging[slot, :16] = tile[:, :128].reshape(16, 4, 128).astype(BF16)
            tails = tile[:, 128:].reshape(4, 2, WIN, 64)
            joined = jnp.concatenate([tails[:, 0], tails[:, 1]], -1)
            staging[slot, 16:24] = joined.reshape(8, 4, 128).astype(BF16)
            staging[slot, 24:] = jnp.full((1, 4, 128), slots[i, j].astype(F32)).astype(BF16)

            @pl.when(target >= 0)
            def _(slot=slot, target=target):
                pltpu.make_async_copy(staging.at[slot], send_ref.at[target], sems.at[slot]).start()

    @pl.when(step == pl.num_programs(0) - 1)
    def _():
        def finish(slot, carry):
            target = targets[lax.rem(slot, 2), slot // 2]

            @pl.when(target >= 0)
            def _():
                pltpu.make_async_copy(staging.at[slot], send_ref.at[target], sems.at[slot]).wait()

            return carry

        lax.fori_loop(0, staging.shape[0], finish, 0)


def whole(array):
    zeros = (0,) * array.ndim
    return pl.BlockSpec(array.shape, lambda *_: zeros)


def layer_spec(array, position, layer):
    if position in (1, 2):
        return whole(array)
    rest = array.shape[1:]
    at = (layer,) + (0,) * len(rest)
    return pl.BlockSpec((None,) + rest, lambda *_: at)


def layer_scratch(n_heads, n_feat):
    square = pltpu.VMEM((n_feat, n_feat), BF16)
    return [pltpu.VMEM((8, WIN, 128), F32), square, square, square]


def first_layer(embedded, targets, slots, temper, token, consts, params, devices, groups=16):
    n_heads, n_feat = consts[3].shape
    columns = embedded.shape[1] // (WIN * n_feat)
    side = jax.ShapeDtypeStruct((80, n_feat), BF16)
    upper = jax.ShapeDtypeStruct((2 * columns, 16, n_feat), BF16)
    mid = jax.ShapeDtypeStruct((2 * columns, 32, n_feat), BF16)
    mid_spec = pl.BlockSpec((2 * groups, 32, n_feat), lambda g: (g, 0, 0))
    return pl.pallas_call(
        functools.partial(first_kernel, groups),
        grid=(columns // groups,),
        out_shape=(mid, mid, upper, side, jax.ShapeDtypeStruct((devices, 25, 4, 128), BF16)),
        in_specs=[SMEM, SMEM, SMEM, pl.BlockSpec((2 * WIN, groups * WIN * n_feat), lambda g: (0, g))]
        + [whole(a) for a in (token,) + consts]
        + [layer_spec(a, n, 0) for n, a in enumerate(params)],
        out_specs=(mid_spec, mid_spec, pl.BlockSpec((2 * groups, 16, n_feat), lambda g: (g, 0, 0)), whole(side), ANY),
        scratch_shapes=[pltpu.VMEM((CELLS, n_heads * CELLS), F32)]
        + layer_scratch(n_heads, n_feat)
        + [
            pltpu.VMEM((groups * 2 * CELLS, n_heads * CELLS), BF16),
            pltpu.VMEM((2 * columns, 25, 4, 128), BF16),
            pltpu.VMEM((devices, 1, 4, 128), BF16),
            pltpu.SemaphoreType.DMA((2 * columns,)),
            pltpu.SemaphoreType.DMA,
        ],
        compiler_params=pltpu.CompilerParams(vmem_limit_bytes=VMEM_BYTES),
        cost_estimate=pl.CostEstimate(flops=2 * 10**9, bytes_accessed=6 * 10**6, transcendentals=10**6),
        name="first_layer",
    )(targets, slots, temper, embedded, token, *consts, *params)


def second_kernel(
    groups,
    place, temper, mid0_ref, mid1_ref, below_ref, right_ref, corner_ref,
    coords_ref, heads_ref, ones_ref, mask_ref,
    net_in, net_first, net_out, qkv_ref, proj_ref, up_ref, down_ref, gain_ref,
    out_ref, rows_ref, side_ref,
    bias_ref, strips_ref, q_w, k_w, v_w, ext, ring, p_ref, sems,
):
    step = pl.program_id(0)
    n_heads, n_feat = mask_ref.shape
    n_half = mid0_ref.shape[0]
    row, col, last_row, last_col = place[0], place[1], place[2], place[3]
    width = HALF * n_feat

    @pl.when(step == 0)
    def _():
        own = pl.ds(0, n_half)
        copies = [
            pltpu.make_async_copy(src, dst, sems.at[n])
            for n, (src, dst) in enumerate(
                [
                    (mid0_ref, ext.at[0, own]),
                    (mid1_ref, ext.at[1, own]),
                    (right_ref.at[pl.ds(0, 32)], ext.at[0, n_half]),
                    (right_ref.at[pl.ds(32, 32)], ext.at[1, n_half]),
                    (below_ref, ring.at[own]),
                    (corner_ref.at[pl.ds(64, 16)], ring.at[n_half]),
                ]
            )
        ]
        for copy in copies:
            copy.start()
        out_ref[:, :width] = jnp.zeros((2 * WIN, width), BF16)
        split_weights(qkv_ref, q_w, k_w, v_w)
        bias_strips(coords_ref, net_in, net_first[1:2, :], net_out[:, 1, :], strips_ref)
        strips = [turned(strips_ref[h]) for h in range(n_heads)]
        lane = lax.broadcasted_iota(jnp.int32, (WIN, n_heads * CELLS), 1)
        upper = lax.broadcasted_iota(jnp.int32, (WIN, n_heads * CELLS), 0) < HALF
        other_rows = upper != (lane % WIN < HALF)
        for w in range(WIN):
            other_cols = (lane % CELLS >= CELLS // 2) != (w >= HALF)
            rows = slice(w * WIN, (w + 1) * WIN)
            bias = bias_rows(strips, w)
            away = -100.0 * LOG2E
            bias_ref[0, rows, :] = bias
            bias_ref[1, rows, :] = bias + jnp.where(other_cols, away, 0.0)
            bias_ref[2, rows, :] = bias + jnp.where(other_rows, away, 0.0)
            bias_ref[3, rows, :] = bias + jnp.where(other_rows | other_cols, away, 0.0)
        for copy in copies:
            copy.wait()

    upper = lax.broadcasted_iota(jnp.int32, (CELLS, n_feat), 0) % WIN < HALF
    tiles = []
    for group in range(groups):
        at = 2 * (step * groups + group) + 1
        zero = jnp.concatenate([ext[0, at], ext[0, at + 1]], 0)
        one = jnp.concatenate([ext[1, at], ext[1, at + 1]], 0)
        two = jnp.concatenate([whole_rows(ring[at + half].astype(F32)) for half in range(2)], 0)
        tiles += [jnp.where(upper, one, zero), jnp.where(upper, two.astype(BF16), one)]
    x = jnp.concatenate(tiles, 0)
    low_cut = (row == last_row).astype(jnp.int32)

    def bias_of(n):
        column = step * groups + n // 2
        cut = ((col == last_col) & (column == n_half // 2 - 1)).astype(jnp.int32)
        return bias_ref[cut + 2 * low_cut * (n % 2)]

    mixed = attend(
        x, q_w, k_w, v_w, temper_row(temper, 1, mask_ref), heads_ref, ones_ref, mask_ref, bias_of, p_ref
    )
    y = dense_tail(x.astype(F32), mixed, proj_ref, up_ref, down_ref, gain_ref).astype(F32)

    for group in range(groups):
        first = y[2 * group * CELLS : (2 * group + 1) * CELLS]
        second = y[(2 * group + 1) * CELLS : (2 * group + 2) * CELLS]
        zero = jnp.where(upper, second, first)
        one = jnp.where(upper, first, second)
        for half in range(2):
            slabs = []
            for w in range(half * HALF, (half + 1) * HALF):
                rows = slice(w * WIN, (w + 1) * WIN)
                slabs.append(jnp.concatenate([zero[rows], one[rows]], 0))
            strip = jnp.concatenate(slabs, 1).astype(BF16)
            at = 2 * (step * groups + group) + 1 + half
            if half == 0 or group < groups - 1:
                out_ref[:, pl.ds(pl.multiple_of(at * width, 128), width)] = strip
            else:

                @pl.when(at < n_half)
                def _(at=at, strip=strip):
                    out_ref[:, pl.ds(pl.multiple_of(at * width, 128), width)] = strip

                @pl.when(at == n_half)
                def _(strip=strip):
                    side_ref[...] = strip

    @pl.when(step == pl.num_programs(0) - 1)
    def _():
        quarter = rows_ref.shape[1]
        first = lax.broadcasted_iota(jnp.int32, (WIN, quarter), 0) < HALF
        tops = [out_ref[:, n * quarter : (n + 1) * quarter][:WIN].astype(F32) for n in range(4)]
        pairs = [
            jnp.where(first, tops[2 * n], pltpu.roll(tops[2 * n + 1], HALF, 0)) for n in range(2)
        ]
        rows_ref[...] = jnp.concatenate(pairs, 0).astype(BF16)


def second_layer(place, temper, pieces, consts, params, groups=8):
    n_heads, n_feat = consts[3].shape
    n_half = pieces[0].shape[0]
    out = jax.ShapeDtypeStruct((2 * WIN, n_half * HALF * n_feat), BF16)
    rows = jax.ShapeDtypeStruct((2 * WIN, n_half * n_feat), BF16)
    side = jax.ShapeDtypeStruct((2 * WIN, HALF * n_feat), BF16)
    return pl.pallas_call(
        functools.partial(second_kernel, groups),
        grid=(n_half // 2 // groups,),
        out_shape=(out, rows, side),
        in_specs=[SMEM, SMEM]
        + [ANY] * len(pieces)
        + [whole(a) for a in consts]
        + [layer_spec(a, n, 1) for n, a in enumerate(params)],
        out_specs=(whole(out), whole(rows), whole(side)),
        scratch_shapes=[pltpu.VMEM((4, CELLS, n_heads * CELLS), F32)]
        + layer_scratch(n_heads, n_feat)
        + [
            pltpu.VMEM((2, n_half + 1, 32, n_feat), BF16),
            pltpu.VMEM((n_half + 1, 16, n_feat), BF16),
            pltpu.VMEM((groups * 2 * CELLS, n_heads * CELLS), BF16),
            pltpu.SemaphoreType.DMA((6,)),
        ],
        compiler_params=pltpu.CompilerParams(vmem_limit_bytes=VMEM_BYTES),
        cost_estimate=pl.CostEstimate(flops=10**11, bytes_accessed=10**7, transcendentals=10**6),
        name="second_layer",
    )(place, temper, *pieces, *consts, *params)


def merge_features(own_ref, rows_ref, side_ref, corner_ref, out_ref):
    quarter, width = rows_ref.shape[1], side_ref.shape[1]
    first = lax.broadcasted_iota(jnp.int32, (WIN, quarter), 0) < HALF
    for n in range(4):
        lanes = slice(n * quarter, (n + 1) * quarter)
        own = own_ref[:, lanes].astype(F32)
        top = rows_ref[...].astype(F32)[n // 2 * WIN : (n // 2 + 1) * WIN]
        top = pltpu.roll(top, HALF, 0) if n % 2 else top
        merged = jnp.concatenate([jnp.where(first, top, own[:WIN]), own[WIN:]], 0)
        out_ref[:, lanes] = merged.astype(BF16)
    corner = lax.broadcasted_iota(jnp.int32, (2 * WIN, width), 0) < HALF
    merged = jnp.where(corner, corner_ref[...].astype(F32), side_ref[...].astype(F32))
    out_ref[:, :width] = merged.astype(BF16)


def last_kernel(
    entries_ref, own_hbm, rows_ref, side_ref, corner_ref, features_hbm, packed_ref,
    marks_ref, held, own_ref, features_ref, sems, slot_sems,
):
    slots = packed_ref.shape[0]
    marks_copy = pltpu.make_async_copy(entries_ref.at[:, pl.ds(24, 1)], marks_ref, sems.at[0])
    own_copy = pltpu.make_async_copy(own_hbm, own_ref, sems.at[1])
    marks_copy.start()
    own_copy.start()
    marks_copy.wait()
    marks = marks_ref[...][:, 0].astype(F32)
    lane = lax.broadcasted_iota(jnp.int32, marks.shape, 2).astype(F32)
    sender = lax.broadcasted_iota(jnp.int32, marks.shape, 0).astype(F32)
    found = jnp.max(jnp.where(marks == lane, sender, 0.0), 0).astype(jnp.int32)
    windows = [
        pltpu.make_async_copy(entries_ref.at[found[0, slot]], held.at[slot], slot_sems.at[slot])
        for slot in range(slots)
    ]
    for copy in windows:
        copy.start()
    own_copy.wait()
    merge_features(own_ref, rows_ref, side_ref, corner_ref, features_ref)
    leave = pltpu.make_async_copy(features_ref, features_hbm, sems.at[2])
    leave.start()
    for copy in windows:
        copy.wait()
    lane = lax.broadcasted_iota(jnp.int32, (slots, 128), 1)

    def rows_of(at):
        rows = held[:, at // 4 : at // 4 + 2].astype(F32).reshape(slots, WIN, 128)
        return jnp.swapaxes(rows, 0, 1)

    for pair in range(WIN // 2):
        even = rows_of(2 * pair * WIN)
        odd = rows_of((2 * pair + 1) * WIN)
        tails = rows_of(CELLS + pair * WIN)
        for u in range(WIN):
            moved = pltpu.roll(odd[u], 64, 1)
            joined = [
                even[u],
                jnp.where(lane < 64, tails[u], moved),
                jnp.where(lane < 64, moved, tails[u]),
            ]
            at = (u * WIN + 2 * pair) * 192
            packed_ref[:, at : at + 384] = jnp.concatenate(joined, 1).astype(BF16)
    leave.wait()


def last_steps(arrived, own, rows, side, corner, slots, width):
    return pl.pallas_call(
        last_kernel,
        out_shape=(jax.ShapeDtypeStruct(own.shape, BF16), jax.ShapeDtypeStruct((slots, width), BF16)),
        in_specs=[ANY, ANY] + [pl.BlockSpec(memory_space=pltpu.VMEM)] * 3,
        out_specs=(ANY, pl.BlockSpec(memory_space=pltpu.VMEM)),
        scratch_shapes=[
            pltpu.VMEM((arrived.shape[0], 1, 4, 128), BF16),
            pltpu.VMEM((slots,) + arrived.shape[1:], BF16),
        ]
        + [pltpu.VMEM(own.shape, BF16)] * 2
        + [pltpu.SemaphoreType.DMA((3,)), pltpu.SemaphoreType.DMA((slots,))],
        compiler_params=pltpu.CompilerParams(vmem_limit_bytes=LAST_BYTES),
        name="last_steps",
    )(arrived, own, rows, side, corner)


def moved(block, rows, cols):
    n_row, n_col = lax.axis_size("row"), lax.axis_size("col")
    route = [
        (r * n_col + c, (r + rows) % n_row * n_col + (c + cols) % n_col)
        for r in range(n_row)
        for c in range(n_col)
    ]
    return lax.ppermute(block, ("row", "col"), route)


def local(
    embedded,
    window_target_device,
    window_device_slot,
    cloud_mask_token,
    query_key_value_weight,
    projection_weight,
    up_weight,
    down_weight,
    bias_net_input_weight,
    bias_net_first_bias,
    bias_net_output_weight,
    temper,
    norm_gain_values,
):
    n_row, n_col = lax.axis_size("row"), lax.axis_size("col")
    n_heads, n_feat = temper.shape[1], cloud_mask_token.shape[0]
    slots = window_target_device.size // 2
    row, col = lax.axis_index("row"), lax.axis_index("col")
    place = jnp.stack([row, col, n_row - 1, n_col - 1]).astype(jnp.int32)
    consts = constants(n_heads, n_feat)
    params = (
        bias_net_input_weight,
        bias_net_first_bias,
        jnp.transpose(bias_net_output_weight, (2, 0, 1)),
        query_key_value_weight,
        projection_weight,
        up_weight,
        jnp.swapaxes(down_weight, 1, 2),
        norm_gain_values,
    )
    mid0, mid1, upper, left, send = first_layer(
        embedded, window_target_device, window_device_slot, temper, cloud_mask_token, consts, params,
        n_row * n_col,
    )
    pieces = (mid0, mid1, moved(upper, -1, 0), moved(left, 0, -1), moved(left, -1, -1))
    arrived = lax.all_to_all(send, ("row", "col"), split_axis=0, concat_axis=0, tiled=True)
    own, rows, side = second_layer(place, temper, pieces, consts, params)
    return last_steps(
        arrived, own, moved(rows, 1, 0), moved(side, 0, 1), moved(side, 1, 1), slots, CELLS * n_feat
    )


def solution(mesh):
    in_specs = (P("row", "col"),) * 3 + (P(),) * 10
    out_specs = (P("row", "col"), P(("row", "col"), None))
    return jax.shard_map(local, mesh=mesh, in_specs=in_specs, out_specs=out_specs, check_vma=False)
```

```python
import functools
import math

import jax
import jax.numpy as jnp
import numpy as np
from jax import lax
from jax.experimental import pallas as pl
from jax.experimental.pallas import tpu as pltpu
from jax.sharding import PartitionSpec as P

WIN = 8
HALF = WIN // 2
CELLS = WIN * WIN
LOG2E = math.log2(math.e)
F32 = jnp.float32
BF16 = jnp.bfloat16
VMEM_BYTES = 60 * 2**20
LAST_BYTES = 64 * 2**20 - 2**16
SMEM = pl.BlockSpec(memory_space=pltpu.SMEM)
ANY = pl.BlockSpec(memory_space=pl.ANY)


def log_step(offset):
    scaled = np.abs(offset).astype(np.float32) * np.float32(8.0 / (WIN - 1))
    return np.sign(offset) * np.log2(scaled + 1.0) / 3.0


def offset_coords():
    lane = np.arange(128)
    across = np.maximum(WIN - 1 - lane // WIN, 1 - WIN)
    down = np.concatenate([-(lane % WIN), np.minimum(WIN - lane % WIN, WIN - 1)])
    return np.stack([log_step(down), log_step(np.tile(across, 2))], 1).astype(np.float32)


def head_blocks(rows, row_block, cols, col_block):
    same = (np.arange(rows) // row_block)[:, None] == (np.arange(cols) // col_block)[None, :]
    return same.astype(np.float32)


def constants(n_heads, n_feat):
    per_head = n_feat // n_heads
    return (
        jnp.asarray(offset_coords(), F32),
        jnp.asarray(head_blocks(n_feat, per_head, n_feat, per_head), BF16),
        jnp.asarray(head_blocks(n_heads * CELLS, CELLS, n_feat, per_head), BF16),
        jnp.asarray(head_blocks(n_heads, 1, n_feat, per_head), BF16),
    )


def dot(a, b):
    return jnp.dot(a, b, preferred_element_type=F32)


def dot_nt(a, b):
    return lax.dot_general(a, b, (((1,), (1,)), ((), ())), preferred_element_type=F32)


def bias_strips(coords_ref, net_in, net_first, net_out, strips_ref):
    coords = coords_ref[...]
    units = jnp.maximum(
        coords[:, 0:1] * net_in[0:1, :] + coords[:, 1:2] * net_in[1:2, :] + net_first, 0.0
    )
    logits = lax.dot_general(
        net_out, units, (((1,), (1,)), ((), ())),
        precision=lax.Precision.HIGHEST, preferred_element_type=F32,
    )
    n_heads = logits.shape[0]
    logits = jnp.concatenate([logits, jnp.zeros((8 - n_heads, 256), F32)], 0)
    table = 16.0 * LOG2E / (1.0 + jnp.exp(-logits))
    before, after = table[:, :128], table[:, 128:]
    cell = lax.broadcasted_iota(jnp.int32, (8, 128), 1) % WIN
    for u in range(WIN):
        strip = jnp.where(
            cell >= u,
            pltpu.roll(before, u, 1) if u else before,
            pltpu.roll(after, (u - WIN) % 128, 1),
        )
        strips_ref[:, u, :] = strip


def turned(strip):
    cell = lax.broadcasted_iota(jnp.int32, (WIN, 128), 1) % WIN
    strip = pltpu.roll(strip, HALF, 0)
    return jnp.where(cell < HALF, pltpu.roll(strip, 128 - HALF, 1), pltpu.roll(strip, HALF, 1))


def bias_rows(strips, w):
    lane = lax.broadcasted_iota(jnp.int32, (WIN, 128), 1)
    back = (WIN - 1 - w) * WIN
    parts = []
    for pair in range(len(strips) // 2):
        low = pltpu.roll(strips[2 * pair], (128 - back) % 128, 1)
        high = pltpu.roll(strips[2 * pair + 1], (192 - back) % 128, 1)
        parts.append(jnp.where(lane < CELLS, low, high))
    return jnp.concatenate(parts, 1)


def layer_norm(values, gain_row):
    row_mean = jnp.mean(values, -1, keepdims=True)
    centred = values - row_mean
    spread = jnp.mean(centred * centred, -1, keepdims=True)
    return centred * lax.rsqrt(spread + 1e-05) * gain_row


def unit_vectors(t, heads_ref):
    t = t.astype(BF16).astype(F32)
    squares = dot((t * t).astype(BF16), heads_ref[...])
    return t * lax.rsqrt(squares + 1e-06)


def temper_row(temper, layer, mask_ref):
    row = jnp.zeros((1, mask_ref.shape[1]), F32)
    for h in range(mask_ref.shape[0]):
        row = row + (temper[layer, h] * LOG2E) * mask_ref[h : h + 1, :].astype(F32)
    return row


def spread_heads(t, mask_ref):
    low = [t[:, :128] * mask_ref[h : h + 1, :128] for h in range(4)]
    high = [t[:, 128:] * mask_ref[h : h + 1, 128:] for h in range(4, 6)]
    return jnp.concatenate(low, 0), jnp.concatenate(high, 0)


def scores_of(q, k, mask_ref):
    low, high = spread_heads(k, mask_ref)
    return jnp.concatenate([dot_nt(q[:, :128], low), dot_nt(q[:, 128:], high)], 1)


def weighted(p, low, high):
    return jnp.concatenate([dot(p[:, :256], low), dot(p[:, 256:], high)], 1)


def totals_of(p, ones_ref):
    return weighted(p, ones_ref[:256, :128], ones_ref[256:, 128:])


def dense_tail(x, mixed, proj_ref, up_ref, down_ref, gain_ref):
    attended = dot(mixed.astype(BF16), proj_ref[...])
    hidden = (x + layer_norm(attended, gain_ref[0:1, :])).astype(BF16)
    raised = dot(hidden, up_ref[...])
    expanded = (0.5 * raised * (1.0 + lax.erf(raised * math.sqrt(0.5)))).astype(BF16)
    reduced = dot_nt(expanded, down_ref[...])
    return (hidden.astype(F32) + layer_norm(reduced, gain_ref[1:2, :])).astype(BF16)


def attend(x, q_w, k_w, v_w, temper, heads_ref, ones_ref, mask_ref, bias_of, p_ref):
    n_windows = x.shape[0] // CELLS
    q = (unit_vectors(dot(x, q_w[...]), heads_ref) * temper).astype(BF16)
    k = unit_vectors(dot(x, k_w[...]), heads_ref).astype(BF16)
    v = dot(x, v_w[...]).astype(BF16)
    mixed = []
    for n in range(n_windows):
        rows = slice(n * CELLS, (n + 1) * CELLS)
        p_ref[rows, :] = jnp.exp2(scores_of(q[rows], k[rows], mask_ref) + bias_of(n)).astype(BF16)
    for n in range(n_windows):
        rows = slice(n * CELLS, (n + 1) * CELLS)
        mixed.append(weighted(p_ref[rows, :], *spread_heads(v[rows], mask_ref)))
    return jnp.concatenate(mixed, 0) / totals_of(p_ref[...], ones_ref)


def split_weights(qkv_ref, q_w, k_w, v_w):
    n_feat = q_w.shape[0]
    q_w[...] = qkv_ref[:, :n_feat]
    k_w[...] = qkv_ref[:, n_feat : 2 * n_feat]
    v_w[...] = qkv_ref[:, 2 * n_feat :]


def half_rows(tile):
    first = lax.broadcasted_iota(jnp.int32, (WIN, tile.shape[1]), 0) < HALF
    pairs = []
    for pair in range(2):
        even = tile[2 * pair * WIN : (2 * pair + 1) * WIN]
        odd = tile[(2 * pair + 1) * WIN : (2 * pair + 2) * WIN]
        pairs.append(jnp.where(first, even, pltpu.roll(odd, HALF, 0)))
    return jnp.concatenate(pairs, 0)


def whole_rows(halves):
    tiles = []
    for pair in range(2):
        rows = halves[pair * WIN : (pair + 1) * WIN]
        tiles += [rows, pltpu.roll(rows, HALF, 0)]
    return jnp.concatenate(tiles, 0)


def first_kernel(
    groups,
    targets, slots, temper, emb_ref, token_ref, coords_ref, heads_ref, ones_ref, mask_ref,
    net_in, net_first, net_out, qkv_ref, proj_ref, up_ref, down_ref, gain_ref,
    mid0_ref, mid1_ref, upper_ref, left_ref, send_ref,
    bias_ref, strips_ref, q_w, k_w, v_w, p_ref, staging, blank, sems, blank_sem,
):
    step = pl.program_id(0)
    n_heads, n_feat = mask_ref.shape

    no_slots = pltpu.make_async_copy(blank, send_ref.at[:, pl.ds(24, 1)], blank_sem)

    @pl.when(step == 0)
    def _():
        blank[...] = jnp.full(blank.shape, -1.0, BF16)
        no_slots.start()
        bias_strips(coords_ref, net_in, net_first[0:1, :], net_out[:, 0, :], strips_ref)
        strips = [strips_ref[h] for h in range(n_heads)]
        for w in range(WIN):
            bias_ref[w * WIN : (w + 1) * WIN, :] = bias_rows(strips, w)
        split_weights(qkv_ref, q_w, k_w, v_w)

    tiles = []
    for group in range(groups):
        slabs = []
        for w in range(WIN):
            at = (group * WIN + w) * n_feat
            slabs.append(emb_ref[:, at : at + n_feat].astype(F32))
        for i in range(2):
            tiles.append(jnp.concatenate([s[i * WIN : (i + 1) * WIN] for s in slabs], 0))
    x = jnp.concatenate(tiles, 0)
    mixed = attend(
        x.astype(BF16), q_w, k_w, v_w, temper_row(temper, 0, mask_ref), heads_ref, ones_ref, mask_ref,
        lambda n: bias_ref[...], p_ref,
    )

    @pl.when(step == 0)
    def _():
        no_slots.wait()

    y = jnp.concatenate(
        [
            dense_tail(x[n : n + 512], mixed[n : n + 512], proj_ref, up_ref, down_ref, gain_ref)
            for n in range(0, x.shape[0], 512)
        ],
        0,
    ).astype(F32)

    token = token_ref[...].astype(F32).reshape(1, n_feat)
    for group in range(groups):
        for i in range(2):
            n = 2 * group + i
            j = step * groups + group
            target = targets[i, j]
            tile = y[n * CELLS : (n + 1) * CELLS]
            kept = jnp.where(target >= 0, tile, token)
            rows = kept.astype(BF16)
            mid = (mid0_ref, mid1_ref)[i]
            mid[2 * group] = rows[:32]
            mid[2 * group + 1] = rows[32:]
            if i == 0:
                halves = [half_rows(kept[half * 32 : (half + 1) * 32]).astype(BF16) for half in range(2)]
                upper_ref[2 * group] = halves[0]
                upper_ref[2 * group + 1] = halves[1]
            if group == 0:

                @pl.when(step == 0)
                def _(i=i, rows=rows, halves=halves):
                    left_ref[i * 32 : (i + 1) * 32] = rows[:32]
                    if i == 0:
                        left_ref[64:] = halves[0]

            slot = j * 2 + i
            staging[slot, :16] = tile[:, :128].reshape(16, 4, 128).astype(BF16)
            tails = tile[:, 128:].reshape(4, 2, WIN, 64)
            joined = jnp.concatenate([tails[:, 0], tails[:, 1]], -1)
            staging[slot, 16:24] = joined.reshape(8, 4, 128).astype(BF16)
            staging[slot, 24:] = jnp.full((1, 4, 128), slots[i, j].astype(F32)).astype(BF16)

            @pl.when(target >= 0)
            def _(slot=slot, target=target):
                pltpu.make_async_copy(staging.at[slot], send_ref.at[target], sems.at[slot]).start()

    @pl.when(step == pl.num_programs(0) - 1)
    def _():
        def finish(slot, carry):
            target = targets[lax.rem(slot, 2), slot // 2]

            @pl.when(target >= 0)
            def _():
                pltpu.make_async_copy(staging.at[slot], send_ref.at[target], sems.at[slot]).wait()

            return carry

        lax.fori_loop(0, staging.shape[0], finish, 0)


def whole(array):
    zeros = (0,) * array.ndim
    return pl.BlockSpec(array.shape, lambda *_: zeros)


def layer_spec(array, position, layer):
    if position in (1, 2):
        return whole(array)
    rest = array.shape[1:]
    at = (layer,) + (0,) * len(rest)
    return pl.BlockSpec((None,) + rest, lambda *_: at)


def layer_scratch(n_heads, n_feat):
    square = pltpu.VMEM((n_feat, n_feat), BF16)
    return [pltpu.VMEM((8, WIN, 128), F32), square, square, square]


def first_layer(embedded, targets, slots, temper, token, consts, params, devices, groups=16):
    n_heads, n_feat = consts[3].shape
    columns = embedded.shape[1] // (WIN * n_feat)
    side = jax.ShapeDtypeStruct((80, n_feat), BF16)
    upper = jax.ShapeDtypeStruct((2 * columns, 16, n_feat), BF16)
    mid = jax.ShapeDtypeStruct((2 * columns, 32, n_feat), BF16)
    mid_spec = pl.BlockSpec((2 * groups, 32, n_feat), lambda g: (g, 0, 0))
    return pl.pallas_call(
        functools.partial(first_kernel, groups),
        grid=(columns // groups,),
        out_shape=(mid, mid, upper, side, jax.ShapeDtypeStruct((devices, 25, 4, 128), BF16)),
        in_specs=[SMEM, SMEM, SMEM, pl.BlockSpec((2 * WIN, groups * WIN * n_feat), lambda g: (0, g))]
        + [whole(a) for a in (token,) + consts]
        + [layer_spec(a, n, 0) for n, a in enumerate(params)],
        out_specs=(mid_spec, mid_spec, pl.BlockSpec((2 * groups, 16, n_feat), lambda g: (g, 0, 0)), whole(side), ANY),
        scratch_shapes=[pltpu.VMEM((CELLS, n_heads * CELLS), F32)]
        + layer_scratch(n_heads, n_feat)
        + [
            pltpu.VMEM((groups * 2 * CELLS, n_heads * CELLS), BF16),
            pltpu.VMEM((2 * columns, 25, 4, 128), BF16),
            pltpu.VMEM((devices, 1, 4, 128), BF16),
            pltpu.SemaphoreType.DMA((2 * columns,)),
            pltpu.SemaphoreType.DMA,
        ],
        compiler_params=pltpu.CompilerParams(vmem_limit_bytes=VMEM_BYTES),
        cost_estimate=pl.CostEstimate(flops=2 * 10**9, bytes_accessed=6 * 10**6, transcendentals=10**6),
        name="first_layer",
    )(targets, slots, temper, embedded, token, *consts, *params)


def second_kernel(
    groups,
    place, temper, mid0_ref, mid1_ref, below_ref, right_ref, corner_ref,
    coords_ref, heads_ref, ones_ref, mask_ref,
    net_in, net_first, net_out, qkv_ref, proj_ref, up_ref, down_ref, gain_ref,
    out_ref, rows_ref, side_ref,
    bias_ref, strips_ref, q_w, k_w, v_w, ext, ring, p_ref, sems,
):
    step = pl.program_id(0)
    n_heads, n_feat = mask_ref.shape
    n_half = mid0_ref.shape[0]
    row, col, last_row, last_col = place[0], place[1], place[2], place[3]
    width = HALF * n_feat

    @pl.when(step == 0)
    def _():
        own = pl.ds(0, n_half)
        copies = [
            pltpu.make_async_copy(src, dst, sems.at[n])
            for n, (src, dst) in enumerate(
                [
                    (mid0_ref, ext.at[0, own]),
                    (mid1_ref, ext.at[1, own]),
                    (right_ref.at[pl.ds(0, 32)], ext.at[0, n_half]),
                    (right_ref.at[pl.ds(32, 32)], ext.at[1, n_half]),
                    (below_ref, ring.at[own]),
                    (corner_ref.at[pl.ds(64, 16)], ring.at[n_half]),
                ]
            )
        ]
        for copy in copies:
            copy.start()
        out_ref[:, :width] = jnp.zeros((2 * WIN, width), BF16)
        split_weights(qkv_ref, q_w, k_w, v_w)
        bias_strips(coords_ref, net_in, net_first[1:2, :], net_out[:, 1, :], strips_ref)
        strips = [turned(strips_ref[h]) for h in range(n_heads)]
        lane = lax.broadcasted_iota(jnp.int32, (WIN, n_heads * CELLS), 1)
        upper = lax.broadcasted_iota(jnp.int32, (WIN, n_heads * CELLS), 0) < HALF
        other_rows = upper != (lane % WIN < HALF)
        for w in range(WIN):
            other_cols = (lane % CELLS >= CELLS // 2) != (w >= HALF)
            rows = slice(w * WIN, (w + 1) * WIN)
            bias = bias_rows(strips, w)
            away = -100.0 * LOG2E
            bias_ref[0, rows, :] = bias
            bias_ref[1, rows, :] = bias + jnp.where(other_cols, away, 0.0)
            bias_ref[2, rows, :] = bias + jnp.where(other_rows, away, 0.0)
            bias_ref[3, rows, :] = bias + jnp.where(other_rows | other_cols, away, 0.0)
        for copy in copies:
            copy.wait()

    upper = lax.broadcasted_iota(jnp.int32, (CELLS, n_feat), 0) % WIN < HALF
    tiles = []
    for group in range(groups):
        at = 2 * (step * groups + group) + 1
        zero = jnp.concatenate([ext[0, at], ext[0, at + 1]], 0)
        one = jnp.concatenate([ext[1, at], ext[1, at + 1]], 0)
        two = jnp.concatenate([whole_rows(ring[at + half].astype(F32)) for half in range(2)], 0)
        tiles += [jnp.where(upper, one, zero), jnp.where(upper, two.astype(BF16), one)]
    x = jnp.concatenate(tiles, 0)
    low_cut = (row == last_row).astype(jnp.int32)

    def bias_of(n):
        column = step * groups + n // 2
        cut = ((col == last_col) & (column == n_half // 2 - 1)).astype(jnp.int32)
        return bias_ref[cut + 2 * low_cut * (n % 2)]

    mixed = attend(
        x, q_w, k_w, v_w, temper_row(temper, 1, mask_ref), heads_ref, ones_ref, mask_ref, bias_of, p_ref
    )
    y = dense_tail(x.astype(F32), mixed, proj_ref, up_ref, down_ref, gain_ref).astype(F32)

    for group in range(groups):
        first = y[2 * group * CELLS : (2 * group + 1) * CELLS]
        second = y[(2 * group + 1) * CELLS : (2 * group + 2) * CELLS]
        zero = jnp.where(upper, second, first)
        one = jnp.where(upper, first, second)
        for half in range(2):
            slabs = []
            for w in range(half * HALF, (half + 1) * HALF):
                rows = slice(w * WIN, (w + 1) * WIN)
                slabs.append(jnp.concatenate([zero[rows], one[rows]], 0))
            strip = jnp.concatenate(slabs, 1).astype(BF16)
            at = 2 * (step * groups + group) + 1 + half
            if half == 0 or group < groups - 1:
                out_ref[:, pl.ds(pl.multiple_of(at * width, 128), width)] = strip
            else:

                @pl.when(at < n_half)
                def _(at=at, strip=strip):
                    out_ref[:, pl.ds(pl.multiple_of(at * width, 128), width)] = strip

                @pl.when(at == n_half)
                def _(strip=strip):
                    side_ref[...] = strip

    @pl.when(step == pl.num_programs(0) - 1)
    def _():
        quarter = rows_ref.shape[1]
        first = lax.broadcasted_iota(jnp.int32, (WIN, quarter), 0) < HALF
        tops = [out_ref[:, n * quarter : (n + 1) * quarter][:WIN].astype(F32) for n in range(4)]
        pairs = [
            jnp.where(first, tops[2 * n], pltpu.roll(tops[2 * n + 1], HALF, 0)) for n in range(2)
        ]
        rows_ref[...] = jnp.concatenate(pairs, 0).astype(BF16)


def second_layer(place, temper, pieces, consts, params, groups=8):
    n_heads, n_feat = consts[3].shape
    n_half = pieces[0].shape[0]
    out = jax.ShapeDtypeStruct((2 * WIN, n_half * HALF * n_feat), BF16)
    rows = jax.ShapeDtypeStruct((2 * WIN, n_half * n_feat), BF16)
    side = jax.ShapeDtypeStruct((2 * WIN, HALF * n_feat), BF16)
    return pl.pallas_call(
        functools.partial(second_kernel, groups),
        grid=(n_half // 2 // groups,),
        out_shape=(out, rows, side),
        in_specs=[SMEM, SMEM]
        + [ANY] * len(pieces)
        + [whole(a) for a in consts]
        + [layer_spec(a, n, 1) for n, a in enumerate(params)],
        out_specs=(whole(out), whole(rows), whole(side)),
        scratch_shapes=[pltpu.VMEM((4, CELLS, n_heads * CELLS), F32)]
        + layer_scratch(n_heads, n_feat)
        + [
            pltpu.VMEM((2, n_half + 1, 32, n_feat), BF16),
            pltpu.VMEM((n_half + 1, 16, n_feat), BF16),
            pltpu.VMEM((groups * 2 * CELLS, n_heads * CELLS), BF16),
            pltpu.SemaphoreType.DMA((6,)),
        ],
        compiler_params=pltpu.CompilerParams(vmem_limit_bytes=VMEM_BYTES),
        cost_estimate=pl.CostEstimate(flops=10**11, bytes_accessed=10**7, transcendentals=10**6),
        name="second_layer",
    )(place, temper, *pieces, *consts, *params)


def merge_features(own_ref, rows_ref, side_ref, corner_ref, out_ref):
    quarter, width = rows_ref.shape[1], side_ref.shape[1]
    first = lax.broadcasted_iota(jnp.int32, (WIN, quarter), 0) < HALF
    for n in range(4):
        lanes = slice(n * quarter, (n + 1) * quarter)
        own = own_ref[:, lanes].astype(F32)
        top = rows_ref[...].astype(F32)[n // 2 * WIN : (n // 2 + 1) * WIN]
        top = pltpu.roll(top, HALF, 0) if n % 2 else top
        merged = jnp.concatenate([jnp.where(first, top, own[:WIN]), own[WIN:]], 0)
        out_ref[:, lanes] = merged.astype(BF16)
    corner = lax.broadcasted_iota(jnp.int32, (2 * WIN, width), 0) < HALF
    merged = jnp.where(corner, corner_ref[...].astype(F32), side_ref[...].astype(F32))
    out_ref[:, :width] = merged.astype(BF16)


def last_kernel(
    entries_ref, own_hbm, rows_hbm, side_hbm, corner_hbm, features_hbm, packed_ref,
    marks_ref, held, own_ref, features_ref, rows_ref, side_ref, corner_ref, sems, slot_sems,
):
    slots = packed_ref.shape[0]
    marks_copy = pltpu.make_async_copy(entries_ref.at[:, pl.ds(24, 1)], marks_ref, sems.at[0])
    own_copy = pltpu.make_async_copy(own_hbm, own_ref, sems.at[1])
    marks_copy.start()
    own_copy.start()
    halos = [
        pltpu.make_async_copy(src, dst, sems.at[3 + n])
        for n, (src, dst) in enumerate(
            [(rows_hbm, rows_ref), (side_hbm, side_ref), (corner_hbm, corner_ref)]
        )
    ]
    for copy in halos:
        copy.start()
    marks_copy.wait()
    marks = marks_ref[...][:, 0].astype(F32)
    lane = lax.broadcasted_iota(jnp.int32, marks.shape, 2).astype(F32)
    sender = lax.broadcasted_iota(jnp.int32, marks.shape, 0).astype(F32)
    found = jnp.max(jnp.where(marks == lane, sender, 0.0), 0).astype(jnp.int32)
    windows = [
        pltpu.make_async_copy(entries_ref.at[found[0, slot]], held.at[slot], slot_sems.at[slot])
        for slot in range(slots)
    ]
    for copy in windows:
        copy.start()
    own_copy.wait()
    for copy in halos:
        copy.wait()
    merge_features(own_ref, rows_ref, side_ref, corner_ref, features_ref)
    leave = pltpu.make_async_copy(features_ref, features_hbm, sems.at[2])
    leave.start()
    for copy in windows:
        copy.wait()
    lane = lax.broadcasted_iota(jnp.int32, (slots, 128), 1)

    def rows_of(at):
        rows = held[:, at // 4 : at // 4 + 2].astype(F32).reshape(slots, WIN, 128)
        return jnp.swapaxes(rows, 0, 1)

    for pair in range(WIN // 2):
        even = rows_of(2 * pair * WIN)
        odd = rows_of((2 * pair + 1) * WIN)
        tails = rows_of(CELLS + pair * WIN)
        for u in range(WIN):
            moved = pltpu.roll(odd[u], 64, 1)
            joined = [
                even[u],
                jnp.where(lane < 64, tails[u], moved),
                jnp.where(lane < 64, moved, tails[u]),
            ]
            at = (u * WIN + 2 * pair) * 192
            packed_ref[:, at : at + 384] = jnp.concatenate(joined, 1).astype(BF16)
    leave.wait()


def last_steps(arrived, own, rows, side, corner, slots, width):
    return pl.pallas_call(
        last_kernel,
        out_shape=(jax.ShapeDtypeStruct(own.shape, BF16), jax.ShapeDtypeStruct((slots, width), BF16)),
        in_specs=[ANY] * 5,
        out_specs=(ANY, pl.BlockSpec(memory_space=pltpu.VMEM)),
        scratch_shapes=[
            pltpu.VMEM((arrived.shape[0], 1, 4, 128), BF16),
            pltpu.VMEM((slots,) + arrived.shape[1:], BF16),
        ]
        + [pltpu.VMEM(own.shape, BF16)] * 2
        + [pltpu.VMEM(a.shape, BF16) for a in (rows, side, corner)]
        + [pltpu.SemaphoreType.DMA((6,)), pltpu.SemaphoreType.DMA((slots,))],
        compiler_params=pltpu.CompilerParams(vmem_limit_bytes=LAST_BYTES),
        name="last_steps",
    )(arrived, own, rows, side, corner)


def moved(block, rows, cols):
    n_row, n_col = lax.axis_size("row"), lax.axis_size("col")
    route = [
        (r * n_col + c, (r + rows) % n_row * n_col + (c + cols) % n_col)
        for r in range(n_row)
        for c in range(n_col)
    ]
    return lax.ppermute(block, ("row", "col"), route)


def local(
    embedded,
    window_target_device,
    window_device_slot,
    cloud_mask_token,
    query_key_value_weight,
    projection_weight,
    up_weight,
    down_weight,
    bias_net_input_weight,
    bias_net_first_bias,
    bias_net_output_weight,
    temper,
    norm_gain_values,
):
    n_row, n_col = lax.axis_size("row"), lax.axis_size("col")
    n_heads, n_feat = temper.shape[1], cloud_mask_token.shape[0]
    slots = window_target_device.size // 2
    row, col = lax.axis_index("row"), lax.axis_index("col")
    place = jnp.stack([row, col, n_row - 1, n_col - 1]).astype(jnp.int32)
    consts = constants(n_heads, n_feat)
    params = (
        bias_net_input_weight,
        bias_net_first_bias,
        jnp.transpose(bias_net_output_weight, (2, 0, 1)),
        query_key_value_weight,
        projection_weight,
        up_weight,
        jnp.swapaxes(down_weight, 1, 2),
        norm_gain_values,
    )
    mid0, mid1, upper, left, send = first_layer(
        embedded, window_target_device, window_device_slot, temper, cloud_mask_token, consts, params,
        n_row * n_col,
    )
    pieces = (mid0, mid1, moved(upper, -1, 0), moved(left, 0, -1), moved(left, -1, -1))
    arrived = lax.all_to_all(send, ("row", "col"), split_axis=0, concat_axis=0, tiled=True)
    own, rows, side = second_layer(place, temper, pieces, consts, params)
    return last_steps(
        arrived, own, moved(rows, 1, 0), moved(side, 0, 1), moved(side, 1, 1), slots, CELLS * n_feat
    )


def solution(mesh):
    in_specs = (P("row", "col"),) * 3 + (P(),) * 10
    out_specs = (P("row", "col"), P(("row", "col"), None))
    return jax.shard_map(local, mesh=mesh, in_specs=in_specs, out_specs=out_specs, check_vma=False)
```

```python
import functools
import math

import jax
import jax.numpy as jnp
import numpy as np
from jax import lax
from jax.experimental import pallas as pl
from jax.experimental.pallas import tpu as pltpu
from jax.sharding import PartitionSpec as P

WIN = 8
HALF = WIN // 2
CELLS = WIN * WIN
LOG2E = math.log2(math.e)
F32 = jnp.float32
BF16 = jnp.bfloat16
VMEM_BYTES = 60 * 2**20
LAST_BYTES = 64 * 2**20 - 2**16
SMEM = pl.BlockSpec(memory_space=pltpu.SMEM)
ANY = pl.BlockSpec(memory_space=pl.ANY)


def log_step(offset):
    scaled = np.abs(offset).astype(np.float32) * np.float32(8.0 / (WIN - 1))
    return np.sign(offset) * np.log2(scaled + 1.0) / 3.0


def offset_coords():
    lane = np.arange(128)
    across = np.maximum(WIN - 1 - lane // WIN, 1 - WIN)
    down = np.concatenate([-(lane % WIN), np.minimum(WIN - lane % WIN, WIN - 1)])
    return np.stack([log_step(down), log_step(np.tile(across, 2))], 1).astype(np.float32)


def head_blocks(rows, row_block, cols, col_block):
    same = (np.arange(rows) // row_block)[:, None] == (np.arange(cols) // col_block)[None, :]
    return same.astype(np.float32)


def constants(n_heads, n_feat):
    per_head = n_feat // n_heads
    return (
        jnp.asarray(offset_coords(), F32),
        jnp.asarray(head_blocks(n_feat, per_head, n_feat, per_head), BF16),
        jnp.asarray(head_blocks(n_heads * CELLS, CELLS, n_feat, per_head), BF16),
        jnp.asarray(head_blocks(n_heads, 1, n_feat, per_head), BF16),
    )


def dot(a, b):
    return jnp.dot(a, b, preferred_element_type=F32)


def dot_nt(a, b):
    return lax.dot_general(a, b, (((1,), (1,)), ((), ())), preferred_element_type=F32)


def bias_strips(coords_ref, net_in, net_first, net_out, strips_ref):
    coords = coords_ref[...]
    units = jnp.maximum(
        coords[:, 0:1] * net_in[0:1, :] + coords[:, 1:2] * net_in[1:2, :] + net_first, 0.0
    )
    logits = lax.dot_general(
        net_out, units, (((1,), (1,)), ((), ())),
        precision=lax.Precision.HIGHEST, preferred_element_type=F32,
    )
    n_heads = logits.shape[0]
    logits = jnp.concatenate([logits, jnp.zeros((8 - n_heads, 256), F32)], 0)
    table = 16.0 * LOG2E / (1.0 + jnp.exp(-logits))
    before, after = table[:, :128], table[:, 128:]
    cell = lax.broadcasted_iota(jnp.int32, (8, 128), 1) % WIN
    for u in range(WIN):
        strip = jnp.where(
            cell >= u,
            pltpu.roll(before, u, 1) if u else before,
            pltpu.roll(after, (u - WIN) % 128, 1),
        )
        strips_ref[:, u, :] = strip


def turned(strip):
    cell = lax.broadcasted_iota(jnp.int32, (WIN, 128), 1) % WIN
    strip = pltpu.roll(strip, HALF, 0)
    return jnp.where(cell < HALF, pltpu.roll(strip, 128 - HALF, 1), pltpu.roll(strip, HALF, 1))


def bias_rows(strips, w):
    lane = lax.broadcasted_iota(jnp.int32, (WIN, 128), 1)
    back = (WIN - 1 - w) * WIN
    parts = []
    for pair in range(len(strips) // 2):
        low = pltpu.roll(strips[2 * pair], (128 - back) % 128, 1)
        high = pltpu.roll(strips[2 * pair + 1], (192 - back) % 128, 1)
        parts.append(jnp.where(lane < CELLS, low, high))
    return jnp.concatenate(parts, 1)


def layer_norm(values, gain_row):
    row_mean = jnp.mean(values, -1, keepdims=True)
    centred = values - row_mean
    spread = jnp.mean(centred * centred, -1, keepdims=True)
    return centred * lax.rsqrt(spread + 1e-05) * gain_row


def unit_vectors(t, heads_ref):
    t = t.astype(BF16).astype(F32)
    squares = dot((t * t).astype(BF16), heads_ref[...])
    return t * lax.rsqrt(squares + 1e-06)


def temper_row(temper, layer, mask_ref):
    row = jnp.zeros((1, mask_ref.shape[1]), F32)
    for h in range(mask_ref.shape[0]):
        row = row + (temper[layer, h] * LOG2E) * mask_ref[h : h + 1, :].astype(F32)
    return row


def spread_heads(t, mask_ref):
    low = [t[:, :128] * mask_ref[h : h + 1, :128] for h in range(4)]
    high = [t[:, 128:] * mask_ref[h : h + 1, 128:] for h in range(4, 6)]
    return jnp.concatenate(low, 0), jnp.concatenate(high, 0)


def scores_of(q, k, mask_ref):
    low, high = spread_heads(k, mask_ref)
    return jnp.concatenate([dot_nt(q[:, :128], low), dot_nt(q[:, 128:], high)], 1)


def weighted(p, low, high):
    return jnp.concatenate([dot(p[:, :256], low), dot(p[:, 256:], high)], 1)


def totals_of(p, ones_ref):
    return weighted(p, ones_ref[:256, :128], ones_ref[256:, 128:])


def dense_tail(x, mixed, proj_ref, up_ref, down_ref, gain_ref):
    attended = dot(mixed.astype(BF16), proj_ref[...])
    hidden = (x + layer_norm(attended, gain_ref[0:1, :])).astype(BF16)
    raised = dot(hidden, up_ref[...])
    expanded = (0.5 * raised * (1.0 + lax.erf(raised * math.sqrt(0.5)))).astype(BF16)
    reduced = dot_nt(expanded, down_ref[...])
    return (hidden.astype(F32) + layer_norm(reduced, gain_ref[1:2, :])).astype(BF16)


def attend(x, q_w, k_w, v_w, temper, heads_ref, ones_ref, mask_ref, bias_of, p_ref):
    n_windows = x.shape[0] // CELLS
    q = (unit_vectors(dot(x, q_w[...]), heads_ref) * temper).astype(BF16)
    k = unit_vectors(dot(x, k_w[...]), heads_ref).astype(BF16)
    v = dot(x, v_w[...]).astype(BF16)
    mixed = []
    for n in range(n_windows):
        rows = slice(n * CELLS, (n + 1) * CELLS)
        p_ref[rows, :] = jnp.exp2(scores_of(q[rows], k[rows], mask_ref) + bias_of(n)).astype(BF16)
    for n in range(n_windows):
        rows = slice(n * CELLS, (n + 1) * CELLS)
        mixed.append(weighted(p_ref[rows, :], *spread_heads(v[rows], mask_ref)))
    return jnp.concatenate(mixed, 0) / totals_of(p_ref[...], ones_ref)


def split_weights(qkv_ref, q_w, k_w, v_w):
    n_feat = q_w.shape[0]
    q_w[...] = qkv_ref[:, :n_feat]
    k_w[...] = qkv_ref[:, n_feat : 2 * n_feat]
    v_w[...] = qkv_ref[:, 2 * n_feat :]


def half_rows(tile):
    first = lax.broadcasted_iota(jnp.int32, (WIN, tile.shape[1]), 0) < HALF
    pairs = []
    for pair in range(2):
        even = tile[2 * pair * WIN : (2 * pair + 1) * WIN]
        odd = tile[(2 * pair + 1) * WIN : (2 * pair + 2) * WIN]
        pairs.append(jnp.where(first, even, pltpu.roll(odd, HALF, 0)))
    tails = jnp.concatenate([pair[:, 128:] for pair in pairs], 1)
    return jnp.concatenate([pair[:, :128] for pair in pairs] + [tails], 0)


def whole_rows(halves):
    tiles = []
    for pair in range(2):
        tails = halves[2 * WIN :, pair * 64 : (pair + 1) * 64]
        rows = jnp.concatenate([halves[pair * WIN : (pair + 1) * WIN], tails], 1)
        tiles += [rows, pltpu.roll(rows, HALF, 0)]
    return jnp.concatenate(tiles, 0)


def first_kernel(
    groups,
    targets, slots, temper, emb_ref, token_ref, coords_ref, heads_ref, ones_ref, mask_ref,
    net_in, net_first, net_out, qkv_ref, proj_ref, up_ref, down_ref, gain_ref,
    mid0_ref, mid1_ref, upper_ref, left_ref, corner_ref, send_ref,
    bias_ref, strips_ref, q_w, k_w, v_w, p_ref, staging, blank, sems, blank_sem,
):
    step = pl.program_id(0)
    n_heads, n_feat = mask_ref.shape

    no_slots = pltpu.make_async_copy(blank, send_ref.at[:, pl.ds(24, 1)], blank_sem)

    @pl.when(step == 0)
    def _():
        blank[...] = jnp.full(blank.shape, -1.0, BF16)
        no_slots.start()
        bias_strips(coords_ref, net_in, net_first[0:1, :], net_out[:, 0, :], strips_ref)
        strips = [strips_ref[h] for h in range(n_heads)]
        for w in range(WIN):
            bias_ref[w * WIN : (w + 1) * WIN, :] = bias_rows(strips, w)
        split_weights(qkv_ref, q_w, k_w, v_w)

    tiles = []
    for group in range(groups):
        slabs = []
        for w in range(WIN):
            at = (group * WIN + w) * n_feat
            slabs.append(emb_ref[:, at : at + n_feat].astype(F32))
        for i in range(2):
            tiles.append(jnp.concatenate([s[i * WIN : (i + 1) * WIN] for s in slabs], 0))
    x = jnp.concatenate(tiles, 0)
    mixed = attend(
        x.astype(BF16), q_w, k_w, v_w, temper_row(temper, 0, mask_ref), heads_ref, ones_ref, mask_ref,
        lambda n: bias_ref[...], p_ref,
    )

    @pl.when(step == 0)
    def _():
        no_slots.wait()

    y = jnp.concatenate(
        [
            dense_tail(x[n : n + 512], mixed[n : n + 512], proj_ref, up_ref, down_ref, gain_ref)
            for n in range(0, x.shape[0], 512)
        ],
        0,
    ).astype(F32)

    token = token_ref[...].astype(F32).reshape(1, n_feat)
    for group in range(groups):
        for i in range(2):
            n = 2 * group + i
            j = step * groups + group
            target = targets[i, j]
            tile = y[n * CELLS : (n + 1) * CELLS]
            kept = jnp.where(target >= 0, tile, token)
            rows = kept.astype(BF16)
            mid = (mid0_ref, mid1_ref)[i]
            mid[2 * group] = rows[:32]
            mid[2 * group + 1] = rows[32:]
            if i == 0:
                halves = [half_rows(kept[half * 32 : (half + 1) * 32]).astype(BF16) for half in range(2)]
                upper_ref[2 * group] = halves[0]
                upper_ref[2 * group + 1] = halves[1]
            if group == 0:

                @pl.when(step == 0)
                def _(i=i, rows=rows, halves=halves):
                    left_ref[i * 32 : (i + 1) * 32] = rows[:32]
                    if i == 0:
                        corner_ref[...] = halves[0]

            slot = j * 2 + i
            staging[slot, :16] = tile[:, :128].reshape(16, 4, 128).astype(BF16)
            tails = tile[:, 128:].reshape(4, 2, WIN, 64)
            joined = jnp.concatenate([tails[:, 0], tails[:, 1]], -1)
            staging[slot, 16:24] = joined.reshape(8, 4, 128).astype(BF16)
            staging[slot, 24:] = jnp.full((1, 4, 128), slots[i, j].astype(F32)).astype(BF16)

            @pl.when(target >= 0)
            def _(slot=slot, target=target):
                pltpu.make_async_copy(staging.at[slot], send_ref.at[target], sems.at[slot]).start()

    @pl.when(step == pl.num_programs(0) - 1)
    def _():
        def finish(slot, carry):
            target = targets[lax.rem(slot, 2), slot // 2]

            @pl.when(target >= 0)
            def _():
                pltpu.make_async_copy(staging.at[slot], send_ref.at[target], sems.at[slot]).wait()

            return carry

        lax.fori_loop(0, staging.shape[0], finish, 0)


def whole(array):
    zeros = (0,) * array.ndim
    return pl.BlockSpec(array.shape, lambda *_: zeros)


def layer_spec(array, position, layer):
    if position in (1, 2):
        return whole(array)
    rest = array.shape[1:]
    at = (layer,) + (0,) * len(rest)
    return pl.BlockSpec((None,) + rest, lambda *_: at)


def layer_scratch(n_heads, n_feat):
    square = pltpu.VMEM((n_feat, n_feat), BF16)
    return [pltpu.VMEM((8, WIN, 128), F32), square, square, square]


def first_layer(embedded, targets, slots, temper, token, consts, params, devices, groups=16):
    n_heads, n_feat = consts[3].shape
    columns = embedded.shape[1] // (WIN * n_feat)
    side = jax.ShapeDtypeStruct((64, n_feat), BF16)
    upper = jax.ShapeDtypeStruct((2 * columns, 24, 128), BF16)
    corner = jax.ShapeDtypeStruct((24, 128), BF16)
    mid = jax.ShapeDtypeStruct((2 * columns, 32, n_feat), BF16)
    mid_spec = pl.BlockSpec((2 * groups, 32, n_feat), lambda g: (g, 0, 0))
    return pl.pallas_call(
        functools.partial(first_kernel, groups),
        grid=(columns // groups,),
        out_shape=(mid, mid, upper, side, corner, jax.ShapeDtypeStruct((devices, 25, 4, 128), BF16)),
        in_specs=[SMEM, SMEM, SMEM, pl.BlockSpec((2 * WIN, groups * WIN * n_feat), lambda g: (0, g))]
        + [whole(a) for a in (token,) + consts]
        + [layer_spec(a, n, 0) for n, a in enumerate(params)],
        out_specs=(mid_spec, mid_spec, pl.BlockSpec((2 * groups, 24, 128), lambda g: (g, 0, 0)), whole(side), whole(corner), ANY),
        scratch_shapes=[pltpu.VMEM((CELLS, n_heads * CELLS), F32)]
        + layer_scratch(n_heads, n_feat)
        + [
            pltpu.VMEM((groups * 2 * CELLS, n_heads * CELLS), BF16),
            pltpu.VMEM((2 * columns, 25, 4, 128), BF16),
            pltpu.VMEM((devices, 1, 4, 128), BF16),
            pltpu.SemaphoreType.DMA((2 * columns,)),
            pltpu.SemaphoreType.DMA,
        ],
        compiler_params=pltpu.CompilerParams(vmem_limit_bytes=VMEM_BYTES),
        cost_estimate=pl.CostEstimate(flops=2 * 10**9, bytes_accessed=6 * 10**6, transcendentals=10**6),
        name="first_layer",
    )(targets, slots, temper, embedded, token, *consts, *params)


def second_kernel(
    groups,
    place, temper, mid0_ref, mid1_ref, below_ref, right_ref, corner_ref,
    coords_ref, heads_ref, ones_ref, mask_ref,
    net_in, net_first, net_out, qkv_ref, proj_ref, up_ref, down_ref, gain_ref,
    out_ref, rows_ref, side_ref,
    bias_ref, strips_ref, q_w, k_w, v_w, ext, ring, p_ref, sems,
):
    step = pl.program_id(0)
    n_heads, n_feat = mask_ref.shape
    n_half = mid0_ref.shape[0]
    row, col, last_row, last_col = place[0], place[1], place[2], place[3]
    width = HALF * n_feat

    @pl.when(step == 0)
    def _():
        own = pl.ds(0, n_half)
        copies = [
            pltpu.make_async_copy(src, dst, sems.at[n])
            for n, (src, dst) in enumerate(
                [
                    (mid0_ref, ext.at[0, own]),
                    (mid1_ref, ext.at[1, own]),
                    (right_ref.at[pl.ds(0, 32)], ext.at[0, n_half]),
                    (right_ref.at[pl.ds(32, 32)], ext.at[1, n_half]),
                    (below_ref, ring.at[own]),
                    (corner_ref, ring.at[n_half]),
                ]
            )
        ]
        for copy in copies:
            copy.start()
        out_ref[:, :width] = jnp.zeros((2 * WIN, width), BF16)
        split_weights(qkv_ref, q_w, k_w, v_w)
        bias_strips(coords_ref, net_in, net_first[1:2, :], net_out[:, 1, :], strips_ref)
        strips = [turned(strips_ref[h]) for h in range(n_heads)]
        lane = lax.broadcasted_iota(jnp.int32, (WIN, n_heads * CELLS), 1)
        upper = lax.broadcasted_iota(jnp.int32, (WIN, n_heads * CELLS), 0) < HALF
        other_rows = upper != (lane % WIN < HALF)
        for w in range(WIN):
            other_cols = (lane % CELLS >= CELLS // 2) != (w >= HALF)
            rows = slice(w * WIN, (w + 1) * WIN)
            bias = bias_rows(strips, w)
            away = -100.0 * LOG2E
            bias_ref[0, rows, :] = bias
            bias_ref[1, rows, :] = bias + jnp.where(other_cols, away, 0.0)
            bias_ref[2, rows, :] = bias + jnp.where(other_rows, away, 0.0)
            bias_ref[3, rows, :] = bias + jnp.where(other_rows | other_cols, away, 0.0)
        for copy in copies:
            copy.wait()

    upper = lax.broadcasted_iota(jnp.int32, (CELLS, n_feat), 0) % WIN < HALF
    tiles = []
    for group in range(groups):
        at = 2 * (step * groups + group) + 1
        zero = jnp.concatenate([ext[0, at], ext[0, at + 1]], 0)
        one = jnp.concatenate([ext[1, at], ext[1, at + 1]], 0)
        two = jnp.concatenate([whole_rows(ring[at + half].astype(F32)) for half in range(2)], 0)
        tiles += [jnp.where(upper, one, zero), jnp.where(upper, two.astype(BF16), one)]
    x = jnp.concatenate(tiles, 0)
    low_cut = (row == last_row).astype(jnp.int32)

    def bias_of(n):
        column = step * groups + n // 2
        cut = ((col == last_col) & (column == n_half // 2 - 1)).astype(jnp.int32)
        return bias_ref[cut + 2 * low_cut * (n % 2)]

    mixed = attend(
        x, q_w, k_w, v_w, temper_row(temper, 1, mask_ref), heads_ref, ones_ref, mask_ref, bias_of, p_ref
    )
    y = dense_tail(x.astype(F32), mixed, proj_ref, up_ref, down_ref, gain_ref).astype(F32)

    for group in range(groups):
        first = y[2 * group * CELLS : (2 * group + 1) * CELLS]
        second = y[(2 * group + 1) * CELLS : (2 * group + 2) * CELLS]
        zero = jnp.where(upper, second, first)
        one = jnp.where(upper, first, second)
        for half in range(2):
            slabs = []
            for w in range(half * HALF, (half + 1) * HALF):
                rows = slice(w * WIN, (w + 1) * WIN)
                slabs.append(jnp.concatenate([zero[rows], one[rows]], 0))
            strip = jnp.concatenate(slabs, 1).astype(BF16)
            at = 2 * (step * groups + group) + 1 + half
            if half == 0 or group < groups - 1:
                out_ref[:, pl.ds(pl.multiple_of(at * width, 128), width)] = strip
            else:

                @pl.when(at < n_half)
                def _(at=at, strip=strip):
                    out_ref[:, pl.ds(pl.multiple_of(at * width, 128), width)] = strip

                @pl.when(at == n_half)
                def _(strip=strip):
                    side_ref[...] = strip

    @pl.when(step == pl.num_programs(0) - 1)
    def _():
        quarter = rows_ref.shape[1]
        first = lax.broadcasted_iota(jnp.int32, (WIN, quarter), 0) < HALF
        tops = [out_ref[:, n * quarter : (n + 1) * quarter][:WIN].astype(F32) for n in range(4)]
        pairs = [
            jnp.where(first, tops[2 * n], pltpu.roll(tops[2 * n + 1], HALF, 0)) for n in range(2)
        ]
        rows_ref[...] = jnp.concatenate(pairs, 0).astype(BF16)


def second_layer(place, temper, pieces, consts, params, groups=8):
    n_heads, n_feat = consts[3].shape
    n_half = pieces[0].shape[0]
    out = jax.ShapeDtypeStruct((2 * WIN, n_half * HALF * n_feat), BF16)
    rows = jax.ShapeDtypeStruct((2 * WIN, n_half * n_feat), BF16)
    side = jax.ShapeDtypeStruct((2 * WIN, HALF * n_feat), BF16)
    return pl.pallas_call(
        functools.partial(second_kernel, groups),
        grid=(n_half // 2 // groups,),
        out_shape=(out, rows, side),
        in_specs=[SMEM, SMEM]
        + [ANY] * len(pieces)
        + [whole(a) for a in consts]
        + [layer_spec(a, n, 1) for n, a in enumerate(params)],
        out_specs=(whole(out), whole(rows), whole(side)),
        scratch_shapes=[pltpu.VMEM((4, CELLS, n_heads * CELLS), F32)]
        + layer_scratch(n_heads, n_feat)
        + [
            pltpu.VMEM((2, n_half + 1, 32, n_feat), BF16),
            pltpu.VMEM((n_half + 1, 24, 128), BF16),
            pltpu.VMEM((groups * 2 * CELLS, n_heads * CELLS), BF16),
            pltpu.SemaphoreType.DMA((6,)),
        ],
        compiler_params=pltpu.CompilerParams(vmem_limit_bytes=VMEM_BYTES),
        cost_estimate=pl.CostEstimate(flops=10**11, bytes_accessed=10**7, transcendentals=10**6),
        name="second_layer",
    )(place, temper, *pieces, *consts, *params)


def merge_features(own_ref, rows_ref, side_ref, corner_ref, out_ref):
    quarter, width = rows_ref.shape[1], side_ref.shape[1]
    first = lax.broadcasted_iota(jnp.int32, (WIN, quarter), 0) < HALF
    for n in range(4):
        lanes = slice(n * quarter, (n + 1) * quarter)
        own = own_ref[:, lanes].astype(F32)
        top = rows_ref[...].astype(F32)[n // 2 * WIN : (n // 2 + 1) * WIN]
        top = pltpu.roll(top, HALF, 0) if n % 2 else top
        merged = jnp.concatenate([jnp.where(first, top, own[:WIN]), own[WIN:]], 0)
        out_ref[:, lanes] = merged.astype(BF16)
    corner = lax.broadcasted_iota(jnp.int32, (2 * WIN, width), 0) < HALF
    merged = jnp.where(corner, corner_ref[...].astype(F32), side_ref[...].astype(F32))
    out_ref[:, :width] = merged.astype(BF16)


def last_kernel(
    entries_ref, own_hbm, rows_hbm, side_hbm, corner_hbm, features_hbm, packed_ref,
    marks_ref, held, own_ref, features_ref, rows_ref, side_ref, corner_ref, sems, slot_sems,
):
    slots = packed_ref.shape[0]
    marks_copy = pltpu.make_async_copy(entries_ref.at[:, pl.ds(24, 1)], marks_ref, sems.at[0])
    own_copy = pltpu.make_async_copy(own_hbm, own_ref, sems.at[1])
    marks_copy.start()
    own_copy.start()
    halos = [
        pltpu.make_async_copy(src, dst, sems.at[3 + n])
        for n, (src, dst) in enumerate(
            [(rows_hbm, rows_ref), (side_hbm, side_ref), (corner_hbm, corner_ref)]
        )
    ]
    for copy in halos:
        copy.start()
    marks_copy.wait()
    marks = marks_ref[...][:, 0].astype(F32)
    lane = lax.broadcasted_iota(jnp.int32, marks.shape, 2).astype(F32)
    sender = lax.broadcasted_iota(jnp.int32, marks.shape, 0).astype(F32)
    found = jnp.max(jnp.where(marks == lane, sender, 0.0), 0).astype(jnp.int32)
    windows = [
        pltpu.make_async_copy(entries_ref.at[found[0, slot]], held.at[slot], slot_sems.at[slot])
        for slot in range(slots)
    ]
    for copy in windows:
        copy.start()
    own_copy.wait()
    for copy in halos:
        copy.wait()
    merge_features(own_ref, rows_ref, side_ref, corner_ref, features_ref)
    leave = pltpu.make_async_copy(features_ref, features_hbm, sems.at[2])
    leave.start()
    for copy in windows:
        copy.wait()
    lane = lax.broadcasted_iota(jnp.int32, (slots, 128), 1)

    def rows_of(at):
        rows = held[:, at // 4 : at // 4 + 2].astype(F32).reshape(slots, WIN, 128)
        return jnp.swapaxes(rows, 0, 1)

    for pair in range(WIN // 2):
        even = rows_of(2 * pair * WIN)
        odd = rows_of((2 * pair + 1) * WIN)
        tails = rows_of(CELLS + pair * WIN)
        for u in range(WIN):
            moved = pltpu.roll(odd[u], 64, 1)
            joined = [
                even[u],
                jnp.where(lane < 64, tails[u], moved),
                jnp.where(lane < 64, moved, tails[u]),
            ]
            at = (u * WIN + 2 * pair) * 192
            packed_ref[:, at : at + 384] = jnp.concatenate(joined, 1).astype(BF16)
    leave.wait()


def last_steps(arrived, own, rows, side, corner, slots, width):
    return pl.pallas_call(
        last_kernel,
        out_shape=(jax.ShapeDtypeStruct(own.shape, BF16), jax.ShapeDtypeStruct((slots, width), BF16)),
        in_specs=[ANY] * 5,
        out_specs=(ANY, pl.BlockSpec(memory_space=pltpu.VMEM)),
        scratch_shapes=[
            pltpu.VMEM((arrived.shape[0], 1, 4, 128), BF16),
            pltpu.VMEM((slots,) + arrived.shape[1:], BF16),
        ]
        + [pltpu.VMEM(own.shape, BF16)] * 2
        + [pltpu.VMEM(a.shape, BF16) for a in (rows, side, corner)]
        + [pltpu.SemaphoreType.DMA((6,)), pltpu.SemaphoreType.DMA((slots,))],
        compiler_params=pltpu.CompilerParams(vmem_limit_bytes=LAST_BYTES),
        name="last_steps",
    )(arrived, own, rows, side, corner)


def moved(block, rows, cols):
    n_row, n_col = lax.axis_size("row"), lax.axis_size("col")
    route = [
        (r * n_col + c, (r + rows) % n_row * n_col + (c + cols) % n_col)
        for r in range(n_row)
        for c in range(n_col)
    ]
    return lax.ppermute(block, ("row", "col"), route)


def local(
    embedded,
    window_target_device,
    window_device_slot,
    cloud_mask_token,
    query_key_value_weight,
    projection_weight,
    up_weight,
    down_weight,
    bias_net_input_weight,
    bias_net_first_bias,
    bias_net_output_weight,
    temper,
    norm_gain_values,
):
    n_row, n_col = lax.axis_size("row"), lax.axis_size("col")
    n_heads, n_feat = temper.shape[1], cloud_mask_token.shape[0]
    slots = window_target_device.size // 2
    row, col = lax.axis_index("row"), lax.axis_index("col")
    place = jnp.stack([row, col, n_row - 1, n_col - 1]).astype(jnp.int32)
    consts = constants(n_heads, n_feat)
    params = (
        bias_net_input_weight,
        bias_net_first_bias,
        jnp.transpose(bias_net_output_weight, (2, 0, 1)),
        query_key_value_weight,
        projection_weight,
        up_weight,
        jnp.swapaxes(down_weight, 1, 2),
        norm_gain_values,
    )
    mid0, mid1, upper, left, corner, send = first_layer(
        embedded, window_target_device, window_device_slot, temper, cloud_mask_token, consts, params,
        n_row * n_col,
    )
    pieces = (mid0, mid1, moved(upper, -1, 0), moved(left, 0, -1), moved(corner, -1, -1))
    arrived = lax.all_to_all(send, ("row", "col"), split_axis=0, concat_axis=0, tiled=True)
    own, rows, side = second_layer(place, temper, pieces, consts, params)
    return last_steps(
        arrived, own, moved(rows, 1, 0), moved(side, 0, 1), moved(side, 1, 1), slots, CELLS * n_feat
    )


def solution(mesh):
    in_specs = (P("row", "col"),) * 3 + (P(),) * 10
    out_specs = (P("row", "col"), P(("row", "col"), None))
    return jax.shard_map(local, mesh=mesh, in_specs=in_specs, out_specs=out_specs, check_vma=False)
```
